256 devices in a mesh: segment: 8 (over y_lo, x), az: 32 (over y_hi, z, core).
Axes of the slice: x: 4, y: 4 (y_hi: 2, y_lo: 2; y = y_hi * 2 + y_lo), z: 8, core: 2. Of those that a mesh axis runs over, the one named last changes fastest.
Arguments:
- stored_inputs: bfloat16 [4, 8, 3, 2048, 512], P(None, 'segment', None, 'az'), may hold values from -6 to 6
- filter_weights: bfloat16 [8, 3, 3, 512, 512], P('segment'), may hold values from -0.09375 to 0.09375
- pending_slopes: bfloat16 [8, 3, 2048, 512], P('segment', None, 'az'), may hold values from -6 to 6
- topmost_slopes: bfloat16 [3, 3, 2048, 512], P(None, None, 'az'), may hold values from -6 to 6
Outputs:
- sent: bfloat16 [4, 8, 3, 2048, 512], P(None, 'segment', None, 'az')
- weight_grads: bfloat16 [8, 3, 3, 512, 512], P('segment', None, None, 'az')
The draws below stay inside these ranges and needn't reach their ends.
All inputs are finite; a program needn't handle non-finite values.
Results may differ from the reference program's by a relative error of at most 0.022.
Values may be sent and summed in bfloat16 or wider, within the bound.
No kernel may reach another device: no remote copies, remote signals or barrier semaphores. Data moves between devices by JAX's collectives and lax.ppermute only.
A program may use at most 128 MiB of HBM per device.

```python
import math
import jax
import jax.numpy as jnp
from jax import lax

FEATURE_DEPTH = 512
VERTICAL_BEAMS = 3
STEPS = 4
NUMBER_OF_PARTS = 8
HORIZONTAL_BINS = 2048
N_AZ = 32


def with_spikes(array, own_key, source, target, blocks, factor):
    owner, partner = [(jnp.arange(array.shape[position]) // (array.shape[position] // blocks)).reshape([-1 if axis == position else 1 for axis in range(array.ndim)]) for position in (source, target)]
    chosen = jax.random.permutation(own_key, blocks)[partner]
    strong = (owner == chosen) | (owner == (partner + blocks // 2) % blocks)
    return jnp.where(strong, factor * array, array)


def steps_of(own_key, dims, shards, low, high):
    factor_of = 1.0
    for axis_at, shards_of in shards:
        draws = jax.random.uniform(jax.random.fold_in(jax.random.fold_in(own_key, 6), axis_at), (shards_of,), jnp.float32, low / len(shards), high / len(shards))
        factor_of = factor_of * jnp.repeat(jnp.exp(draws), dims[axis_at] // shards_of).reshape((-1,) + (1,) * (len(dims) - 1 - axis_at))
    return factor_of


def scatter_about(own_key, extent, deviation, most, shards=(), kind=jnp.bfloat16):
    level = steps_of(own_key, extent, shards, -0.22, 0.18) if shards else 1.0
    drawn = jax.random.normal(own_key, extent, jnp.float32) * deviation * level
    return jnp.minimum(jnp.maximum(drawn, -most), most).astype(kind)


def bell_draw_with(key, extent, scale, limit, shards, heavy, dtype=jnp.bfloat16):
    drawn = scale * jax.random.normal(key, extent, jnp.float32)
    if shards:
        drawn = drawn * steps_of(key, extent, shards, -0.22, 0.18)
    return jnp.clip(with_spikes(drawn, jax.random.fold_in(key, 3), *heavy), -limit, limit).astype(dtype)


def setup_inputs(seed: int = 0) -> dict:
    seeds = jax.random.split(jax.random.key(seed), 5)
    stored_inputs = bell_draw_with(seeds[0], (STEPS, NUMBER_OF_PARTS, VERTICAL_BEAMS, HORIZONTAL_BINS, FEATURE_DEPTH), 1.0, 6.0, ((1, 8), (3, 32)), (3, 4, 32, 2.75))
    filter_weights = scatter_about(seeds[1], (NUMBER_OF_PARTS, 3, 3, FEATURE_DEPTH, FEATURE_DEPTH), (9 * FEATURE_DEPTH) ** -0.5, 0.09375, ((0, 8),))
    pending_slopes = scatter_about(seeds[2], (NUMBER_OF_PARTS, VERTICAL_BEAMS, HORIZONTAL_BINS, FEATURE_DEPTH), 1.0, 6.0, ((0, 8), (2, 32)))
    topmost_slopes = scatter_about(seeds[3], (STEPS - 1, VERTICAL_BEAMS, HORIZONTAL_BINS, FEATURE_DEPTH), 1.0, 6.0, ((2, 32),))
    return {"stored_inputs": stored_inputs, "filter_weights": filter_weights, "pending_slopes": pending_slopes, "topmost_slopes": topmost_slopes}


def patch_rows(padded, height, width):
    parts = [padded[row_off:row_off + height, col_off:col_off + width, :] for row_off in range(3) for col_off in range(3)]
    return jnp.concatenate(parts, axis=-1).reshape(height * width, -1)

def circular_pad(field):
    padded = jnp.pad(field, ((1, 1), (0, 0), (0, 0)))
    return jnp.concatenate([padded[:, -1:], padded, padded[:, :1]], axis=1)

def by_blocks(stacked):
    depth = stacked.shape[-1]
    shaped = stacked.reshape(STEPS, VERTICAL_BEAMS, N_AZ, HORIZONTAL_BINS // N_AZ, depth)
    return jnp.transpose(shaped, (2, 0, 1, 3, 4)).reshape(N_AZ, -1, depth)

def add_block(carry, pair):
    left, right = pair
    partial_value = lax.dot_general(left, right, (((0,), (0,)), ((), ())), preferred_element_type=jnp.float32)
    rounded = lax.optimization_barrier(partial_value.astype(jnp.bfloat16))
    return (carry + rounded.astype(jnp.float32), None)

def reference(stored_inputs, filter_weights, pending_slopes, topmost_slopes):
    channels = filter_weights.shape[-1]
    forward = filter_weights.reshape(NUMBER_OF_PARTS, 9 * channels, channels)
    flipped = jnp.transpose(filter_weights[:, ::-1, ::-1], (0, 1, 2, 4, 3)).reshape(NUMBER_OF_PARTS, 9 * channels, channels)
    arriving_slope = [pending_slopes[block_transform] for block_transform in range(NUMBER_OF_PARTS)]
    kept = [[] for block_transform in range(NUMBER_OF_PARTS)]
    emitted = []
    for step in range(STEPS):
        outgoing = []
        for block_transform in range(NUMBER_OF_PARTS):
            emitted_slope = arriving_slope[block_transform].reshape(VERTICAL_BEAMS * HORIZONTAL_BINS, channels).astype(jnp.float32)
            columns_x = patch_rows(circular_pad(stored_inputs[step, block_transform]), VERTICAL_BEAMS, HORIZONTAL_BINS)
            preact = jnp.dot(columns_x, forward[block_transform], preferred_element_type=jnp.float32)
            gate = jax.nn.sigmoid(preact)
            grad_pre = (emitted_slope * gate * (1.0 + preact * (1.0 - gate))).astype(jnp.bfloat16)
            kept[block_transform].append(grad_pre)
            columns_g = patch_rows(circular_pad(grad_pre.reshape(VERTICAL_BEAMS, HORIZONTAL_BINS, channels)), VERTICAL_BEAMS, HORIZONTAL_BINS)
            back = jnp.dot(columns_g, flipped[block_transform], preferred_element_type=jnp.float32)
            grad_in = (emitted_slope + back).astype(jnp.bfloat16).reshape(VERTICAL_BEAMS, HORIZONTAL_BINS, channels)
            outgoing.append(grad_in)
        emitted.append(jnp.stack(outgoing))
        if step + 1 < STEPS:
            arriving_slope = [outgoing[block_transform + 1] for block_transform in range(NUMBER_OF_PARTS - 1)] + [topmost_slopes[step]]
    scale = 1.0 / math.sqrt(STEPS * VERTICAL_BEAMS * HORIZONTAL_BINS)
    results = []
    for block_transform in range(NUMBER_OF_PARTS):
        columns_all = by_blocks(jnp.stack([patch_rows(circular_pad(stored_inputs[step, block_transform]), VERTICAL_BEAMS, HORIZONTAL_BINS) for step in range(STEPS)]))
        grads_all = by_blocks(jnp.stack(kept[block_transform]))
        total, unused = lax.scan(add_block, jnp.zeros((9 * channels, channels), jnp.float32), (columns_all, grads_all))
        results.append((total * scale).reshape(3, 3, channels, channels))
    weight_grads = jnp.stack(results).astype(jnp.bfloat16)
    return (jnp.stack(emitted), weight_grads)
```

```python
import math

import jax
import jax.numpy as jnp
from jax import lax
from jax.sharding import PartitionSpec as P

BF = jnp.bfloat16
F32 = jnp.float32


def az_route(move):
    route = []
    for i in range(32):
        h, z, c = move(i // 16, (i // 2) % 8, i % 2)
        route.append((i, (h % 2) * 16 + (z % 8) * 2 + c % 2))
    return route


RIGHT = [(i, (i + 1) % 32) for i in range(32)]
LEFT = [(i, (i - 1) % 32) for i in range(32)]
CORE = az_route(lambda h, z, c: (h, z, c + 1))
PAIR = az_route(lambda h, z, c: (h, z ^ 1, c))
DIAG = az_route(lambda h, z, c: (h, z ^ 1, c + 1))
FAR = az_route(lambda h, z, c: (h + 1, z, c))


def send(block, route):
    return lax.ppermute(block, "az", route)


def relay(block):
    count = lax.axis_size("segment")
    return lax.ppermute(block, "segment", [(i, i - 1) for i in range(1, count)])


def pad_rows(field):
    return jnp.pad(field, ((1, 1), (0, 0), (0, 0)))


def patch_rows(field, reverse=False):
    padded = pad_rows(field)
    height, width = field.shape[0], field.shape[1] - 2
    taps = [(a, b) for a in range(3) for b in range(3)]
    if reverse:
        taps = [(2 - a, 2 - b) for a, b in taps]
    parts = [padded[a : a + height, b : b + width] for a, b in taps]
    return jnp.concatenate(parts, axis=-1).reshape(height * width, -1)


def add(left, right):
    return (left.astype(F32) + right.astype(F32)).astype(BF)


def pick(block, index, axis):
    return lax.dynamic_index_in_dim(block, index, axis, keepdims=False)


def fold_far(block, h):
    return add(send(pick(block, 1 - h, 1), FAR), pick(block, h, 1))


def fold_ring(block, j):
    half = block.shape[-1] // 2
    sides = ((1, block[..., :half]), (-1, block[..., half:]))
    held = [pick(part, (j - d) % 4, 1) for d, part in sides]
    for s in range(3):
        held = [
            add(
                send(held[n], az_route(lambda h, z, c, d=d: (h, z + 2 * d, c))),
                pick(part, (j - d * (s + 2)) % 4, 1),
            )
            for n, (d, part) in enumerate(sides)
        ]
    return jnp.concatenate(held, axis=-1)


def body(stored_inputs, filter_weights, pending_slopes, topmost_slopes):
    x = stored_inputs[:, 0]
    steps, height, width, ch = x.shape
    pending = pending_slopes[0]
    top = topmost_slopes
    az = lax.axis_index("az")
    h, j = az // 16, (az // 4) % 4
    quarter = az % 4
    last = lax.axis_index("segment") == lax.axis_size("segment") - 1
    forward = filter_weights[0].reshape(9 * ch, ch)
    taps = filter_weights[0].reshape(9, ch, ch)
    scale = 1.0 / math.sqrt(steps * height * width * 32)

    def pack(cut):
        parts = [cut(x, 5, 2), cut(pending, 4, 1), cut(top, 3, 2)]
        return jnp.concatenate([p.reshape(-1, ch) for p in parts], axis=0)

    def unpack(rows):
        a, b = steps * height * 5, steps * height * 5 + height * 4
        return (
            rows[:a].reshape(steps, height, 5, ch),
            rows[a:b].reshape(height, 4, ch),
            rows[b:].reshape(steps - 1, height, 3, ch),
        )

    def tail_of(v, n, axis):
        return lax.slice_in_dim(v, width - n, width, axis=axis)

    def head_of(v, n, axis):
        return lax.slice_in_dim(v, 0, n, axis=axis)

    lows = unpack(send(pack(tail_of), RIGHT))
    highs = unpack(send(pack(head_of), LEFT))
    x_wide = jnp.concatenate([lows[0], x, highs[0]], axis=2)
    pending_wide = jnp.concatenate([lows[1], pending, highs[1]], axis=1)
    top_wide = jnp.concatenate([lows[2], top, highs[2]], axis=2)

    lane = jnp.arange(ch)
    source = ((lane % 128) // 16) * 64 + (lane // 128) * 16 + lane % 16
    order = (jnp.arange(ch)[:, None] == source[None, :]).astype(BF)
    x_near = x_wide[:, :, 4:-4]
    x_near = jnp.dot(x_near.reshape(-1, ch), order, preferred_element_type=F32).astype(BF)
    x_near = x_near.reshape(steps * height * (width + 2), 4, 128)
    x_core = send(pick(x_near, quarter ^ 1, 1), CORE)
    x_pair = send(pick(x_near, quarter ^ 2, 1), PAIR)
    x_diag = send(pick(x_near, quarter ^ 3, 1), DIAG)
    gathered = [
        v.reshape(steps, height, width + 2, 128)
        for v in (pick(x_near, quarter, 1), x_core, x_pair, x_diag)
    ]

    def slope_factor(t):
        field = x_wide[t, :, t : x_wide.shape[2] - t]
        preact = jnp.dot(patch_rows(field), forward, preferred_element_type=F32)
        gate = jax.nn.sigmoid(preact)
        return gate * (1.0 + preact * (1.0 - gate))

    slope = pending_wide
    total = jnp.zeros((9 * 128, ch), F32)
    emitted = []
    for t in range(steps):
        wide = slope.shape[1]
        factor = slope_factor(t)
        grad = (slope.reshape(-1, ch).astype(F32) * factor).astype(BF).reshape(height, wide, ch)
        own = grad[:, 3 - t + 1 : wide - (3 - t + 1)]
        from_core = send(own, CORE)
        from_pair = send(own, PAIR)
        from_diag = send(from_pair, CORE)
        patches = patch_rows(grad, reverse=True).reshape(-1, 9, ch)
        back = lax.dot_general(
            patches, taps, (((1, 2), (0, 2)), ((), ())), preferred_element_type=F32
        ).reshape(height, wide - 2, ch)
        out = (slope[:, 1:-1].astype(F32) + back).astype(BF)
        emitted.append(out[:, 3 - t : wide - 2 - (3 - t)])
        left = jnp.concatenate([patch_rows(v[t]) for v in gathered], axis=0)
        right = jnp.concatenate([v.reshape(-1, ch) for v in (own, from_core, from_pair, from_diag)], axis=0)
        total = total + lax.dot_general(
            left, right, (((0,), (0,)), ((), ())), preferred_element_type=F32
        )
        if t + 1 < steps:
            above = top_wide[t][:, t : top_wide.shape[2] - t]
            slope = jnp.where(last, above, relay(out))

    block = total.astype(BF).reshape(9, 2, 4, 16, ch)
    cut = ch // 2
    first = fold_ring(fold_far(block[..., :cut].reshape(9, 2, 64, cut), h).reshape(9, 4, 16, cut), j)
    second = block[..., cut:].transpose(0, 2, 1, 3, 4).reshape(9, 4, 32, cut)
    second = fold_far(fold_ring(second, j).reshape(9, 2, 16, cut), h)
    summed = jnp.concatenate([first, second], axis=-1).astype(F32)
    weight_grads = (summed * scale).astype(BF).reshape(1, 3, 3, 16, ch)
    return (jnp.stack(emitted)[:, None], weight_grads)


def solution(mesh):
    return jax.shard_map(
        body,
        mesh=mesh,
        in_specs=(
            P(None, "segment", None, "az", None),
            P("segment", None, None, None, None),
            P("segment", None, "az", None),
            P(None, None, "az", None),
        ),
        out_specs=(P(None, "segment", None, "az", None), P("segment", None, None, "az", None)),
        check_vma=False,
    )
```

```python
import math

import jax
import jax.numpy as jnp
from jax import lax
from jax.experimental import pallas as pl
from jax.experimental.pallas import tpu as pltpu
from jax.sharding import PartitionSpec as P

BF = jnp.bfloat16
F32 = jnp.float32
ROWS, WIDTH, CH, STEPS = 3, 64, 512, 4
WIDE = WIDTH + 8
QUARTER = CH // 4


def az_route(move):
    route = []
    for i in range(32):
        h, z, c = move(i // 16, (i // 2) % 8, i % 2)
        route.append((i, (h % 2) * 16 + (z % 8) * 2 + c % 2))
    return route


RIGHT = [(i, (i + 1) % 32) for i in range(32)]
LEFT = [(i, (i - 1) % 32) for i in range(32)]
CORE = az_route(lambda h, z, c: (h, z, c + 1))
PAIR = az_route(lambda h, z, c: (h, z ^ 1, c))
DIAG = az_route(lambda h, z, c: (h, z ^ 1, c + 1))
FAR = az_route(lambda h, z, c: (h + 1, z, c))
UP = az_route(lambda h, z, c: (h, z + 2, c))
DOWN = az_route(lambda h, z, c: (h, z - 2, c))


def send(block, route):
    return lax.ppermute(block, "az", route)


def relay(block):
    count = lax.axis_size("segment")
    return lax.ppermute(block, "segment", [(i, i - 1) for i in range(1, count)])


def params(mib=48):
    return pltpu.CompilerParams(vmem_limit_bytes=mib * 1024 * 1024)


def cost(flops, size):
    return pl.CostEstimate(flops=int(flops), bytes_accessed=int(size), transcendentals=0)


VMEM = pl.BlockSpec(memory_space=pltpu.VMEM)
SMEM = pl.BlockSpec(memory_space=pltpu.SMEM)


def block(shape, *index):
    return pl.BlockSpec(shape, lambda *_: index)


def pack_kernel(x_right, p_right, t_right, x_left, p_left, t_left, right_ref, left_ref):
    for refs, first, out in (((x_right, p_right, t_right), 8, right_ref), ((x_left, p_left, t_left), 0, left_ref)):
        xs, ps, ts = refs
        for r in range(ROWS):
            planes = [xs[t, r] for t in range(STEPS)] + [ps[r]] + [ts[t, r] for t in range(STEPS - 1)]
            for n, plane in enumerate(planes):
                out[n * ROWS + r] = plane.astype(F32)[first : first + 8].astype(BF)


def pack_edges(x, pending, top):
    def specs(edge):
        return [
            block((STEPS, ROWS, 16, CH), 0, 0, edge, 0),
            block((ROWS, 16, CH), 0, edge, 0),
            block((STEPS - 1, ROWS, 16, CH), 0, 0, edge, 0),
        ]

    shape = jax.ShapeDtypeStruct((24, 8, CH), BF)
    return pl.pallas_call(
        pack_kernel,
        grid=(1,),
        out_shape=(shape, shape),
        in_specs=specs(3) + specs(0),
        out_specs=(block((24, 8, CH), 0, 0, 0),) * 2,
        compiler_params=params(),
        cost_estimate=cost(0, 1 << 20),
    )(x, pending, top, x, pending, top)


def first_four(high, low):
    pick = lax.broadcasted_iota(jnp.int32, high.shape, 0) < 4
    return jnp.where(pick, high, low)


def widen(own, high, low):
    return jnp.concatenate([own.astype(F32), first_four(high.astype(F32), low.astype(F32))], axis=0)


def factor_kernel(x_ref, low_ref, high_ref, w_ref, out_ref):
    wide = WIDTH + 16
    planes = [
        jnp.concatenate(
            [x_ref[0, r].astype(F32), high_ref[r].astype(F32), low_ref[r].astype(F32)], axis=0
        )
        for r in range(ROWS)
    ]
    field = jnp.concatenate(planes, axis=0).astype(BF)
    sums = []
    for b in range(3):
        up = jnp.dot(field[: 2 * wide], w_ref[b], preferred_element_type=F32)
        mid = jnp.dot(field, w_ref[3 + b], preferred_element_type=F32)
        down = jnp.dot(field[wide:], w_ref[6 + b], preferred_element_type=F32)
        rows = []
        for r in range(ROWS):
            value = mid[r * wide : (r + 1) * wide]
            if r > 0:
                value = value + up[(r - 1) * wide : r * wide]
            if r < 2:
                value = value + down[r * wide : (r + 1) * wide]
            rows.append(value)
        sums.append(rows)
    for r in range(ROWS):
        preact = pltpu.roll(sums[0][r], 1, 0) + sums[1][r] + pltpu.roll(sums[2][r], wide - 1, 0)
        gate = jax.nn.sigmoid(preact)
        value = gate * (1.0 + preact * (1.0 - gate))
        out_ref[0, r, :WIDTH] = value[:WIDTH]
        out_ref[0, r, WIDTH:] = first_four(value[WIDTH : WIDTH + 8], value[WIDTH + 8 :])


def slope_factors(x, low, high, weights, first, count):
    return pl.pallas_call(
        factor_kernel,
        grid=(count,),
        out_shape=jax.ShapeDtypeStruct((count, ROWS, WIDE, CH), F32),
        in_specs=[
            pl.BlockSpec((1, ROWS, WIDTH, CH), lambda n: (first + n, 0, 0, 0)),
            pl.BlockSpec((ROWS, 8, CH), lambda n: (first + n, 0, 0)),
            pl.BlockSpec((ROWS, 8, CH), lambda n: (first + n, 0, 0)),
            pl.BlockSpec((9, CH, CH), lambda n: (0, 0, 0)),
        ],
        out_specs=pl.BlockSpec((1, ROWS, WIDE, CH), lambda n: (n, 0, 0, 0)),
        compiler_params=params(),
        cost_estimate=cost(count * 1.2e9, 5e6),
    )(x, low, high, weights)


def back_kernel(first, *refs):
    if first:
        own_ref, low_ref, high_ref, factor_ref, w_ref, sent_ref, grad_ref = refs
    else:
        flag_ref, own_ref, low_ref, high_ref, relay_ref, factor_ref, w_ref, sent_ref, grad_ref = refs
    slopes = []
    for r in range(ROWS):
        own = own_ref[r] if first else own_ref[0, r]
        slope = widen(own, high_ref[r], low_ref[r])
        if not first:
            slope = jnp.where(flag_ref[0] == 1, slope, relay_ref[r].astype(F32))
        slopes.append(slope)
    grads = []
    for r in range(ROWS):
        grad = slopes[r] * factor_ref[0, r]
        grad_ref[r] = grad[:WIDTH].astype(BF)
        grads.append(grad)
    field = jnp.concatenate(grads, axis=0).astype(BF)
    above = jnp.concatenate(grads[1:], axis=0).astype(BF)
    below = jnp.concatenate(grads[:2], axis=0).astype(BF)
    turned = (((1,), (1,)), ((), ()))
    sums = []
    for b in range(3):
        up = lax.dot_general(above, w_ref[b], turned, preferred_element_type=F32)
        mid = lax.dot_general(field, w_ref[3 + b], turned, preferred_element_type=F32)
        down = lax.dot_general(below, w_ref[6 + b], turned, preferred_element_type=F32)
        rows = []
        for r in range(ROWS):
            value = mid[r * WIDE : (r + 1) * WIDE]
            if r < 2:
                value = value + up[r * WIDE : (r + 1) * WIDE]
            if r > 0:
                value = value + down[(r - 1) * WIDE : r * WIDE]
            rows.append(value)
        sums.append(rows)
    for r in range(ROWS):
        value = pltpu.roll(sums[0][r], WIDE - 1, 0) + sums[1][r] + pltpu.roll(sums[2][r], 1, 0)
        sent_ref[r] = (slopes[r] + value).astype(BF)


def back_step(own, low, high, factors, weights, t, flag=None, arrived=None):
    first = t == 0
    edge = block((ROWS, 8, CH), 4 + t, 0, 0)
    operands = [own, low, high]
    if first:
        specs = [block((ROWS, WIDTH, CH), 0, 0, 0), edge, edge]
    else:
        specs = [SMEM, block((1, ROWS, WIDTH, CH), t - 1, 0, 0, 0), edge, edge]
        specs += [block((ROWS, WIDE, CH), 0, 0, 0)]
        operands = [flag, *operands, arrived]
    specs += [block((1, ROWS, WIDE, CH), max(t - 1, 0), 0, 0, 0), block((9, CH, CH), 0, 0, 0)]
    return pl.pallas_call(
        lambda *refs: back_kernel(first, *refs),
        grid=(1,),
        out_shape=(
            jax.ShapeDtypeStruct((ROWS, WIDE, CH), BF),
            jax.ShapeDtypeStruct((ROWS, WIDTH, CH), BF),
        ),
        in_specs=specs,
        out_specs=(block((ROWS, WIDE, CH), 0, 0, 0), block((ROWS, WIDTH, CH), 0, 0, 0)),
        compiler_params=params(),
        cost_estimate=cost(1.1e9, 6e6),
    )(*operands, factors, weights)


def spread_kernel(place_ref, x_ref, low_ref, high_ref, out0, out1, out2, out3, order_ref):
    @pl.when(pl.program_id(0) == 0)
    def _():
        h, j, q = place_ref[0], place_ref[1], place_ref[2]
        lane = lax.broadcasted_iota(jnp.int32, (8, CH), 1)
        slot, rest = lane // QUARTER, lane % QUARTER
        quarter = jnp.bitwise_xor(slot, q)
        half = jnp.bitwise_xor(rest // 64, h)
        turn = jnp.bitwise_and(rest // 16 + j, 3)
        source = (half * 4 + turn) * 64 + quarter * 16 + rest % 16
        row = lax.broadcasted_iota(jnp.int32, (CH, CH), 0)
        order_ref[...] = jnp.where(row == source[:1], 1.0, 0.0).astype(BF)

    planes = [widen(x_ref[0, r], high_ref[r], low_ref[r]) for r in range(ROWS)]
    field = jnp.concatenate(planes, axis=0).astype(BF)
    value = jnp.dot(field, order_ref[...], preferred_element_type=F32)
    for n, out in enumerate((out0, out1, out2, out3)):
        for r in range(ROWS):
            out[0, r] = value[r * WIDE : (r + 1) * WIDE, n * QUARTER : (n + 1) * QUARTER].astype(BF)


def spread(place, x, low, high):
    shape = jax.ShapeDtypeStruct((STEPS, ROWS, WIDE, QUARTER), BF)
    return pl.pallas_call(
        spread_kernel,
        grid=(STEPS,),
        out_shape=(shape,) * 4,
        in_specs=[
            SMEM,
            pl.BlockSpec((1, ROWS, WIDTH, CH), lambda n: (n, 0, 0, 0)),
            pl.BlockSpec((ROWS, 8, CH), lambda n: (n, 0, 0)),
            pl.BlockSpec((ROWS, 8, CH), lambda n: (n, 0, 0)),
        ],
        out_specs=(pl.BlockSpec((1, ROWS, WIDE, QUARTER), lambda n: (n, 0, 0, 0)),) * 4,
        scratch_shapes=[pltpu.VMEM((CH, CH), BF)],
        compiler_params=params(),
        cost_estimate=cost(4.5e8, 2e6),
    )(place, x, low, high)


def weight_kernel(more, last, *refs):
    xs, gs = refs[:4], refs[4:8]
    out_ref = refs[-1]
    left, right = [], []
    for r in range(ROWS):
        taps = [[], [], []]
        for x_ref in xs:
            plane = x_ref[0, r].astype(F32)
            for b, shift in enumerate((1, 0, WIDE - 1)):
                moved = pltpu.roll(plane, shift, 0) if shift else plane
                taps[b].append(moved[:WIDTH])
        left.append(
            jnp.concatenate([jnp.concatenate(parts, axis=0).astype(BF) for parts in taps], axis=1)
        )
        right.append(jnp.concatenate([g[r] for g in gs], axis=0))
    for a in range(3):
        ls = left[: 2 + (a > 0)] if a < 2 else left[1:]
        rs = right[1:] if a == 0 else (right if a == 1 else right[:2])
        value = lax.dot_general(
            jnp.concatenate(ls, axis=0),
            jnp.concatenate(rs, axis=0),
            (((0,), (0,)), ((), ())),
            preferred_element_type=F32,
        )
        for b in range(3):
            part = value[b * QUARTER : (b + 1) * QUARTER]
            if more:
                part = part + refs[8][a * 3 + b]
            out_ref[a * 3 + b] = part.astype(BF) if last else part


def weight_step(xs, gs, t, total):
    more, last = t > 0, t == STEPS - 1
    whole = block((9, QUARTER, CH), 0, 0, 0)
    operands = [*xs, *gs] + ([total] if more else [])
    return pl.pallas_call(
        lambda *refs: weight_kernel(more, last, *refs),
        grid=(1,),
        out_shape=jax.ShapeDtypeStruct((9, QUARTER, CH), BF if last else F32),
        in_specs=[block((1, ROWS, WIDE, QUARTER), t, 0, 0, 0)] * 4
        + [block((ROWS, WIDTH, CH), 0, 0, 0)] * 4
        + ([whole] if more else []),
        out_specs=whole,
        compiler_params=params(),
        cost_estimate=cost(9e8, 6e6),
    )(*operands)


def add(left, right):
    return (left.astype(F32) + right.astype(F32)).astype(BF)


def fold_far(part):
    return add(send(part[:, 1], FAR), part[:, 0])


def fold_ring(part):
    half = part.shape[-1] // 2
    ups, downs = part[..., :half], part[..., half:]
    up, down = ups[:, 3], downs[:, 1]
    for s in range(3):
        up = add(send(up, UP), ups[:, 2 - s])
        down = add(send(down, DOWN), downs[:, (s + 2) % 4])
    return jnp.concatenate([up, down], axis=-1)


def body(stored_inputs, filter_weights, pending_slopes, topmost_slopes):
    x = stored_inputs[:, 0]
    pending = pending_slopes[0]
    top = topmost_slopes
    weights = filter_weights[0].reshape(9, CH, CH)
    az = lax.axis_index("az")
    place = jnp.stack([az // 16, (az // 4) % 4, az % 4]).astype(jnp.int32)
    last = lax.axis_index("segment") == lax.axis_size("segment") - 1
    flag = last.astype(jnp.int32).reshape(1)
    scale = 1.0 / math.sqrt(STEPS * ROWS * WIDTH * lax.axis_size("az"))

    right_edge, left_edge = pack_edges(x, pending, top)
    low = send(right_edge, RIGHT)
    high = send(left_edge, LEFT)

    factors = slope_factors(x, low, high, weights, 0, 1)
    sent, own = back_step(pending, low, high, factors, weights, 0)
    arrived = relay(sent)
    emitted = [sent[:, :WIDTH]]
    factors = slope_factors(x, low, high, weights, 1, 3)

    spreads = spread(place, x, low, high)
    xs = [spreads[0], send(spreads[1], CORE), send(spreads[2], PAIR), send(spreads[3], DIAG)]

    total = None
    for t in range(STEPS):
        from_core = send(own, CORE)
        from_pair = send(own, PAIR)
        from_diag = send(from_pair, CORE)
        total = weight_step(xs, (own, from_core, from_pair, from_diag), t, total)
        if t + 1 < STEPS:
            sent, own = back_step(top, low, high, factors, weights, t + 1, flag, arrived)
            emitted.append(sent[:, :WIDTH])
            if t + 2 < STEPS:
                arrived = relay(sent)

    cut = CH // 2
    part = total.reshape(9, 2, 4, 16, CH)
    first = fold_ring(fold_far(part[..., :cut]))
    second = part[..., cut:].transpose(0, 2, 1, 3, 4).reshape(9, 4, 32, cut)
    second = fold_far(fold_ring(second).reshape(9, 2, 16, cut))
    summed = jnp.concatenate([first, second], axis=-1).astype(F32)
    weight_grads = (summed * scale).astype(BF).reshape(1, 3, 3, 16, CH)
    return (jnp.stack(emitted)[:, None], weight_grads)


def solution(mesh):
    return jax.shard_map(
        body,
        mesh=mesh,
        in_specs=(
            P(None, "segment", None, "az", None),
            P("segment", None, None, None, None),
            P("segment", None, "az", None),
            P(None, None, "az", None),
        ),
        out_specs=(P(None, "segment", None, "az", None), P("segment", None, None, "az", None)),
        check_vma=False,
    )
```

```python
import math

import jax
import jax.numpy as jnp
from jax import lax
from jax.experimental import pallas as pl
from jax.experimental.pallas import tpu as pltpu
from jax.sharding import PartitionSpec as P

BF = jnp.bfloat16
F32 = jnp.float32
ROWS, WIDTH, CH, STEPS = 3, 64, 512, 4
WIDE = WIDTH + 8
HALF = CH // 2


def az_route(move):
    route = []
    for i in range(32):
        h, z, c = move(i // 16, (i // 2) % 8, i % 2)
        route.append((i, (h % 2) * 16 + (z % 8) * 2 + c % 2))
    return route


RIGHT = [(i, (i + 1) % 32) for i in range(32)]
LEFT = [(i, (i - 1) % 32) for i in range(32)]
CORE = az_route(lambda h, z, c: (h, z, c + 1))
PAIR = az_route(lambda h, z, c: (h, z ^ 1, c))
FAR = az_route(lambda h, z, c: (h + 1, z, c))
UP = az_route(lambda h, z, c: (h, z + 2, c))
ACROSS = az_route(lambda h, z, c: (h, z + 4, c))
DOWN = az_route(lambda h, z, c: (h, z - 2, c))


def send(block, route):
    return lax.ppermute(block, "az", route)


def relay(block):
    count = lax.axis_size("segment")
    return lax.ppermute(block, "segment", [(i, i - 1) for i in range(1, count)])


def params(mib=24):
    return pltpu.CompilerParams(vmem_limit_bytes=mib * 1024 * 1024)


def cost(flops, size):
    return pl.CostEstimate(flops=int(flops), bytes_accessed=int(size), transcendentals=0)


VMEM = pl.BlockSpec(memory_space=pltpu.VMEM)
SMEM = pl.BlockSpec(memory_space=pltpu.SMEM)


def block(shape, *index):
    return pl.BlockSpec(shape, lambda *_: index)


def pack_kernel(x_right, p_right, t_right, x_left, p_left, t_left, right_ref, left_ref):
    for refs, first, out in (((x_right, p_right, t_right), 8, right_ref), ((x_left, p_left, t_left), 0, left_ref)):
        xs, ps, ts = refs
        for r in range(ROWS):
            planes = [xs[t, r] for t in range(STEPS)] + [ps[r]] + [ts[t, r] for t in range(STEPS - 1)]
            for n, plane in enumerate(planes):
                out[n * ROWS + r] = plane.astype(F32)[first : first + 8].astype(BF)


def pack_edges(x, pending, top):
    def specs(edge):
        return [
            block((STEPS, ROWS, 16, CH), 0, 0, edge, 0),
            block((ROWS, 16, CH), 0, edge, 0),
            block((STEPS - 1, ROWS, 16, CH), 0, 0, edge, 0),
        ]

    x, pending, top = (pltpu.with_memory_space_constraint(v, pltpu.HBM) for v in (x, pending, top))
    shape = jax.ShapeDtypeStruct((24, 8, CH), BF)
    return pl.pallas_call(
        pack_kernel,
        grid=(1,),
        out_shape=(shape, shape),
        in_specs=specs(3) + specs(0),
        out_specs=(block((24, 8, CH), 0, 0, 0),) * 2,
        compiler_params=params(),
        cost_estimate=cost(0, 1 << 20),
    )(x, pending, top, x, pending, top)


def first_four(high, low):
    pick = lax.broadcasted_iota(jnp.int32, high.shape, 0) < 4
    return jnp.where(pick, high, low)


def widen(own, high, low):
    return jnp.concatenate([own.astype(F32), first_four(high.astype(F32), low.astype(F32))], axis=0)


def factor_kernel(x_ref, low_ref, high_ref, w_ref, out_ref):
    wide = WIDTH + 16
    planes = [
        jnp.concatenate(
            [x_ref[0, r].astype(F32), high_ref[r].astype(F32), low_ref[r].astype(F32)], axis=0
        )
        for r in range(ROWS)
    ]
    field = jnp.concatenate(planes, axis=0).astype(BF)
    sums = []
    for b in range(3):
        up = jnp.dot(field[: 2 * wide], w_ref[b], preferred_element_type=F32)
        mid = jnp.dot(field, w_ref[3 + b], preferred_element_type=F32)
        down = jnp.dot(field[wide:], w_ref[6 + b], preferred_element_type=F32)
        rows = []
        for r in range(ROWS):
            value = mid[r * wide : (r + 1) * wide]
            if r > 0:
                value = value + up[(r - 1) * wide : r * wide]
            if r < 2:
                value = value + down[r * wide : (r + 1) * wide]
            rows.append(value)
        sums.append(rows)
    for r in range(ROWS):
        preact = pltpu.roll(sums[0][r], 1, 0) + sums[1][r] + pltpu.roll(sums[2][r], wide - 1, 0)
        gate = jax.nn.sigmoid(preact)
        value = gate * (1.0 + preact * (1.0 - gate))
        out_ref[0, r, :WIDTH] = value[:WIDTH]
        out_ref[0, r, WIDTH:] = first_four(value[WIDTH : WIDTH + 8], value[WIDTH + 8 :])


def slope_factors(x, low, high, weights, first):
    return pl.pallas_call(
        factor_kernel,
        grid=(1,),
        out_shape=jax.ShapeDtypeStruct((1, ROWS, WIDE, CH), F32),
        in_specs=[
            pl.BlockSpec((1, ROWS, WIDTH, CH), lambda n: (first + n, 0, 0, 0)),
            pl.BlockSpec((ROWS, 8, CH), lambda n: (first + n, 0, 0)),
            pl.BlockSpec((ROWS, 8, CH), lambda n: (first + n, 0, 0)),
            VMEM,
        ],
        out_specs=pl.BlockSpec((1, ROWS, WIDE, CH), lambda n: (n, 0, 0, 0)),
        compiler_params=params(),
        cost_estimate=cost(1.2e9, 5e6),
    )(x, low, high, weights)


def back_kernel(first, *refs):
    if first:
        own_ref, low_ref, high_ref, factor_ref, w_ref, sent_ref, grad_ref = refs
    else:
        flag_ref, own_ref, low_ref, high_ref, relay_ref, factor_ref, w_ref, sent_ref, grad_ref = refs
    slopes = []
    for r in range(ROWS):
        own = own_ref[r] if first else own_ref[0, r]
        slope = widen(own, high_ref[r], low_ref[r])
        if not first:
            slope = jnp.where(flag_ref[0] == 1, slope, relay_ref[r].astype(F32))
        slopes.append(slope)
    grads = []
    for r in range(ROWS):
        grad = slopes[r] * factor_ref[0, r]
        grad_ref[r] = grad.astype(BF)
        grads.append(grad)
    field = jnp.concatenate(grads, axis=0).astype(BF)
    above = jnp.concatenate(grads[1:], axis=0).astype(BF)
    below = jnp.concatenate(grads[:2], axis=0).astype(BF)
    turned = (((1,), (1,)), ((), ()))
    sums = []
    for b in range(3):
        up = lax.dot_general(above, w_ref[b], turned, preferred_element_type=F32)
        mid = lax.dot_general(field, w_ref[3 + b], turned, preferred_element_type=F32)
        down = lax.dot_general(below, w_ref[6 + b], turned, preferred_element_type=F32)
        rows = []
        for r in range(ROWS):
            value = mid[r * WIDE : (r + 1) * WIDE]
            if r < 2:
                value = value + up[r * WIDE : (r + 1) * WIDE]
            if r > 0:
                value = value + down[(r - 1) * WIDE : r * WIDE]
            rows.append(value)
        sums.append(rows)
    for r in range(ROWS):
        value = pltpu.roll(sums[0][r], WIDE - 1, 0) + sums[1][r] + pltpu.roll(sums[2][r], 1, 0)
        sent_ref[r] = (slopes[r] + value).astype(BF)


def back_step(own, low, high, factors, weights, t, flag=None, arrived=None):
    first = t == 0
    edge = block((ROWS, 8, CH), 4 + t, 0, 0)
    operands = [own, low, high]
    if first:
        specs = [block((ROWS, WIDTH, CH), 0, 0, 0), edge, edge]
    else:
        specs = [SMEM, block((1, ROWS, WIDTH, CH), t - 1, 0, 0, 0), edge, edge]
        specs += [block((ROWS, WIDE, CH), 0, 0, 0)]
        operands = [flag, *operands, arrived]
    specs += [block((1, ROWS, WIDE, CH), 0, 0, 0, 0), VMEM]
    return pl.pallas_call(
        lambda *refs: back_kernel(first, *refs),
        grid=(1,),
        out_shape=(
            jax.ShapeDtypeStruct((ROWS, WIDE, CH), BF),
            jax.ShapeDtypeStruct((ROWS, WIDE, CH), BF),
        ),
        in_specs=specs,
        out_specs=(block((ROWS, WIDE, CH), 0, 0, 0), block((ROWS, WIDE, CH), 0, 0, 0)),
        compiler_params=params(),
        cost_estimate=cost(1.1e9, 6e6),
    )(*operands, factors, weights)


def spread_kernel(place_ref, x_ref, out0, out1, order_ref):
    @pl.when(pl.program_id(0) == 0)
    def _():
        h, j, k, c = (place_ref[n] for n in range(4))
        lane = lax.broadcasted_iota(jnp.int32, (8, CH), 1)
        chip = jnp.bitwise_xor(lane // HALF, k)
        core = jnp.bitwise_xor(lane // 128 % 2, c)
        far = jnp.bitwise_xor(lane // 64 % 2, h)
        turn = jnp.bitwise_and(lane // 16 + j, 3)
        source = ((far * 4 + turn) * 4 + chip * 2 + core) * 16 + lane % 16
        row = lax.broadcasted_iota(jnp.int32, (CH, CH), 0)
        order_ref[...] = jnp.where(row == source[:1], 1.0, 0.0).astype(BF)

    field = jnp.concatenate([x_ref[0, r] for r in range(ROWS)], axis=0)
    value = jnp.dot(field, order_ref[...], preferred_element_type=F32)
    for n, out in enumerate((out0, out1)):
        for r in range(ROWS):
            out[0, r] = value[r * WIDTH : (r + 1) * WIDTH, n * HALF : (n + 1) * HALF].astype(BF)


def spread(place, x):
    shape = jax.ShapeDtypeStruct((STEPS, ROWS, WIDTH, HALF), BF)
    return pl.pallas_call(
        spread_kernel,
        grid=(STEPS,),
        out_shape=(shape,) * 2,
        in_specs=[
            SMEM,
            pl.BlockSpec((1, ROWS, WIDTH, CH), lambda n: (n, 0, 0, 0)),
        ],
        out_specs=(pl.BlockSpec((1, ROWS, WIDTH, HALF), lambda n: (n, 0, 0, 0)),) * 2,
        scratch_shapes=[pltpu.VMEM((CH, CH), BF)],
        compiler_params=params(),
        cost_estimate=cost(4.5e8, 2e6),
    )(place, x)


def tap_products(xs, gs):
    left, right = [], []
    for r in range(ROWS):
        left.append(jnp.concatenate([x[r] for x in xs], axis=0))
        taps = [[], [], []]
        for g in gs:
            plane = g[r].astype(F32)
            for b, shift in enumerate((WIDE - 1, 0, 1)):
                moved = pltpu.roll(plane, shift, 0) if shift else plane
                taps[b].append(moved[:WIDTH])
        right.append(
            jnp.concatenate([jnp.concatenate(parts, axis=0).astype(BF) for parts in taps], axis=1)
        )
    pairs = ((left[:2], right[1:]), (left, right), (left[1:], right[:2]))
    return [
        lax.dot_general(
            jnp.concatenate(ls, axis=0),
            jnp.concatenate(rs, axis=0),
            (((0,), (0,)), ((), ())),
            preferred_element_type=F32,
        )
        for ls, rs in pairs
    ]


def early_kernel(x0, x1, *refs):
    gs, out_ref = refs[:6], refs[6]
    for t in range(STEPS - 1):
        values = tap_products((x0[t], x1[t]), (gs[2 * t], gs[2 * t + 1]))
        for a, value in enumerate(values):
            out_ref[a] = value if t == 0 else out_ref[a] + value


def early_products(xs, gs):
    return pl.pallas_call(
        early_kernel,
        out_shape=jax.ShapeDtypeStruct((3, HALF, 3 * CH), F32),
        in_specs=[VMEM] * 8,
        out_specs=VMEM,
        compiler_params=params(),
        cost_estimate=cost(3e9, 8e6),
    )(*xs, *gs)


def late_kernel(x0, x1, g0, g1, total_ref, mine_ref, other_ref):
    for a, value in enumerate(tap_products((x0[0], x1[0]), (g0, g1))):
        value = value + total_ref[a]
        for b in range(3):
            for n, out in enumerate((mine_ref, other_ref)):
                for far in range(2):
                    for turn in range(4):
                        at = ((n * 2 + far) * 4 + turn) * 16
                        out[far, turn, a * 3 + b] = value[at : at + 16, b * CH : (b + 1) * CH].astype(BF)


def late_products(xs, gs, total):
    shape = jax.ShapeDtypeStruct((2, 4, 9, 16, CH), BF)
    whole = block((2, 4, 9, 16, CH), 0, 0, 0, 0, 0)
    return pl.pallas_call(
        late_kernel,
        grid=(1,),
        out_shape=(shape, shape),
        in_specs=[block((1, ROWS, WIDTH, HALF), STEPS - 1, 0, 0, 0)] * 2
        + [block((ROWS, WIDE, CH), 0, 0, 0)] * 2
        + [block((3, HALF, 3 * CH), 0, 0, 0)],
        out_specs=(whole, whole),
        compiler_params=params(),
        cost_estimate=cost(1e9, 8e6),
    )(*xs, *gs, total)


def grad_kernel(flag_ref, own_ref, low_ref, high_ref, relay_ref, factor_ref, grad_ref):
    for r in range(ROWS):
        slope = widen(own_ref[0, r], high_ref[r], low_ref[r])
        slope = jnp.where(flag_ref[0] == 1, slope, relay_ref[r].astype(F32))
        grad_ref[r] = (slope * factor_ref[0, r]).astype(BF)


def last_grad(flag, top, low, high, arrived, factors):
    edge = block((ROWS, 8, CH), 3 + STEPS, 0, 0)
    return pl.pallas_call(
        grad_kernel,
        grid=(1,),
        out_shape=jax.ShapeDtypeStruct((ROWS, WIDE, CH), BF),
        in_specs=[
            SMEM,
            block((1, ROWS, WIDTH, CH), STEPS - 2, 0, 0, 0),
            edge,
            edge,
            block((ROWS, WIDE, CH), 0, 0, 0),
            block((1, ROWS, WIDE, CH), 0, 0, 0, 0),
        ],
        out_specs=block((ROWS, WIDE, CH), 0, 0, 0),
        compiler_params=params(),
        cost_estimate=cost(1e6, 1e6),
    )(flag, top, low, high, arrived, factors)


def load_kernel(source_ref, out_ref, done):
    copy = pltpu.make_async_copy(source_ref, out_ref, done)
    copy.start()
    copy.wait()


def load(weights):
    return pl.pallas_call(
        load_kernel,
        out_shape=pltpu.VMEM(weights.shape, BF),
        in_specs=[pl.BlockSpec(memory_space=pltpu.HBM)],
        out_specs=VMEM,
        scratch_shapes=[pltpu.SemaphoreType.DMA],
        compiler_params=params(),
        cost_estimate=cost(0, 9e6),
    )(weights)


def total_of(*parts):
    value = parts[0].astype(F32)
    for part in parts[1:]:
        value = value + part.astype(F32)
    return value


def after(value, *others):
    return lax.optimization_barrier((value, *others))[0]


def body(stored_inputs, filter_weights, pending_slopes, topmost_slopes):
    x = stored_inputs[:, 0]
    pending = pending_slopes[0]
    top = topmost_slopes
    az = lax.axis_index("az")
    place = jnp.stack([az // 16, (az // 4) % 4, (az // 2) % 2, az % 2]).astype(jnp.int32)
    last = lax.axis_index("segment") == lax.axis_size("segment") - 1
    flag = last.astype(jnp.int32).reshape(1)
    scale = 1.0 / math.sqrt(STEPS * ROWS * WIDTH * lax.axis_size("az"))

    right_edge, left_edge = pack_edges(x, pending, top)
    low = send(right_edge, RIGHT)
    high = send(left_edge, LEFT)
    weights = load(after(filter_weights[0].reshape(9, CH, CH), right_edge))
    mine, other = spread(after(place, left_edge), x)
    xs = (mine, send(other, PAIR))

    emitted, fields = [], []
    slope, arrived = pending, None
    weights = pltpu.with_memory_space_constraint(weights, pltpu.VMEM)
    factors = slope_factors(after(x, mine), low, high, weights, 0)
    for t in range(STEPS):
        if t == STEPS - 1:
            own = last_grad(flag, top, low, high, arrived, factors)
            arrived, factors = lax.optimization_barrier((arrived, factors, own))[:2]
        sent, grad = back_step(slope, low, high, factors, weights, t, flag, arrived)
        emitted.append(sent[:, :WIDTH])
        slope = top
        if t < STEPS - 1:
            own = grad
            arrived = relay(sent)
            factors = slope_factors(after(x, sent), low, high, weights, t + 1)
            own = after(own, factors)
        fields.append((own, send(own, PAIR)))

    total = early_products(xs, [g for pair in fields[:-1] for g in pair])
    mine, other = late_products(xs, fields[-1], total)
    other = send(other, CORE)
    near = [total_of(mine[n], other[n]).astype(BF) for n in range(2)]
    near = total_of(near[0], send(near[1], FAR)).astype(BF)
    ups, across, downs = send(near[1], UP), send(near[2], ACROSS), send(near[3], DOWN)
    weight_grads = (total_of(near[0], ups, across, downs) * scale).astype(BF).reshape(1, 3, 3, 16, CH)
    return (jnp.stack(emitted)[:, None], weight_grads)


def solution(mesh):
    return jax.shard_map(
        body,
        mesh=mesh,
        in_specs=(
            P(None, "segment", None, "az", None),
            P("segment", None, None, None, None),
            P("segment", None, "az", None),
            P(None, None, "az", None),
        ),
        out_specs=(P(None, "segment", None, "az", None), P("segment", None, None, "az", None)),
        check_vma=False,
    )
```

```python
import math

import jax
import jax.numpy as jnp
from jax import lax
from jax.experimental import pallas as pl
from jax.experimental.pallas import tpu as pltpu
from jax.sharding import PartitionSpec as P

BF = jnp.bfloat16
F32 = jnp.float32
ROWS, WIDTH, CH, STEPS = 3, 64, 512, 4
WIDE = WIDTH + 8
HALF = CH // 2


def az_route(move):
    route = []
    for i in range(32):
        h, z, c = move(i // 16, (i // 2) % 8, i % 2)
        route.append((i, (h % 2) * 16 + (z % 8) * 2 + c % 2))
    return route


RIGHT = [(i, (i + 1) % 32) for i in range(32)]
LEFT = [(i, (i - 1) % 32) for i in range(32)]
CORE = az_route(lambda h, z, c: (h, z, c + 1))
PAIR = az_route(lambda h, z, c: (h, z ^ 1, c))
FAR = az_route(lambda h, z, c: (h + 1, z, c))
UP = az_route(lambda h, z, c: (h, z + 2, c))
ACROSS = az_route(lambda h, z, c: (h, z + 4, c))
DOWN = az_route(lambda h, z, c: (h, z - 2, c))


def send(block, route):
    return lax.ppermute(block, "az", route)


def relay(block):
    count = lax.axis_size("segment")
    return lax.ppermute(block, "segment", [(i, i - 1) for i in range(1, count)])


def params(mib=24):
    return pltpu.CompilerParams(vmem_limit_bytes=mib * 1024 * 1024)


def cost(flops, size):
    return pl.CostEstimate(flops=int(flops), bytes_accessed=int(size), transcendentals=0)


VMEM = pl.BlockSpec(memory_space=pltpu.VMEM)
SMEM = pl.BlockSpec(memory_space=pltpu.SMEM)


def block(shape, *index):
    return pl.BlockSpec(shape, lambda *_: index)


def pack_kernel(x_right, p_right, t_right, x_left, p_left, t_left, right_ref, left_ref):
    for refs, first, out in (((x_right, p_right, t_right), 8, right_ref), ((x_left, p_left, t_left), 0, left_ref)):
        xs, ps, ts = refs
        for r in range(ROWS):
            planes = [xs[t, r] for t in range(STEPS)] + [ps[r]] + [ts[t, r] for t in range(STEPS - 1)]
            for n, plane in enumerate(planes):
                out[n * ROWS + r] = plane.astype(F32)[first : first + 8].astype(BF)


def pack_edges(x, pending, top):
    def specs(edge):
        return [
            block((STEPS, ROWS, 16, CH), 0, 0, edge, 0),
            block((ROWS, 16, CH), 0, edge, 0),
            block((STEPS - 1, ROWS, 16, CH), 0, 0, edge, 0),
        ]

    x, pending, top = (pltpu.with_memory_space_constraint(v, pltpu.HBM) for v in (x, pending, top))
    shape = jax.ShapeDtypeStruct((24, 8, CH), BF)
    return pl.pallas_call(
        pack_kernel,
        grid=(1,),
        out_shape=(shape, shape),
        in_specs=specs(3) + specs(0),
        out_specs=(block((24, 8, CH), 0, 0, 0),) * 2,
        compiler_params=params(),
        cost_estimate=cost(0, 1 << 20),
    )(x, pending, top, x, pending, top)


def first_four(high, low):
    pick = lax.broadcasted_iota(jnp.int32, high.shape, 0) < 4
    return jnp.where(pick, high, low)


def widen(own, high, low):
    return jnp.concatenate([own.astype(F32), first_four(high.astype(F32), low.astype(F32))], axis=0)


def factor_kernel(x_ref, low_ref, high_ref, w_ref, out_ref):
    wide = WIDTH + 16
    planes = [
        jnp.concatenate(
            [x_ref[0, r].astype(F32), high_ref[r].astype(F32), low_ref[r].astype(F32)], axis=0
        )
        for r in range(ROWS)
    ]
    field = jnp.concatenate(planes, axis=0).astype(BF)
    sums = []
    for b in range(3):
        up = jnp.dot(field[: 2 * wide], w_ref[b], preferred_element_type=F32)
        mid = jnp.dot(field, w_ref[3 + b], preferred_element_type=F32)
        down = jnp.dot(field[wide:], w_ref[6 + b], preferred_element_type=F32)
        rows = []
        for r in range(ROWS):
            value = mid[r * wide : (r + 1) * wide]
            if r > 0:
                value = value + up[(r - 1) * wide : r * wide]
            if r < 2:
                value = value + down[r * wide : (r + 1) * wide]
            rows.append(value)
        sums.append(rows)
    for r in range(ROWS):
        preact = pltpu.roll(sums[0][r], 1, 0) + sums[1][r] + pltpu.roll(sums[2][r], wide - 1, 0)
        gate = jax.nn.sigmoid(preact)
        value = gate * (1.0 + preact * (1.0 - gate))
        out_ref[0, r, :WIDTH] = value[:WIDTH]
        out_ref[0, r, WIDTH:] = first_four(value[WIDTH : WIDTH + 8], value[WIDTH + 8 :])


def slope_factors(x, low, high, weights, first):
    weights = pltpu.with_memory_space_constraint(weights, pltpu.VMEM)
    return pl.pallas_call(
        factor_kernel,
        grid=(1,),
        out_shape=jax.ShapeDtypeStruct((1, ROWS, WIDE, CH), F32),
        in_specs=[
            pl.BlockSpec((1, ROWS, WIDTH, CH), lambda n: (first + n, 0, 0, 0)),
            pl.BlockSpec((ROWS, 8, CH), lambda n: (first + n, 0, 0)),
            pl.BlockSpec((ROWS, 8, CH), lambda n: (first + n, 0, 0)),
            VMEM,
        ],
        out_specs=pl.BlockSpec((1, ROWS, WIDE, CH), lambda n: (n, 0, 0, 0)),
        compiler_params=params(),
        cost_estimate=cost(1.2e9, 5e6),
    )(x, low, high, weights)


def back_kernel(first, *refs):
    if first:
        own_ref, low_ref, high_ref, factor_ref, w_ref, sent_ref, grad_ref = refs
    else:
        flag_ref, own_ref, low_ref, high_ref, relay_ref, factor_ref, w_ref, sent_ref, grad_ref = refs
    slopes = []
    for r in range(ROWS):
        own = own_ref[r] if first else own_ref[0, r]
        slope = widen(own, high_ref[r], low_ref[r])
        if not first:
            slope = jnp.where(flag_ref[0] == 1, slope, relay_ref[r].astype(F32))
        slopes.append(slope)
    grads = []
    for r in range(ROWS):
        grad = slopes[r] * factor_ref[0, r]
        grad_ref[r] = grad.astype(BF)
        grads.append(grad)
    field = jnp.concatenate(grads, axis=0).astype(BF)
    above = jnp.concatenate(grads[1:], axis=0).astype(BF)
    below = jnp.concatenate(grads[:2], axis=0).astype(BF)
    turned = (((1,), (1,)), ((), ()))
    sums = []
    for b in range(3):
        up = lax.dot_general(above, w_ref[b], turned, preferred_element_type=F32)
        mid = lax.dot_general(field, w_ref[3 + b], turned, preferred_element_type=F32)
        down = lax.dot_general(below, w_ref[6 + b], turned, preferred_element_type=F32)
        rows = []
        for r in range(ROWS):
            value = mid[r * WIDE : (r + 1) * WIDE]
            if r < 2:
                value = value + up[r * WIDE : (r + 1) * WIDE]
            if r > 0:
                value = value + down[(r - 1) * WIDE : r * WIDE]
            rows.append(value)
        sums.append(rows)
    for r in range(ROWS):
        value = pltpu.roll(sums[0][r], WIDE - 1, 0) + sums[1][r] + pltpu.roll(sums[2][r], 1, 0)
        sent_ref[r] = (slopes[r] + value).astype(BF)


def back_step(own, low, high, factors, weights, t, flag=None, arrived=None):
    first = t == 0
    weights = pltpu.with_memory_space_constraint(weights, pltpu.VMEM)
    edge = block((ROWS, 8, CH), 4 + t, 0, 0)
    operands = [own, low, high]
    if first:
        specs = [block((ROWS, WIDTH, CH), 0, 0, 0), edge, edge]
    else:
        specs = [SMEM, block((1, ROWS, WIDTH, CH), t - 1, 0, 0, 0), edge, edge]
        specs += [block((ROWS, WIDE, CH), 0, 0, 0)]
        operands = [flag, *operands, arrived]
    specs += [block((1, ROWS, WIDE, CH), 0, 0, 0, 0), VMEM]
    return pl.pallas_call(
        lambda *refs: back_kernel(first, *refs),
        grid=(1,),
        out_shape=(
            jax.ShapeDtypeStruct((ROWS, WIDE, CH), BF),
            jax.ShapeDtypeStruct((ROWS, WIDE, CH), BF),
        ),
        in_specs=specs,
        out_specs=(block((ROWS, WIDE, CH), 0, 0, 0), block((ROWS, WIDE, CH), 0, 0, 0)),
        compiler_params=params(),
        cost_estimate=cost(1.1e9, 6e6),
    )(*operands, factors, weights)


def spread_kernel(place_ref, x_ref, source_ref, out0, out1, w_ref, done):
    copy = pltpu.make_async_copy(source_ref, w_ref, done)
    copy.start()
    h, j, k, c = (place_ref[n] for n in range(4))
    lane = lax.broadcasted_iota(jnp.int32, (8, CH), 1)
    chip = jnp.bitwise_xor(lane // HALF, k)
    core = jnp.bitwise_xor(lane // 128 % 2, c)
    far = jnp.bitwise_xor(lane // 64 % 2, h)
    turn = jnp.bitwise_and(lane // 16 + j, 3)
    source = ((far * 4 + turn) * 4 + chip * 2 + core) * 16 + lane % 16
    row = lax.broadcasted_iota(jnp.int32, (CH, CH), 0)
    order = jnp.where(row == source[:1], 1.0, 0.0).astype(BF)
    field = jnp.concatenate([x_ref[t, r] for t in range(STEPS) for r in range(ROWS)], axis=0)
    value = jnp.dot(field, order, preferred_element_type=F32).astype(BF)
    for n, out in enumerate((out0, out1)):
        for t in range(STEPS):
            for r in range(ROWS):
                at = (t * ROWS + r) * WIDTH
                out[t, r] = value[at : at + WIDTH, n * HALF : (n + 1) * HALF]
    copy.wait()


def spread(place, x, weights):
    weights = pltpu.with_memory_space_constraint(weights, pltpu.HBM)
    shape = jax.ShapeDtypeStruct((STEPS, ROWS, WIDTH, HALF), BF)
    return pl.pallas_call(
        spread_kernel,
        out_shape=(shape, shape, pltpu.VMEM(weights.shape, BF)),
        in_specs=[SMEM, VMEM, pl.BlockSpec(memory_space=pltpu.HBM)],
        out_specs=(VMEM, VMEM, VMEM),
        scratch_shapes=[pltpu.SemaphoreType.DMA],
        compiler_params=params(),
        cost_estimate=cost(4.5e8, 1.2e7),
    )(place, x, weights)


def tap_products(xs, gs):
    left, right = [], []
    for r in range(ROWS):
        left.append(jnp.concatenate([x[r] for x in xs], axis=0))
        taps = [[], [], []]
        for g in gs:
            plane = g[r].astype(F32)
            for b, shift in enumerate((WIDE - 1, 0, 1)):
                moved = pltpu.roll(plane, shift, 0) if shift else plane
                taps[b].append(moved[:WIDTH])
        right.append(
            jnp.concatenate([jnp.concatenate(parts, axis=0).astype(BF) for parts in taps], axis=1)
        )
    pairs = ((left[:2], right[1:]), (left, right), (left[1:], right[:2]))
    return [
        lax.dot_general(
            jnp.concatenate(ls, axis=0),
            jnp.concatenate(rs, axis=0),
            (((0,), (0,)), ((), ())),
            preferred_element_type=F32,
        )
        for ls, rs in pairs
    ]


def early_kernel(x0, x1, both0, both1, third0, third1, out_ref):
    for t in range(STEPS - 1):
        gs = (both0[t], both1[t]) if t < 2 else (third0, third1)
        values = tap_products((x0[t], x1[t]), gs)
        for a, value in enumerate(values):
            out_ref[a] = value if t == 0 else out_ref[a] + value


def early_products(xs, *gs):
    return pl.pallas_call(
        early_kernel,
        out_shape=jax.ShapeDtypeStruct((3, HALF, 3 * CH), F32),
        in_specs=[VMEM] * 6,
        out_specs=VMEM,
        compiler_params=params(),
        cost_estimate=cost(3e9, 8e6),
    )(*xs, *gs)


def late_kernel(x0, x1, g0, g1, total_ref, *outs):
    for a, value in enumerate(tap_products((x0[0], x1[0]), (g0, g1))):
        value = value + total_ref[a]
        for b in range(3):
            for n, out in enumerate(outs):
                core, lanes = n // 2, b * CH + n % 2 * HALF
                for far in range(2):
                    for turn in range(4):
                        at = ((core * 2 + far) * 4 + turn) * 16
                        out[far, turn, a * 3 + b] = value[at : at + 16, lanes : lanes + HALF].astype(BF)


def late_products(xs, gs, total):
    shape = jax.ShapeDtypeStruct((2, 4, 9, 16, HALF), BF)
    whole = block((2, 4, 9, 16, HALF), 0, 0, 0, 0, 0)
    return pl.pallas_call(
        late_kernel,
        grid=(1,),
        out_shape=(shape,) * 4,
        in_specs=[block((1, ROWS, WIDTH, HALF), STEPS - 1, 0, 0, 0)] * 2
        + [block((ROWS, WIDE, CH), 0, 0, 0)] * 2
        + [block((3, HALF, 3 * CH), 0, 0, 0)],
        out_specs=(whole,) * 4,
        compiler_params=params(),
        cost_estimate=cost(1e9, 8e6),
    )(*xs, *gs, total)


def grad_kernel(flag_ref, own_ref, low_ref, high_ref, relay_ref, factor_ref, grad_ref):
    for r in range(ROWS):
        slope = widen(own_ref[0, r], high_ref[r], low_ref[r])
        slope = jnp.where(flag_ref[0] == 1, slope, relay_ref[r].astype(F32))
        grad_ref[r] = (slope * factor_ref[0, r]).astype(BF)


def last_grad(flag, top, low, high, arrived, factors):
    edge = block((ROWS, 8, CH), 3 + STEPS, 0, 0)
    return pl.pallas_call(
        grad_kernel,
        grid=(1,),
        out_shape=jax.ShapeDtypeStruct((ROWS, WIDE, CH), BF),
        in_specs=[
            SMEM,
            block((1, ROWS, WIDTH, CH), STEPS - 2, 0, 0, 0),
            edge,
            edge,
            block((ROWS, WIDE, CH), 0, 0, 0),
            block((1, ROWS, WIDE, CH), 0, 0, 0, 0),
        ],
        out_specs=block((ROWS, WIDE, CH), 0, 0, 0),
        compiler_params=params(),
        cost_estimate=cost(1e6, 1e6),
    )(flag, top, low, high, arrived, factors)


def total_of(*parts):
    value = parts[0].astype(F32)
    for part in parts[1:]:
        value = value + part.astype(F32)
    return value


def after(value, *others):
    return lax.optimization_barrier((value, *others))[0]


def body(stored_inputs, filter_weights, pending_slopes, topmost_slopes):
    x = stored_inputs[:, 0]
    pending = pending_slopes[0]
    top = topmost_slopes
    az = lax.axis_index("az")
    place = jnp.stack([az // 16, (az // 4) % 4, (az // 2) % 2, az % 2]).astype(jnp.int32)
    last = lax.axis_index("segment") == lax.axis_size("segment") - 1
    flag = last.astype(jnp.int32).reshape(1)
    scale = 1.0 / math.sqrt(STEPS * ROWS * WIDTH * lax.axis_size("az"))

    right_edge, left_edge = pack_edges(x, pending, top)
    low = send(right_edge, RIGHT)
    high = send(left_edge, LEFT)
    taps = filter_weights[0].reshape(9, CH, CH)
    mine, other, weights = spread(after(place, left_edge), x, taps)
    xs = (mine, send(other, PAIR))

    emitted, fields = [], []
    slope, arrived = pending, None
    weights = pltpu.with_memory_space_constraint(weights, pltpu.VMEM)
    factors = slope_factors(x, low, high, weights, 0)
    for t in range(STEPS):
        if t == STEPS - 1:
            own = last_grad(flag, top, low, high, arrived, factors)
        else:
            sent, grad = back_step(slope, low, high, factors, weights, t, flag, arrived)
            emitted.append(sent[:, :WIDTH])
            slope, weights = top, taps
            own = grad
            arrived = relay(sent)
            waits = (sent, *xs) if t == 1 else (sent,)
            factors = slope_factors(after(x, *waits), low, high, weights, t + 1)
            own = after(own, factors)
            if t == 1:
                own = jnp.stack([fields[0], own])
                fields = []
        fields.append(own if t == 0 else (own, send(own, PAIR)))

    total = early_products(xs, *fields[0], *fields[1])
    parts = late_products(xs, fields[-1], total)
    sums = []
    for n in range(2):
        mine, other = parts[n], send(parts[2 + n], CORE)
        near = [total_of(mine[m], other[m]).astype(BF) for m in range(2)]
        if n == 1:
            arrived = after(arrived, near[1])
        near = total_of(near[0], send(near[1], FAR)).astype(BF)
        across, ups, downs = send(near[2], ACROSS), send(near[1], UP), send(near[3], DOWN)
        sums.append(total_of(near[0], ups, across, downs))
    sent, _ = back_step(top, low, high, factors, taps, STEPS - 1, flag, arrived)
    emitted.append(sent[:, :WIDTH])
    weight_grads = (jnp.concatenate(sums, axis=-1) * scale).astype(BF).reshape(1, 3, 3, 16, CH)
    return (jnp.stack(emitted)[:, None], weight_grads)


def solution(mesh):
    return jax.shard_map(
        body,
        mesh=mesh,
        in_specs=(
            P(None, "segment", None, "az", None),
            P("segment", None, None, None, None),
            P("segment", None, "az", None),
            P(None, None, "az", None),
        ),
        out_specs=(P(None, "segment", None, "az", None), P("segment", None, None, "az", None)),
        check_vma=False,
    )
```

```python
import math

import jax
import jax.numpy as jnp
from jax import lax
from jax.experimental import pallas as pl
from jax.experimental.pallas import tpu as pltpu
from jax.sharding import PartitionSpec as P

BF = jnp.bfloat16
F32 = jnp.float32
ROWS, WIDTH, CH, STEPS = 3, 64, 512, 4
WIDE = WIDTH + 8
HALF = CH // 2


def az_route(move):
    route = []
    for i in range(32):
        h, z, c = move(i // 16, (i // 2) % 8, i % 2)
        route.append((i, (h % 2) * 16 + (z % 8) * 2 + c % 2))
    return route


RIGHT = [(i, (i + 1) % 32) for i in range(32)]
LEFT = [(i, (i - 1) % 32) for i in range(32)]
CORE = az_route(lambda h, z, c: (h, z, c + 1))
PAIR = az_route(lambda h, z, c: (h, z ^ 1, c))
FAR = az_route(lambda h, z, c: (h + 1, z, c))
UP = az_route(lambda h, z, c: (h, z + 2, c))
ACROSS = az_route(lambda h, z, c: (h, z + 4, c))
DOWN = az_route(lambda h, z, c: (h, z - 2, c))


def send(block, route):
    return lax.ppermute(block, "az", route)


def relay(block):
    count = lax.axis_size("segment")
    return lax.ppermute(block, "segment", [(i, i - 1) for i in range(1, count)])


def params(mib=24):
    return pltpu.CompilerParams(vmem_limit_bytes=mib * 1024 * 1024)


def cost(flops, size):
    return pl.CostEstimate(flops=int(flops), bytes_accessed=int(size), transcendentals=0)


VMEM = pl.BlockSpec(memory_space=pltpu.VMEM)
SMEM = pl.BlockSpec(memory_space=pltpu.SMEM)


def block(shape, *index):
    return pl.BlockSpec(shape, lambda *_: index)


def pack_kernel(x_right, p_right, t_right, x_left, p_left, t_left, right_ref, left_ref):
    for refs, first, out in (((x_right, p_right, t_right), 8, right_ref), ((x_left, p_left, t_left), 0, left_ref)):
        xs, ps, ts = refs
        for r in range(ROWS):
            planes = [xs[t, r] for t in range(STEPS)] + [ps[r]] + [ts[t, r] for t in range(STEPS - 1)]
            for n, plane in enumerate(planes):
                out[n * ROWS + r] = plane.astype(F32)[first : first + 8].astype(BF)


def pack_edges(x, pending, top):
    def specs(edge):
        return [
            block((STEPS, ROWS, 16, CH), 0, 0, edge, 0),
            block((ROWS, 16, CH), 0, edge, 0),
            block((STEPS - 1, ROWS, 16, CH), 0, 0, edge, 0),
        ]

    x, pending, top = (pltpu.with_memory_space_constraint(v, pltpu.HBM) for v in (x, pending, top))
    shape = jax.ShapeDtypeStruct((24, 8, CH), BF)
    return pl.pallas_call(
        pack_kernel,
        grid=(1,),
        out_shape=(shape, shape),
        in_specs=specs(3) + specs(0),
        out_specs=(block((24, 8, CH), 0, 0, 0),) * 2,
        compiler_params=params(),
        cost_estimate=cost(0, 1 << 20),
    )(x, pending, top, x, pending, top)


def first_four(high, low):
    pick = lax.broadcasted_iota(jnp.int32, high.shape, 0) < 4
    return jnp.where(pick, high, low)


def widen(own, high, low):
    return jnp.concatenate([own.astype(F32), first_four(high.astype(F32), low.astype(F32))], axis=0)


def factor_kernel(x_ref, low_ref, high_ref, w_ref, out_ref):
    wide = WIDTH + 16
    planes = [
        jnp.concatenate(
            [x_ref[0, r].astype(F32), high_ref[r].astype(F32), low_ref[r].astype(F32)], axis=0
        )
        for r in range(ROWS)
    ]
    field = jnp.concatenate(planes, axis=0).astype(BF)
    sums = []
    for b in range(3):
        up = jnp.dot(field[: 2 * wide], w_ref[b], preferred_element_type=F32)
        mid = jnp.dot(field, w_ref[3 + b], preferred_element_type=F32)
        down = jnp.dot(field[wide:], w_ref[6 + b], preferred_element_type=F32)
        rows = []
        for r in range(ROWS):
            value = mid[r * wide : (r + 1) * wide]
            if r > 0:
                value = value + up[(r - 1) * wide : r * wide]
            if r < 2:
                value = value + down[r * wide : (r + 1) * wide]
            rows.append(value)
        sums.append(rows)
    for r in range(ROWS):
        preact = pltpu.roll(sums[0][r], 1, 0) + sums[1][r] + pltpu.roll(sums[2][r], wide - 1, 0)
        gate = jax.nn.sigmoid(preact)
        value = gate * (1.0 + preact * (1.0 - gate))
        out_ref[0, r, :WIDTH] = value[:WIDTH]
        out_ref[0, r, WIDTH:] = first_four(value[WIDTH : WIDTH + 8], value[WIDTH + 8 :])


def slope_factors(x, low, high, weights, first):
    weights = pltpu.with_memory_space_constraint(weights, pltpu.VMEM)
    return pl.pallas_call(
        factor_kernel,
        grid=(1,),
        out_shape=jax.ShapeDtypeStruct((1, ROWS, WIDE, CH), F32),
        in_specs=[
            pl.BlockSpec((1, ROWS, WIDTH, CH), lambda n: (first + n, 0, 0, 0)),
            pl.BlockSpec((ROWS, 8, CH), lambda n: (first + n, 0, 0)),
            pl.BlockSpec((ROWS, 8, CH), lambda n: (first + n, 0, 0)),
            VMEM,
        ],
        out_specs=pl.BlockSpec((1, ROWS, WIDE, CH), lambda n: (n, 0, 0, 0)),
        compiler_params=params(),
        cost_estimate=cost(1.2e9, 5e6),
    )(x, low, high, weights)


def back_kernel(first, *refs):
    if first:
        own_ref, low_ref, high_ref, factor_ref, w_ref, sent_ref, grad_ref = refs
    else:
        flag_ref, own_ref, low_ref, high_ref, relay_ref, factor_ref, w_ref, sent_ref, grad_ref = refs
    slopes = []
    for r in range(ROWS):
        own = own_ref[r] if first else own_ref[0, r]
        slope = widen(own, high_ref[r], low_ref[r])
        if not first:
            slope = jnp.where(flag_ref[0] == 1, slope, relay_ref[r].astype(F32))
        slopes.append(slope)
    grads = []
    for r in range(ROWS):
        grad = slopes[r] * factor_ref[0, r]
        grad_ref[r] = grad.astype(BF)
        grads.append(grad)
    field = jnp.concatenate(grads, axis=0).astype(BF)
    above = jnp.concatenate(grads[1:], axis=0).astype(BF)
    below = jnp.concatenate(grads[:2], axis=0).astype(BF)
    turned = (((1,), (1,)), ((), ()))
    sums = []
    for b in range(3):
        up = lax.dot_general(above, w_ref[b], turned, preferred_element_type=F32)
        mid = lax.dot_general(field, w_ref[3 + b], turned, preferred_element_type=F32)
        down = lax.dot_general(below, w_ref[6 + b], turned, preferred_element_type=F32)
        rows = []
        for r in range(ROWS):
            value = mid[r * WIDE : (r + 1) * WIDE]
            if r < 2:
                value = value + up[r * WIDE : (r + 1) * WIDE]
            if r > 0:
                value = value + down[(r - 1) * WIDE : r * WIDE]
            rows.append(value)
        sums.append(rows)
    for r in range(ROWS):
        value = pltpu.roll(sums[0][r], WIDE - 1, 0) + sums[1][r] + pltpu.roll(sums[2][r], 1, 0)
        sent_ref[r] = (slopes[r] + value).astype(BF)


def back_step(own, low, high, factors, weights, t, flag=None, arrived=None):
    first = t == 0
    weights = pltpu.with_memory_space_constraint(weights, pltpu.VMEM)
    edge = block((ROWS, 8, CH), 4 + t, 0, 0)
    operands = [own, low, high]
    if first:
        specs = [block((ROWS, WIDTH, CH), 0, 0, 0), edge, edge]
    else:
        specs = [SMEM, block((1, ROWS, WIDTH, CH), t - 1, 0, 0, 0), edge, edge]
        specs += [block((ROWS, WIDE, CH), 0, 0, 0)]
        operands = [flag, *operands, arrived]
    specs += [block((1, ROWS, WIDE, CH), 0, 0, 0, 0), VMEM]
    return pl.pallas_call(
        lambda *refs: back_kernel(first, *refs),
        grid=(1,),
        out_shape=(
            jax.ShapeDtypeStruct((ROWS, WIDE, CH), BF),
            jax.ShapeDtypeStruct((ROWS, WIDE, CH), BF),
        ),
        in_specs=specs,
        out_specs=(block((ROWS, WIDE, CH), 0, 0, 0), block((ROWS, WIDE, CH), 0, 0, 0)),
        compiler_params=params(),
        cost_estimate=cost(1.1e9, 6e6),
    )(*operands, factors, weights)


def spread_kernel(place_ref, x_ref, source_ref, out0, out1, w_ref, field_ref, done):
    copies = [pltpu.make_async_copy(x_ref.at[t], field_ref.at[t], done.at[t]) for t in range(STEPS)]
    copies.append(pltpu.make_async_copy(source_ref, w_ref, done.at[STEPS]))
    for copy in copies:
        copy.start()
    h, j, k, c = (place_ref[n] for n in range(4))
    lane = lax.broadcasted_iota(jnp.int32, (8, CH), 1)
    chip = jnp.bitwise_xor(lane // HALF, k)
    core = jnp.bitwise_xor(lane // 128 % 2, c)
    far = jnp.bitwise_xor(lane // 64 % 2, h)
    turn = jnp.bitwise_and(lane // 16 + j, 3)
    source = ((far * 4 + turn) * 4 + chip * 2 + core) * 16 + lane % 16
    row = lax.broadcasted_iota(jnp.int32, (CH, CH), 0)
    order = jnp.where(row == source[:1], 1.0, 0.0).astype(BF)
    for t in range(STEPS):
        copies[t].wait()
        field = jnp.concatenate([field_ref[t, r] for r in range(ROWS)], axis=0)
        value = jnp.dot(field, order, preferred_element_type=F32).astype(BF)
        for n, out in enumerate((out0, out1)):
            for r in range(ROWS):
                out[t, r] = value[r * WIDTH : (r + 1) * WIDTH, n * HALF : (n + 1) * HALF]
    copies[STEPS].wait()


def spread(place, x, weights):
    x, weights = (pltpu.with_memory_space_constraint(v, pltpu.HBM) for v in (x, weights))
    shape = jax.ShapeDtypeStruct((STEPS, ROWS, WIDTH, HALF), BF)
    return pl.pallas_call(
        spread_kernel,
        out_shape=(shape, shape, pltpu.VMEM(weights.shape, BF)),
        in_specs=[SMEM, pl.BlockSpec(memory_space=pltpu.HBM), pl.BlockSpec(memory_space=pltpu.HBM)],
        out_specs=(VMEM, VMEM, VMEM),
        scratch_shapes=[
            pltpu.VMEM((STEPS, ROWS, WIDTH, CH), BF),
            pltpu.SemaphoreType.DMA((STEPS + 1,)),
        ],
        compiler_params=params(),
        cost_estimate=cost(4.5e8, 1.2e7),
    )(place, x, weights)


def tap_products(xs, gs):
    left, right = [], []
    for r in range(ROWS):
        left.append(jnp.concatenate([x[r] for x in xs], axis=0))
        taps = [[], [], []]
        for g in gs:
            plane = g[r].astype(F32)
            for b, shift in enumerate((WIDE - 1, 0, 1)):
                moved = pltpu.roll(plane, shift, 0) if shift else plane
                taps[b].append(moved[:WIDTH])
        right.append(
            jnp.concatenate([jnp.concatenate(parts, axis=0).astype(BF) for parts in taps], axis=1)
        )
    pairs = ((left[:2], right[1:]), (left, right), (left[1:], right[:2]))
    return [
        lax.dot_general(
            jnp.concatenate(ls, axis=0),
            jnp.concatenate(rs, axis=0),
            (((0,), (0,)), ((), ())),
            preferred_element_type=F32,
        )
        for ls, rs in pairs
    ]


def early_kernel(x0, x1, both0, both1, third0, third1, out_ref):
    for t in range(STEPS - 1):
        gs = (both0[t], both1[t]) if t < 2 else (third0, third1)
        values = tap_products((x0[t], x1[t]), gs)
        for a, value in enumerate(values):
            out_ref[a] = value if t == 0 else out_ref[a] + value


def early_products(xs, *gs):
    return pl.pallas_call(
        early_kernel,
        out_shape=jax.ShapeDtypeStruct((3, HALF, 3 * CH), F32),
        in_specs=[VMEM] * 6,
        out_specs=VMEM,
        compiler_params=params(),
        cost_estimate=cost(3e9, 8e6),
    )(*xs, *gs)


FIRST = 6


def late_kernel(x0, x1, g0, g1, total_ref, *outs):
    for a, value in enumerate(tap_products((x0[0], x1[0]), (g0, g1))):
        value = value + total_ref[a]
        for b in range(3):
            tap = a * 3 + b
            for core in range(2):
                for far in range(2):
                    for turn in range(4):
                        at = ((core * 2 + far) * 4 + turn) * 16
                        part = value[at : at + 16, b * CH : (b + 1) * CH].astype(BF)
                        if tap < FIRST:
                            outs[core][far, turn, tap] = part
                        else:
                            outs[2 + core][turn, far, tap - FIRST] = part


def late_products(xs, gs, total):
    shapes = [(2, 4, FIRST, 16, CH)] * 2 + [(4, 2, 9 - FIRST, 16, CH)] * 2
    return pl.pallas_call(
        late_kernel,
        grid=(1,),
        out_shape=tuple(jax.ShapeDtypeStruct(shape, BF) for shape in shapes),
        in_specs=[block((1, ROWS, WIDTH, HALF), STEPS - 1, 0, 0, 0)] * 2
        + [block((ROWS, WIDE, CH), 0, 0, 0)] * 2
        + [block((3, HALF, 3 * CH), 0, 0, 0)],
        out_specs=tuple(block(shape, 0, 0, 0, 0, 0) for shape in shapes),
        compiler_params=params(),
        cost_estimate=cost(1e9, 8e6),
    )(*xs, *gs, total)


def grad_kernel(flag_ref, own_ref, low_ref, high_ref, relay_ref, factor_ref, grad_ref):
    for r in range(ROWS):
        slope = widen(own_ref[0, r], high_ref[r], low_ref[r])
        slope = jnp.where(flag_ref[0] == 1, slope, relay_ref[r].astype(F32))
        grad_ref[r] = (slope * factor_ref[0, r]).astype(BF)


def last_grad(flag, top, low, high, arrived, factors):
    edge = block((ROWS, 8, CH), 3 + STEPS, 0, 0)
    return pl.pallas_call(
        grad_kernel,
        grid=(1,),
        out_shape=jax.ShapeDtypeStruct((ROWS, WIDE, CH), BF),
        in_specs=[
            SMEM,
            block((1, ROWS, WIDTH, CH), STEPS - 2, 0, 0, 0),
            edge,
            edge,
            block((ROWS, WIDE, CH), 0, 0, 0),
            block((1, ROWS, WIDE, CH), 0, 0, 0, 0),
        ],
        out_specs=block((ROWS, WIDE, CH), 0, 0, 0),
        compiler_params=params(),
        cost_estimate=cost(1e6, 1e6),
    )(flag, top, low, high, arrived, factors)


def total_of(*parts):
    value = parts[0].astype(F32)
    for part in parts[1:]:
        value = value + part.astype(F32)
    return value


def after(value, *others):
    return lax.optimization_barrier((value, *others))[0]


def body(stored_inputs, filter_weights, pending_slopes, topmost_slopes):
    x = stored_inputs[:, 0]
    pending = pending_slopes[0]
    top = topmost_slopes
    az = lax.axis_index("az")
    place = jnp.stack([az // 16, (az // 4) % 4, (az // 2) % 2, az % 2]).astype(jnp.int32)
    last = lax.axis_index("segment") == lax.axis_size("segment") - 1
    flag = last.astype(jnp.int32).reshape(1)
    scale = 1.0 / math.sqrt(STEPS * ROWS * WIDTH * lax.axis_size("az"))

    right_edge, left_edge = pack_edges(x, pending, top)
    low = send(right_edge, RIGHT)
    high = send(left_edge, LEFT)
    taps = filter_weights[0].reshape(9, CH, CH)
    mine, other, weights = spread(after(place, left_edge), x, taps)
    xs = (mine, send(other, PAIR))

    emitted, fields = [], []
    slope, arrived = pending, None
    weights = pltpu.with_memory_space_constraint(weights, pltpu.VMEM)
    factors = slope_factors(x, low, high, weights, 0)
    for t in range(STEPS):
        if t == STEPS - 1:
            own = last_grad(flag, top, low, high, arrived, factors)
        else:
            sent, grad = back_step(slope, low, high, factors, weights, t, flag, arrived)
            emitted.append(sent[:, :WIDTH])
            slope, weights = top, taps
            own = grad
            arrived = relay(sent)
            waits = (sent, *xs) if t == 1 else (sent,)
            factors = slope_factors(after(x, *waits), low, high, weights, t + 1)
            own = after(own, factors)
            if t == 1:
                own = jnp.stack([fields[0], own])
                fields = []
        fields.append(own if t == 0 else (own, send(own, PAIR)))

    total = early_products(xs, *fields[0], *fields[1])
    mine, other, mine_b, other_b = late_products(xs, fields[-1], total)
    other = send(other, CORE)
    near = [total_of(mine[m], other[m]).astype(BF) for m in range(2)]
    far = send(near[1], FAR)
    other_b = send(after(other_b, near[1]), CORE)
    turns = [total_of(mine_b[m], other_b[m]).astype(BF) for m in range(4)]
    arrived = after(arrived, turns[1], turns[2], turns[3])
    arriving = (send(turns[2], ACROSS), send(turns[1], UP), send(turns[3], DOWN))
    near = total_of(near[0], far).astype(BF)
    across, ups, downs = send(near[2], ACROSS), send(near[1], UP), send(near[3], DOWN)
    arriving = lax.optimization_barrier((*arriving, near))[:3]
    turned = total_of(turns[0], *arriving).astype(BF)
    far = send(turned[1], FAR)
    sums = [total_of(near[0], ups, across, downs), total_of(turned[0], far)]
    sent, _ = back_step(top, low, high, factors, taps, STEPS - 1, flag, arrived)
    emitted.append(sent[:, :WIDTH])
    weight_grads = (jnp.concatenate(sums, axis=0) * scale).astype(BF).reshape(1, 3, 3, 16, CH)
    return (jnp.stack(emitted)[:, None], weight_grads)


def solution(mesh):
    return jax.shard_map(
        body,
        mesh=mesh,
        in_specs=(
            P(None, "segment", None, "az", None),
            P("segment", None, None, None, None),
            P("segment", None, "az", None),
            P(None, None, "az", None),
        ),
        out_specs=(P(None, "segment", None, "az", None), P("segment", None, None, "az", None)),
        check_vma=False,
    )
```

```python
import math

import jax
import jax.numpy as jnp
from jax import lax
from jax.experimental import pallas as pl
from jax.experimental.pallas import tpu as pltpu
from jax.sharding import PartitionSpec as P

BF = jnp.bfloat16
F32 = jnp.float32
ROWS, WIDTH, CH, STEPS = 3, 64, 512, 4
WIDE = WIDTH + 8
HALF = CH // 2


def az_route(move):
    route = []
    for i in range(32):
        h, z, c = move(i // 16, (i // 2) % 8, i % 2)
        route.append((i, (h % 2) * 16 + (z % 8) * 2 + c % 2))
    return route


RIGHT = [(i, (i + 1) % 32) for i in range(32)]
LEFT = [(i, (i - 1) % 32) for i in range(32)]
CORE = az_route(lambda h, z, c: (h, z, c + 1))
PAIR = az_route(lambda h, z, c: (h, z ^ 1, c))
FAR = az_route(lambda h, z, c: (h + 1, z, c))
UP = az_route(lambda h, z, c: (h, z + 2, c))
ACROSS = az_route(lambda h, z, c: (h, z + 4, c))
DOWN = az_route(lambda h, z, c: (h, z - 2, c))


def send(block, route):
    return lax.ppermute(block, "az", route)


def relay(block):
    count = lax.axis_size("segment")
    return lax.ppermute(block, "segment", [(i, i - 1) for i in range(1, count)])


def params(mib=24):
    return pltpu.CompilerParams(vmem_limit_bytes=mib * 1024 * 1024)


def cost(flops, size):
    return pl.CostEstimate(flops=int(flops), bytes_accessed=int(size), transcendentals=0)


VMEM = pl.BlockSpec(memory_space=pltpu.VMEM)
SMEM = pl.BlockSpec(memory_space=pltpu.SMEM)


def block(shape, *index):
    return pl.BlockSpec(shape, lambda *_: index)


def pack_kernel(x_right, p_right, t_right, x_left, p_left, t_left, right_ref, left_ref):
    for refs, first, out in (((x_right, p_right, t_right), 8, right_ref), ((x_left, p_left, t_left), 0, left_ref)):
        xs, ps, ts = refs
        for r in range(ROWS):
            planes = [xs[t, r] for t in range(STEPS)] + [ps[r]] + [ts[t, r] for t in range(STEPS - 1)]
            for n, plane in enumerate(planes):
                out[n * ROWS + r] = plane.astype(F32)[first : first + 8].astype(BF)


def pack_edges(x, pending, top):
    def specs(edge):
        return [
            block((STEPS, ROWS, 16, CH), 0, 0, edge, 0),
            block((ROWS, 16, CH), 0, edge, 0),
            block((STEPS - 1, ROWS, 16, CH), 0, 0, edge, 0),
        ]

    x, pending, top = (pltpu.with_memory_space_constraint(v, pltpu.HBM) for v in (x, pending, top))
    shape = jax.ShapeDtypeStruct((24, 8, CH), BF)
    return pl.pallas_call(
        pack_kernel,
        grid=(1,),
        out_shape=(shape, shape),
        in_specs=specs(3) + specs(0),
        out_specs=(block((24, 8, CH), 0, 0, 0),) * 2,
        compiler_params=params(),
        cost_estimate=cost(0, 1 << 20),
    )(x, pending, top, x, pending, top)


def first_four(high, low):
    pick = lax.broadcasted_iota(jnp.int32, high.shape, 0) < 4
    return jnp.where(pick, high, low)


def widen(own, high, low):
    return jnp.concatenate([own.astype(F32), first_four(high.astype(F32), low.astype(F32))], axis=0)


def factor_kernel(x_ref, low_ref, high_ref, w_ref, out_ref):
    wide = WIDTH + 16
    planes = [
        jnp.concatenate(
            [x_ref[0, r].astype(F32), high_ref[r].astype(F32), low_ref[r].astype(F32)], axis=0
        )
        for r in range(ROWS)
    ]
    field = jnp.concatenate(planes, axis=0).astype(BF)
    sums = []
    for b in range(3):
        up = jnp.dot(field[: 2 * wide], w_ref[b], preferred_element_type=F32)
        mid = jnp.dot(field, w_ref[3 + b], preferred_element_type=F32)
        down = jnp.dot(field[wide:], w_ref[6 + b], preferred_element_type=F32)
        rows = []
        for r in range(ROWS):
            value = mid[r * wide : (r + 1) * wide]
            if r > 0:
                value = value + up[(r - 1) * wide : r * wide]
            if r < 2:
                value = value + down[r * wide : (r + 1) * wide]
            rows.append(value)
        sums.append(rows)
    for r in range(ROWS):
        preact = pltpu.roll(sums[0][r], 1, 0) + sums[1][r] + pltpu.roll(sums[2][r], wide - 1, 0)
        gate = jax.nn.sigmoid(preact)
        value = gate * (1.0 + preact * (1.0 - gate))
        out_ref[0, r, :WIDTH] = value[:WIDTH]
        out_ref[0, r, WIDTH:] = first_four(value[WIDTH : WIDTH + 8], value[WIDTH + 8 :])


def slope_factors(x, low, high, weights, first):
    weights = pltpu.with_memory_space_constraint(weights, pltpu.VMEM)
    return pl.pallas_call(
        factor_kernel,
        grid=(1,),
        out_shape=jax.ShapeDtypeStruct((1, ROWS, WIDE, CH), F32),
        in_specs=[
            pl.BlockSpec((1, ROWS, WIDTH, CH), lambda n: (first + n, 0, 0, 0)),
            pl.BlockSpec((ROWS, 8, CH), lambda n: (first + n, 0, 0)),
            pl.BlockSpec((ROWS, 8, CH), lambda n: (first + n, 0, 0)),
            VMEM,
        ],
        out_specs=pl.BlockSpec((1, ROWS, WIDE, CH), lambda n: (n, 0, 0, 0)),
        compiler_params=params(),
        cost_estimate=cost(1.2e9, 5e6),
    )(x, low, high, weights)


def back_kernel(first, *refs):
    if first:
        own_ref, low_ref, high_ref, factor_ref, w_ref, sent_ref, grad_ref = refs
    else:
        flag_ref, own_ref, low_ref, high_ref, relay_ref, factor_ref, w_ref, sent_ref, grad_ref = refs
    slopes = []
    for r in range(ROWS):
        own = own_ref[r] if first else own_ref[0, r]
        slope = widen(own, high_ref[r], low_ref[r])
        if not first:
            slope = jnp.where(flag_ref[0] == 1, slope, relay_ref[r].astype(F32))
        slopes.append(slope)
    grads = []
    for r in range(ROWS):
        grad = slopes[r] * factor_ref[0, r]
        grad_ref[r] = grad.astype(BF)
        grads.append(grad)
    field = jnp.concatenate(grads, axis=0).astype(BF)
    above = jnp.concatenate(grads[1:], axis=0).astype(BF)
    below = jnp.concatenate(grads[:2], axis=0).astype(BF)
    turned = (((1,), (1,)), ((), ()))
    sums = []
    for b in range(3):
        up = lax.dot_general(above, w_ref[b], turned, preferred_element_type=F32)
        mid = lax.dot_general(field, w_ref[3 + b], turned, preferred_element_type=F32)
        down = lax.dot_general(below, w_ref[6 + b], turned, preferred_element_type=F32)
        rows = []
        for r in range(ROWS):
            value = mid[r * WIDE : (r + 1) * WIDE]
            if r < 2:
                value = value + up[r * WIDE : (r + 1) * WIDE]
            if r > 0:
                value = value + down[(r - 1) * WIDE : r * WIDE]
            rows.append(value)
        sums.append(rows)
    for r in range(ROWS):
        value = pltpu.roll(sums[0][r], WIDE - 1, 0) + sums[1][r] + pltpu.roll(sums[2][r], 1, 0)
        sent_ref[r] = (slopes[r] + value).astype(BF)


def back_step(own, low, high, factors, weights, t, flag=None, arrived=None):
    first = t == 0
    weights = pltpu.with_memory_space_constraint(weights, pltpu.VMEM)
    edge = block((ROWS, 8, CH), 4 + t, 0, 0)
    operands = [own, low, high]
    if first:
        specs = [block((ROWS, WIDTH, CH), 0, 0, 0), edge, edge]
    else:
        specs = [SMEM, block((1, ROWS, WIDTH, CH), t - 1, 0, 0, 0), edge, edge]
        specs += [block((ROWS, WIDE, CH), 0, 0, 0)]
        operands = [flag, *operands, arrived]
    specs += [block((1, ROWS, WIDE, CH), 0, 0, 0, 0), VMEM]
    return pl.pallas_call(
        lambda *refs: back_kernel(first, *refs),
        grid=(1,),
        out_shape=(
            jax.ShapeDtypeStruct((ROWS, WIDE, CH), BF),
            jax.ShapeDtypeStruct((ROWS, WIDE, CH), BF),
        ),
        in_specs=specs,
        out_specs=(block((ROWS, WIDE, CH), 0, 0, 0), block((ROWS, WIDE, CH), 0, 0, 0)),
        compiler_params=params(),
        cost_estimate=cost(1.1e9, 6e6),
    )(*operands, factors, weights)


def spread_kernel(place_ref, x_ref, source_ref, out0, out1, w_ref, field_ref, done):
    copies = [pltpu.make_async_copy(x_ref.at[t], field_ref.at[t], done.at[t]) for t in range(STEPS)]
    copies.append(pltpu.make_async_copy(source_ref, w_ref, done.at[STEPS]))
    for copy in copies:
        copy.start()
    h, j, k, c = (place_ref[n] for n in range(4))
    lane = lax.broadcasted_iota(jnp.int32, (8, CH), 1)
    chip = jnp.bitwise_xor(lane // HALF, k)
    core = jnp.bitwise_xor(lane // 128 % 2, c)
    far = jnp.bitwise_xor(lane // 64 % 2, h)
    turn = jnp.bitwise_and(lane // 16 + j, 3)
    source = ((far * 4 + turn) * 4 + chip * 2 + core) * 16 + lane % 16
    row = lax.broadcasted_iota(jnp.int32, (CH, CH), 0)
    order = jnp.where(row == source[:1], 1.0, 0.0).astype(BF)
    for copy in copies[:STEPS]:
        copy.wait()
    field = jnp.concatenate([field_ref[t, r] for t in range(STEPS) for r in range(ROWS)], axis=0)
    value = jnp.dot(field, order, preferred_element_type=F32).astype(BF)
    for n, out in enumerate((out0, out1)):
        for t in range(STEPS):
            for r in range(ROWS):
                at = (t * ROWS + r) * WIDTH
                out[t, r] = value[at : at + WIDTH, n * HALF : (n + 1) * HALF]
    copies[STEPS].wait()


def spread(place, x, weights):
    x, weights = (pltpu.with_memory_space_constraint(v, pltpu.HBM) for v in (x, weights))
    shape = jax.ShapeDtypeStruct((STEPS, ROWS, WIDTH, HALF), BF)
    return pl.pallas_call(
        spread_kernel,
        out_shape=(shape, shape, pltpu.VMEM(weights.shape, BF)),
        in_specs=[SMEM, pl.BlockSpec(memory_space=pltpu.HBM), pl.BlockSpec(memory_space=pltpu.HBM)],
        out_specs=(VMEM, VMEM, VMEM),
        scratch_shapes=[
            pltpu.VMEM((STEPS, ROWS, WIDTH, CH), BF),
            pltpu.SemaphoreType.DMA((STEPS + 1,)),
        ],
        compiler_params=params(),
        cost_estimate=cost(4.5e8, 1.2e7),
    )(place, x, weights)


def tap_products(xs, gs):
    left, right = [], []
    for r in range(ROWS):
        left.append(jnp.concatenate([x[r] for x in xs], axis=0))
        taps = [[], [], []]
        for g in gs:
            plane = g[r].astype(F32)
            for b, shift in enumerate((WIDE - 1, 0, 1)):
                moved = pltpu.roll(plane, shift, 0) if shift else plane
                taps[b].append(moved[:WIDTH])
        right.append(
            jnp.concatenate([jnp.concatenate(parts, axis=0).astype(BF) for parts in taps], axis=1)
        )
    pairs = ((left[:2], right[1:]), (left, right), (left[1:], right[:2]))
    return [
        lax.dot_general(
            jnp.concatenate(ls, axis=0),
            jnp.concatenate(rs, axis=0),
            (((0,), (0,)), ((), ())),
            preferred_element_type=F32,
        )
        for ls, rs in pairs
    ]


def early_kernel(x0, x1, both0, both1, third0, third1, out_ref):
    for t in range(STEPS - 1):
        gs = (both0[t], both1[t]) if t < 2 else (third0, third1)
        values = tap_products((x0[t], x1[t]), gs)
        for a, value in enumerate(values):
            out_ref[a] = value if t == 0 else out_ref[a] + value


def early_products(xs, *gs):
    return pl.pallas_call(
        early_kernel,
        out_shape=jax.ShapeDtypeStruct((3, HALF, 3 * CH), F32),
        in_specs=[VMEM] * 6,
        out_specs=VMEM,
        compiler_params=params(),
        cost_estimate=cost(3e9, 8e6),
    )(*xs, *gs)


FIRST = 6


def late_kernel(x0, x1, g0, g1, total_ref, *outs):
    for a, value in enumerate(tap_products((x0[0], x1[0]), (g0, g1))):
        value = value + total_ref[a]
        for b in range(3):
            tap = a * 3 + b
            for core in range(2):
                for far in range(2):
                    for turn in range(4):
                        at = ((core * 2 + far) * 4 + turn) * 16
                        part = value[at : at + 16, b * CH : (b + 1) * CH].astype(BF)
                        if tap >= FIRST:
                            outs[4 + core][turn, far, tap - FIRST] = part
                        else:
                            outs[2 * far + core][turn, tap] = part


def late_products(xs, gs, total):
    shapes = [(4, FIRST, 16, CH)] * 4 + [(4, 2, 9 - FIRST, 16, CH)] * 2
    return pl.pallas_call(
        late_kernel,
        grid=(1,),
        out_shape=tuple(jax.ShapeDtypeStruct(shape, BF) for shape in shapes),
        in_specs=[block((1, ROWS, WIDTH, HALF), STEPS - 1, 0, 0, 0)] * 2
        + [block((ROWS, WIDE, CH), 0, 0, 0)] * 2
        + [block((3, HALF, 3 * CH), 0, 0, 0)],
        out_specs=tuple(block(shape, *(0,) * len(shape)) for shape in shapes),
        compiler_params=params(),
        cost_estimate=cost(1e9, 8e6),
    )(*xs, *gs, total)


def grad_kernel(flag_ref, own_ref, low_ref, high_ref, relay_ref, factor_ref, grad_ref):
    for r in range(ROWS):
        slope = widen(own_ref[0, r], high_ref[r], low_ref[r])
        slope = jnp.where(flag_ref[0] == 1, slope, relay_ref[r].astype(F32))
        grad_ref[r] = (slope * factor_ref[0, r]).astype(BF)


def last_grad(flag, top, low, high, arrived, factors):
    edge = block((ROWS, 8, CH), 3 + STEPS, 0, 0)
    return pl.pallas_call(
        grad_kernel,
        grid=(1,),
        out_shape=jax.ShapeDtypeStruct((ROWS, WIDE, CH), BF),
        in_specs=[
            SMEM,
            block((1, ROWS, WIDTH, CH), STEPS - 2, 0, 0, 0),
            edge,
            edge,
            block((ROWS, WIDE, CH), 0, 0, 0),
            block((1, ROWS, WIDE, CH), 0, 0, 0, 0),
        ],
        out_specs=block((ROWS, WIDE, CH), 0, 0, 0),
        compiler_params=params(),
        cost_estimate=cost(1e6, 1e6),
    )(flag, top, low, high, arrived, factors)


def total_of(*parts):
    value = parts[0].astype(F32)
    for part in parts[1:]:
        value = value + part.astype(F32)
    return value


def after(value, *others):
    return lax.optimization_barrier((value, *others))[0]


def body(stored_inputs, filter_weights, pending_slopes, topmost_slopes):
    x = stored_inputs[:, 0]
    pending = pending_slopes[0]
    top = topmost_slopes
    az = lax.axis_index("az")
    place = jnp.stack([az // 16, (az // 4) % 4, (az // 2) % 2, az % 2]).astype(jnp.int32)
    last = lax.axis_index("segment") == lax.axis_size("segment") - 1
    flag = last.astype(jnp.int32).reshape(1)
    scale = 1.0 / math.sqrt(STEPS * ROWS * WIDTH * lax.axis_size("az"))

    right_edge, left_edge = pack_edges(x, pending, top)
    low = send(right_edge, RIGHT)
    high = send(left_edge, LEFT)
    taps = filter_weights[0].reshape(9, CH, CH)
    mine, other, weights = spread(after(place, left_edge), x, taps)
    xs = (mine, send(other, PAIR))

    emitted, fields = [], []
    slope, arrived = pending, None
    weights = pltpu.with_memory_space_constraint(weights, pltpu.VMEM)
    factors = slope_factors(x, low, high, weights, 0)
    for t in range(STEPS):
        if t == STEPS - 1:
            own = last_grad(flag, top, low, high, arrived, factors)
        else:
            sent, grad = back_step(slope, low, high, factors, weights, t, flag, arrived)
            emitted.append(sent[:, :WIDTH])
            slope, weights = top, taps
            own = grad
            arrived = relay(sent)
            waits = (sent, *xs) if t == 1 else (sent,)
            factors = slope_factors(after(x, *waits), low, high, weights, t + 1)
            own = after(own, factors)
            if t == 1:
                own = jnp.stack([fields[0], own])
                fields = []
        fields.append(own if t == 0 else (own, send(own, PAIR)))

    total = early_products(xs, *fields[0], *fields[1])
    near, near_other, out_going, out_other, turns, turns_other = late_products(xs, fields[-1], total)
    out_going = total_of(out_going, send(out_other, CORE)).astype(BF)
    far = send(out_going, FAR)
    turns_other, near_other = lax.optimization_barrier((turns_other, near_other, out_going))[:2]
    turns_other, near_other = send(turns_other, CORE), send(near_other, CORE)
    turns = [total_of(turns[m], turns_other[m]).astype(BF) for m in range(4)]
    arrived = after(arrived, *turns[1:])
    arriving = (send(turns[2], ACROSS), send(turns[1], UP), send(turns[3], DOWN))
    near = total_of(near, near_other).astype(BF)
    near = total_of(near, far).astype(BF)
    across, ups, downs = send(near[2], ACROSS), send(near[1], UP), send(near[3], DOWN)
    arriving = lax.optimization_barrier((*arriving, near))[:3]
    turned = total_of(turns[0], *arriving).astype(BF)
    far = send(turned[1], FAR)
    sums = [total_of(near[0], ups, across, downs), total_of(turned[0], far)]
    sent, _ = back_step(top, low, high, factors, taps, STEPS - 1, flag, arrived)
    emitted.append(sent[:, :WIDTH])
    weight_grads = (jnp.concatenate(sums, axis=0) * scale).astype(BF).reshape(1, 3, 3, 16, CH)
    return (jnp.stack(emitted)[:, None], weight_grads)


def solution(mesh):
    return jax.shard_map(
        body,
        mesh=mesh,
        in_specs=(
            P(None, "segment", None, "az", None),
            P("segment", None, None, None, None),
            P("segment", None, "az", None),
            P(None, None, "az", None),
        ),
        out_specs=(P(None, "segment", None, "az", None), P("segment", None, None, "az", None)),
        check_vma=False,
    )
```

```python
import math

import jax
import jax.numpy as jnp
from jax import lax
from jax.experimental import pallas as pl
from jax.experimental.pallas import tpu as pltpu
from jax.sharding import PartitionSpec as P

BF = jnp.bfloat16
F32 = jnp.float32
ROWS, WIDTH, CH, STEPS = 3, 64, 512, 4
WIDE = WIDTH + 8
HALF = CH // 2


def az_route(move):
    route = []
    for i in range(32):
        h, z, c = move(i // 16, (i // 2) % 8, i % 2)
        route.append((i, (h % 2) * 16 + (z % 8) * 2 + c % 2))
    return route


RIGHT = [(i, (i + 1) % 32) for i in range(32)]
LEFT = [(i, (i - 1) % 32) for i in range(32)]
CORE = az_route(lambda h, z, c: (h, z, c + 1))
PAIR = az_route(lambda h, z, c: (h, z ^ 1, c))
FAR = az_route(lambda h, z, c: (h + 1, z, c))
UP = az_route(lambda h, z, c: (h, z + 2, c))
ACROSS = az_route(lambda h, z, c: (h, z + 4, c))
DOWN = az_route(lambda h, z, c: (h, z - 2, c))


def send(block, route):
    return lax.ppermute(block, "az", route)


def relay(block):
    count = lax.axis_size("segment")
    return lax.ppermute(block, "segment", [(i, i - 1) for i in range(1, count)])


def params(mib=24):
    return pltpu.CompilerParams(vmem_limit_bytes=mib * 1024 * 1024)


def cost(flops, size):
    return pl.CostEstimate(flops=int(flops), bytes_accessed=int(size), transcendentals=0)


VMEM = pl.BlockSpec(memory_space=pltpu.VMEM)
SMEM = pl.BlockSpec(memory_space=pltpu.SMEM)


def block(shape, *index):
    return pl.BlockSpec(shape, lambda *_: index)


def pack_kernel(x_right, p_right, t_right, x_left, p_left, t_left, right_ref, left_ref):
    for refs, first, out in (((x_right, p_right, t_right), 8, right_ref), ((x_left, p_left, t_left), 0, left_ref)):
        xs, ps, ts = refs
        for r in range(ROWS):
            planes = [xs[t, r] for t in range(STEPS)] + [ps[r]] + [ts[t, r] for t in range(STEPS - 1)]
            for n, plane in enumerate(planes):
                out[n * ROWS + r] = plane.astype(F32)[first : first + 8].astype(BF)


def pack_edges(x, pending, top):
    def specs(edge):
        return [
            block((STEPS, ROWS, 16, CH), 0, 0, edge, 0),
            block((ROWS, 16, CH), 0, edge, 0),
            block((STEPS - 1, ROWS, 16, CH), 0, 0, edge, 0),
        ]

    x, pending, top = (pltpu.with_memory_space_constraint(v, pltpu.HBM) for v in (x, pending, top))
    shape = jax.ShapeDtypeStruct((24, 8, CH), BF)
    return pl.pallas_call(
        pack_kernel,
        grid=(1,),
        out_shape=(shape, shape),
        in_specs=specs(3) + specs(0),
        out_specs=(block((24, 8, CH), 0, 0, 0),) * 2,
        compiler_params=params(),
        cost_estimate=cost(0, 1 << 20),
    )(x, pending, top, x, pending, top)


def first_four(high, low):
    pick = lax.broadcasted_iota(jnp.int32, high.shape, 0) < 4
    return jnp.where(pick, high, low)


def widen(own, high, low):
    return jnp.concatenate([own.astype(F32), first_four(high.astype(F32), low.astype(F32))], axis=0)


def factor_kernel(x_ref, low_ref, high_ref, w_ref, out_ref):
    wide = WIDTH + 16
    planes = [
        jnp.concatenate(
            [x_ref[0, r].astype(F32), high_ref[r].astype(F32), low_ref[r].astype(F32)], axis=0
        )
        for r in range(ROWS)
    ]
    field = jnp.concatenate(planes, axis=0).astype(BF)
    sums = []
    for b in range(3):
        up = jnp.dot(field[: 2 * wide], w_ref[b], preferred_element_type=F32)
        mid = jnp.dot(field, w_ref[3 + b], preferred_element_type=F32)
        down = jnp.dot(field[wide:], w_ref[6 + b], preferred_element_type=F32)
        rows = []
        for r in range(ROWS):
            value = mid[r * wide : (r + 1) * wide]
            if r > 0:
                value = value + up[(r - 1) * wide : r * wide]
            if r < 2:
                value = value + down[r * wide : (r + 1) * wide]
            rows.append(value)
        sums.append(rows)
    for r in range(ROWS):
        preact = pltpu.roll(sums[0][r], 1, 0) + sums[1][r] + pltpu.roll(sums[2][r], wide - 1, 0)
        gate = jax.nn.sigmoid(preact)
        value = gate * (1.0 + preact * (1.0 - gate))
        out_ref[0, r, :WIDTH] = value[:WIDTH]
        out_ref[0, r, WIDTH:] = first_four(value[WIDTH : WIDTH + 8], value[WIDTH + 8 :])


def slope_factors(x, low, high, weights, first):
    weights = pltpu.with_memory_space_constraint(weights, pltpu.VMEM)
    return pl.pallas_call(
        factor_kernel,
        grid=(1,),
        out_shape=jax.ShapeDtypeStruct((1, ROWS, WIDE, CH), F32),
        in_specs=[
            pl.BlockSpec((1, ROWS, WIDTH, CH), lambda n: (first + n, 0, 0, 0)),
            pl.BlockSpec((ROWS, 8, CH), lambda n: (first + n, 0, 0)),
            pl.BlockSpec((ROWS, 8, CH), lambda n: (first + n, 0, 0)),
            VMEM,
        ],
        out_specs=pl.BlockSpec((1, ROWS, WIDE, CH), lambda n: (n, 0, 0, 0)),
        compiler_params=params(),
        cost_estimate=cost(1.2e9, 5e6),
    )(x, low, high, weights)


def back_kernel(first, last, *refs):
    if first:
        own_ref, low_ref, high_ref, factor_ref, w_ref, sent_ref, grad_ref = refs
    else:
        flag_ref, own_ref, low_ref, high_ref, relay_ref, factor_ref, w_ref = refs[:7]
        sent_ref, grad_ref = (refs[10], None) if last else refs[7:]
    slopes = []
    for r in range(ROWS):
        own = own_ref[r] if first else own_ref[0, r]
        slope = widen(own, high_ref[r], low_ref[r])
        if not first:
            slope = jnp.where(flag_ref[0] == 1, slope, relay_ref[r].astype(F32))
        slopes.append(slope)
    grads = []
    for r in range(ROWS):
        grad = slopes[r] * factor_ref[0, r]
        if not last:
            grad_ref[r] = grad.astype(BF)
        grads.append(grad)
    field = jnp.concatenate(grads, axis=0).astype(BF)
    above = jnp.concatenate(grads[1:], axis=0).astype(BF)
    below = jnp.concatenate(grads[:2], axis=0).astype(BF)
    turned = (((1,), (1,)), ((), ()))
    sums = []
    for b in range(3):
        up = lax.dot_general(above, w_ref[b], turned, preferred_element_type=F32)
        mid = lax.dot_general(field, w_ref[3 + b], turned, preferred_element_type=F32)
        down = lax.dot_general(below, w_ref[6 + b], turned, preferred_element_type=F32)
        rows = []
        for r in range(ROWS):
            value = mid[r * WIDE : (r + 1) * WIDE]
            if r < 2:
                value = value + up[r * WIDE : (r + 1) * WIDE]
            if r > 0:
                value = value + down[(r - 1) * WIDE : r * WIDE]
            rows.append(value)
        sums.append(rows)
    for r in range(ROWS):
        value = pltpu.roll(sums[0][r], WIDE - 1, 0) + sums[1][r] + pltpu.roll(sums[2][r], 1, 0)
        if last:
            sent_ref[STEPS - 1, r] = (slopes[r] + value)[:WIDTH].astype(BF)
            for t in range(STEPS - 1):
                sent_ref[t, r] = refs[7 + t][r, :WIDTH]
        else:
            sent_ref[r] = (slopes[r] + value).astype(BF)


def back_step(own, low, high, factors, weights, t, flag=None, arrived=None, earlier=()):
    first, last = t == 0, t == STEPS - 1
    weights = pltpu.with_memory_space_constraint(weights, pltpu.VMEM)
    edge = block((ROWS, 8, CH), 4 + t, 0, 0)
    operands = [own, low, high]
    if first:
        specs = [block((ROWS, WIDTH, CH), 0, 0, 0), edge, edge]
    else:
        specs = [SMEM, block((1, ROWS, WIDTH, CH), t - 1, 0, 0, 0), edge, edge]
        specs += [block((ROWS, WIDE, CH), 0, 0, 0)]
        operands = [flag, *operands, arrived]
    specs += [block((1, ROWS, WIDE, CH), 0, 0, 0, 0), VMEM]
    wide = block((ROWS, WIDE, CH), 0, 0, 0)
    shape = jax.ShapeDtypeStruct((ROWS, WIDE, CH), BF)
    if last:
        specs += [wide] * len(earlier)
        out_shape = jax.ShapeDtypeStruct((STEPS, ROWS, WIDTH, CH), BF)
        out_specs = block((STEPS, ROWS, WIDTH, CH), 0, 0, 0, 0)
    else:
        out_shape, out_specs = (shape, shape), (wide, wide)
    return pl.pallas_call(
        lambda *refs: back_kernel(first, last, *refs),
        grid=(1,),
        out_shape=out_shape,
        in_specs=specs,
        out_specs=out_specs,
        compiler_params=params(),
        cost_estimate=cost(1.1e9, 6e6),
    )(*operands, factors, weights, *earlier)


def spread_kernel(place_ref, x_ref, source_ref, out0, out1, w_ref, field_ref, done):
    copies = [pltpu.make_async_copy(x_ref.at[t], field_ref.at[t], done.at[t]) for t in range(STEPS)]
    for copy in copies:
        copy.start()
    h, j, k, c = (place_ref[n] for n in range(4))
    lane = lax.broadcasted_iota(jnp.int32, (8, CH), 1)
    chip = jnp.bitwise_xor(lane // HALF, k)
    core = jnp.bitwise_xor(lane // 128 % 2, c)
    far = jnp.bitwise_xor(lane // 64 % 2, h)
    turn = jnp.bitwise_and(lane // 16 + j, 3)
    source = ((far * 4 + turn) * 4 + chip * 2 + core) * 16 + lane % 16
    row = lax.broadcasted_iota(jnp.int32, (CH, CH), 0)
    order = jnp.where(row == source[:1], 1.0, 0.0).astype(BF)
    for copy in copies:
        copy.wait()
    load = pltpu.make_async_copy(source_ref, w_ref, done.at[STEPS])
    load.start()
    field = jnp.concatenate([field_ref[t, r] for t in range(STEPS) for r in range(ROWS)], axis=0)
    value = jnp.dot(field, order, preferred_element_type=F32).astype(BF)
    for n, out in enumerate((out0, out1)):
        for t in range(STEPS):
            for r in range(ROWS):
                at = (t * ROWS + r) * WIDTH
                out[t, r] = value[at : at + WIDTH, n * HALF : (n + 1) * HALF]
    load.wait()


def spread(place, x, weights):
    x, weights = (pltpu.with_memory_space_constraint(v, pltpu.HBM) for v in (x, weights))
    shape = jax.ShapeDtypeStruct((STEPS, ROWS, WIDTH, HALF), BF)
    return pl.pallas_call(
        spread_kernel,
        out_shape=(shape, shape, pltpu.VMEM(weights.shape, BF)),
        in_specs=[SMEM, pl.BlockSpec(memory_space=pltpu.HBM), pl.BlockSpec(memory_space=pltpu.HBM)],
        out_specs=(VMEM, VMEM, VMEM),
        scratch_shapes=[
            pltpu.VMEM((STEPS, ROWS, WIDTH, CH), BF),
            pltpu.SemaphoreType.DMA((STEPS + 1,)),
        ],
        compiler_params=params(),
        cost_estimate=cost(4.5e8, 1.2e7),
    )(place, x, weights)


def tap_products(xs, gs):
    left, right = [], []
    for r in range(ROWS):
        left.append(jnp.concatenate([x[r] for x in xs], axis=0))
        taps = [[], [], []]
        for g in gs:
            plane = g[r].astype(F32)
            for b, shift in enumerate((WIDE - 1, 0, 1)):
                moved = pltpu.roll(plane, shift, 0) if shift else plane
                taps[b].append(moved[:WIDTH])
        right.append(
            jnp.concatenate([jnp.concatenate(parts, axis=0).astype(BF) for parts in taps], axis=1)
        )
    pairs = ((left[:2], right[1:]), (left, right), (left[1:], right[:2]))
    return [
        lax.dot_general(
            jnp.concatenate(ls, axis=0),
            jnp.concatenate(rs, axis=0),
            (((0,), (0,)), ((), ())),
            preferred_element_type=F32,
        )
        for ls, rs in pairs
    ]


def early_kernel(x0, x1, both0, both1, third0, third1, out_ref):
    for t in range(STEPS - 1):
        gs = (both0[t], both1[t]) if t < 2 else (third0, third1)
        values = tap_products((x0[t], x1[t]), gs)
        for a, value in enumerate(values):
            out_ref[a] = value if t == 0 else out_ref[a] + value


def early_products(xs, *gs):
    return pl.pallas_call(
        early_kernel,
        out_shape=jax.ShapeDtypeStruct((3, HALF, 3 * CH), F32),
        in_specs=[VMEM] * 6,
        out_specs=VMEM,
        compiler_params=params(),
        cost_estimate=cost(3e9, 8e6),
    )(*xs, *gs)


FIRST = 6


def late_kernel(x0, x1, g0, g1, total_ref, *outs):
    for a, value in enumerate(tap_products((x0[0], x1[0]), (g0, g1))):
        value = value + total_ref[a]
        for b in range(3):
            tap = a * 3 + b
            for core in range(2):
                for far in range(2):
                    for turn in range(4):
                        at = ((core * 2 + far) * 4 + turn) * 16
                        part = value[at : at + 16, b * CH : (b + 1) * CH].astype(BF)
                        if tap >= FIRST:
                            outs[4 + core][turn, far, tap - FIRST] = part
                        else:
                            outs[2 * far + core][turn, tap] = part


def late_products(xs, gs, total):
    shapes = [(4, FIRST, 16, CH)] * 4 + [(4, 2, 9 - FIRST, 16, CH)] * 2
    return pl.pallas_call(
        late_kernel,
        grid=(1,),
        out_shape=tuple(jax.ShapeDtypeStruct(shape, BF) for shape in shapes),
        in_specs=[block((1, ROWS, WIDTH, HALF), STEPS - 1, 0, 0, 0)] * 2
        + [block((ROWS, WIDE, CH), 0, 0, 0)] * 2
        + [block((3, HALF, 3 * CH), 0, 0, 0)],
        out_specs=tuple(block(shape, *(0,) * len(shape)) for shape in shapes),
        compiler_params=params(),
        cost_estimate=cost(1e9, 8e6),
    )(*xs, *gs, total)


def grad_kernel(flag_ref, own_ref, low_ref, high_ref, relay_ref, factor_ref, grad_ref):
    for r in range(ROWS):
        slope = widen(own_ref[0, r], high_ref[r], low_ref[r])
        slope = jnp.where(flag_ref[0] == 1, slope, relay_ref[r].astype(F32))
        grad_ref[r] = (slope * factor_ref[0, r]).astype(BF)


def last_grad(flag, top, low, high, arrived, factors):
    edge = block((ROWS, 8, CH), 3 + STEPS, 0, 0)
    return pl.pallas_call(
        grad_kernel,
        grid=(1,),
        out_shape=jax.ShapeDtypeStruct((ROWS, WIDE, CH), BF),
        in_specs=[
            SMEM,
            block((1, ROWS, WIDTH, CH), STEPS - 2, 0, 0, 0),
            edge,
            edge,
            block((ROWS, WIDE, CH), 0, 0, 0),
            block((1, ROWS, WIDE, CH), 0, 0, 0, 0),
        ],
        out_specs=block((ROWS, WIDE, CH), 0, 0, 0),
        compiler_params=params(),
        cost_estimate=cost(1e6, 1e6),
    )(flag, top, low, high, arrived, factors)


def total_of(*parts):
    value = parts[0].astype(F32)
    for part in parts[1:]:
        value = value + part.astype(F32)
    return value


def after(value, *others):
    return lax.optimization_barrier((value, *others))[0]


def body(stored_inputs, filter_weights, pending_slopes, topmost_slopes):
    x = stored_inputs[:, 0]
    pending = pending_slopes[0]
    top = topmost_slopes
    az = lax.axis_index("az")
    place = jnp.stack([az // 16, (az // 4) % 4, (az // 2) % 2, az % 2]).astype(jnp.int32)
    last = lax.axis_index("segment") == lax.axis_size("segment") - 1
    flag = last.astype(jnp.int32).reshape(1)
    scale = 1.0 / math.sqrt(STEPS * ROWS * WIDTH * lax.axis_size("az"))

    right_edge, left_edge = pack_edges(x, pending, top)
    low = send(right_edge, RIGHT)
    high = send(left_edge, LEFT)
    taps = filter_weights[0].reshape(9, CH, CH)
    mine, other, weights = spread(after(place, left_edge), x, taps)
    xs = (mine, send(other, PAIR))

    emitted, fields = [], []
    slope, arrived = pending, None
    weights = pltpu.with_memory_space_constraint(weights, pltpu.VMEM)
    factors = slope_factors(x, low, high, weights, 0)
    for t in range(STEPS):
        if t == STEPS - 1:
            own = last_grad(flag, top, low, high, arrived, factors)
        else:
            sent, grad = back_step(slope, low, high, factors, weights, t, flag, arrived)
            emitted.append(sent)
            slope, weights = top, taps
            own = grad
            arrived = relay(sent)
            waits = (sent, *xs) if t == 1 else (sent,)
            factors = slope_factors(after(x, *waits), low, high, weights, t + 1)
            own = after(own, factors)
            if t == 1:
                own = jnp.stack([fields[0], own])
                fields = []
        fields.append(own if t == 0 else (own, send(own, PAIR)))

    total = early_products(xs, *fields[0], *fields[1])
    sent = back_step(top, low, high, factors, taps, STEPS - 1, flag, after(arrived, total), emitted)
    total = after(total, sent)
    near, near_other, out_going, out_other, turns, turns_other = late_products(xs, fields[-1], total)
    out_going = total_of(out_going, send(out_other, CORE)).astype(BF)
    far = send(out_going, FAR)
    turns_other, near_other = lax.optimization_barrier((turns_other, near_other, out_going))[:2]
    turns_other, near_other = send(turns_other, CORE), send(near_other, CORE)
    turns = [total_of(turns[m], turns_other[m]).astype(BF) for m in range(4)]
    arriving = (send(turns[2], ACROSS), send(turns[1], UP), send(turns[3], DOWN))
    near = total_of(near, near_other).astype(BF)
    near = total_of(near, far).astype(BF)
    across, ups, downs = send(near[2], ACROSS), send(near[1], UP), send(near[3], DOWN)
    arriving = lax.optimization_barrier((*arriving, near))[:3]
    turned = total_of(turns[0], *arriving).astype(BF)
    far = send(turned[1], FAR)
    sums = [total_of(near[0], ups, across, downs), total_of(turned[0], far)]
    weight_grads = (jnp.concatenate(sums, axis=0) * scale).astype(BF).reshape(1, 3, 3, 16, CH)
    return (sent[:, None], weight_grads)


def solution(mesh):
    return jax.shard_map(
        body,
        mesh=mesh,
        in_specs=(
            P(None, "segment", None, "az", None),
            P("segment", None, None, None, None),
            P("segment", None, "az", None),
            P(None, None, "az", None),
        ),
        out_specs=(P(None, "segment", None, "az", None), P("segment", None, None, "az", None)),
        check_vma=False,
    )
```

```python
import math

import jax
import jax.numpy as jnp
from jax import lax
from jax.experimental import pallas as pl
from jax.experimental.pallas import tpu as pltpu
from jax.sharding import PartitionSpec as P

BF = jnp.bfloat16
F32 = jnp.float32
ROWS, WIDTH, CH, STEPS = 3, 64, 512, 4
WIDE = WIDTH + 8
HALF = CH // 2


def az_route(move):
    route = []
    for i in range(32):
        h, z, c = move(i // 16, (i // 2) % 8, i % 2)
        route.append((i, (h % 2) * 16 + (z % 8) * 2 + c % 2))
    return route


RIGHT = [(i, (i + 1) % 32) for i in range(32)]
LEFT = [(i, (i - 1) % 32) for i in range(32)]
CORE = az_route(lambda h, z, c: (h, z, c + 1))
PAIR = az_route(lambda h, z, c: (h, z ^ 1, c))
FAR = az_route(lambda h, z, c: (h + 1, z, c))
UP = az_route(lambda h, z, c: (h, z + 2, c))
ACROSS = az_route(lambda h, z, c: (h, z + 4, c))
DOWN = az_route(lambda h, z, c: (h, z - 2, c))


def send(block, route):
    return lax.ppermute(block, "az", route)


def relay(block):
    count = lax.axis_size("segment")
    return lax.ppermute(block, "segment", [(i, i - 1) for i in range(1, count)])


def params(mib=24):
    return pltpu.CompilerParams(vmem_limit_bytes=mib * 1024 * 1024)


def cost(flops, size):
    return pl.CostEstimate(flops=int(flops), bytes_accessed=int(size), transcendentals=0)


VMEM = pl.BlockSpec(memory_space=pltpu.VMEM)
SMEM = pl.BlockSpec(memory_space=pltpu.SMEM)


def block(shape, *index):
    return pl.BlockSpec(shape, lambda *_: index)


def pack_kernel(source_ref, p_right, t_right, p_left, t_left, right_ref, left_ref, x_ref, done):
    copies = [pltpu.make_async_copy(source_ref.at[t], x_ref.at[t], done.at[t]) for t in range(STEPS)]
    for copy in copies:
        copy.start()
    sides = ((p_right, t_right, 8, right_ref), (p_left, t_left, 0, left_ref))
    for ps, ts, first, out in sides:
        for r in range(ROWS):
            planes = [ps[r]] + [ts[t, r] for t in range(STEPS - 1)]
            for n, plane in enumerate(planes):
                out[(STEPS + n) * ROWS + r] = plane.astype(F32)[first : first + 8].astype(BF)
    for t, copy in enumerate(copies):
        copy.wait()
        for ps, ts, first, out in sides:
            for r in range(ROWS):
                plane = x_ref[t, r, WIDTH - 16 :] if first else x_ref[t, r, :16]
                out[t * ROWS + r] = plane.astype(F32)[first : first + 8].astype(BF)


def pack_edges(x, pending, top):
    def specs(edge):
        return [
            block((ROWS, 16, CH), 0, edge, 0),
            block((STEPS - 1, ROWS, 16, CH), 0, 0, edge, 0),
        ]

    x, pending, top = (pltpu.with_memory_space_constraint(v, pltpu.HBM) for v in (x, pending, top))
    shape = jax.ShapeDtypeStruct((24, 8, CH), BF)
    return pl.pallas_call(
        pack_kernel,
        grid=(1,),
        out_shape=(shape, shape, pltpu.VMEM(x.shape, BF)),
        in_specs=[pl.BlockSpec(memory_space=pltpu.HBM)] + specs(3) + specs(0),
        out_specs=(block((24, 8, CH), 0, 0, 0),) * 2 + (VMEM,),
        scratch_shapes=[pltpu.SemaphoreType.DMA((STEPS,))],
        compiler_params=params(),
        cost_estimate=cost(0, 2 << 20),
    )(x, pending, top, pending, top)


def first_four(high, low):
    pick = lax.broadcasted_iota(jnp.int32, high.shape, 0) < 4
    return jnp.where(pick, high, low)


def widen(own, high, low):
    return jnp.concatenate([own.astype(F32), first_four(high.astype(F32), low.astype(F32))], axis=0)


def factor_kernel(x_ref, low_ref, high_ref, w_ref, out_ref):
    wide = WIDTH + 16
    planes = [
        jnp.concatenate(
            [x_ref[0, r].astype(F32), high_ref[r].astype(F32), low_ref[r].astype(F32)], axis=0
        )
        for r in range(ROWS)
    ]
    field = jnp.concatenate(planes, axis=0).astype(BF)
    sums = []
    for b in range(3):
        up = jnp.dot(field[: 2 * wide], w_ref[b], preferred_element_type=F32)
        mid = jnp.dot(field, w_ref[3 + b], preferred_element_type=F32)
        down = jnp.dot(field[wide:], w_ref[6 + b], preferred_element_type=F32)
        rows = []
        for r in range(ROWS):
            value = mid[r * wide : (r + 1) * wide]
            if r > 0:
                value = value + up[(r - 1) * wide : r * wide]
            if r < 2:
                value = value + down[r * wide : (r + 1) * wide]
            rows.append(value)
        sums.append(rows)
    for r in range(ROWS):
        preact = pltpu.roll(sums[0][r], 1, 0) + sums[1][r] + pltpu.roll(sums[2][r], wide - 1, 0)
        gate = jax.nn.sigmoid(preact)
        value = gate * (1.0 + preact * (1.0 - gate))
        out_ref[0, r, :WIDTH] = value[:WIDTH]
        out_ref[0, r, WIDTH:] = first_four(value[WIDTH : WIDTH + 8], value[WIDTH + 8 :])


def slope_factors(x, low, high, weights, first):
    weights = pltpu.with_memory_space_constraint(weights, pltpu.VMEM)
    return pl.pallas_call(
        factor_kernel,
        grid=(1,),
        out_shape=jax.ShapeDtypeStruct((1, ROWS, WIDE, CH), F32),
        in_specs=[
            pl.BlockSpec((1, ROWS, WIDTH, CH), lambda n: (first + n, 0, 0, 0)),
            pl.BlockSpec((ROWS, 8, CH), lambda n: (first + n, 0, 0)),
            pl.BlockSpec((ROWS, 8, CH), lambda n: (first + n, 0, 0)),
            VMEM,
        ],
        out_specs=pl.BlockSpec((1, ROWS, WIDE, CH), lambda n: (n, 0, 0, 0)),
        compiler_params=params(),
        cost_estimate=cost(1.2e9, 5e6),
    )(x, low, high, weights)


def back_kernel(first, *refs):
    if first:
        own_ref, low_ref, high_ref, factor_ref, w_ref, sent_ref, grad_ref = refs
    else:
        flag_ref, own_ref, low_ref, high_ref, relay_ref, factor_ref, w_ref, sent_ref, grad_ref = refs
    slopes = []
    for r in range(ROWS):
        own = own_ref[r] if first else own_ref[0, r]
        slope = widen(own, high_ref[r], low_ref[r])
        if not first:
            slope = jnp.where(flag_ref[0] == 1, slope, relay_ref[r].astype(F32))
        slopes.append(slope)
    grads = []
    for r in range(ROWS):
        grad = slopes[r] * factor_ref[0, r]
        grad_ref[r] = grad.astype(BF)
        grads.append(grad)
    field = jnp.concatenate(grads, axis=0).astype(BF)
    above = jnp.concatenate(grads[1:], axis=0).astype(BF)
    below = jnp.concatenate(grads[:2], axis=0).astype(BF)
    turned = (((1,), (1,)), ((), ()))
    sums = []
    for b in range(3):
        up = lax.dot_general(above, w_ref[b], turned, preferred_element_type=F32)
        mid = lax.dot_general(field, w_ref[3 + b], turned, preferred_element_type=F32)
        down = lax.dot_general(below, w_ref[6 + b], turned, preferred_element_type=F32)
        rows = []
        for r in range(ROWS):
            value = mid[r * WIDE : (r + 1) * WIDE]
            if r < 2:
                value = value + up[r * WIDE : (r + 1) * WIDE]
            if r > 0:
                value = value + down[(r - 1) * WIDE : r * WIDE]
            rows.append(value)
        sums.append(rows)
    for r in range(ROWS):
        value = pltpu.roll(sums[0][r], WIDE - 1, 0) + sums[1][r] + pltpu.roll(sums[2][r], 1, 0)
        sent_ref[r] = (slopes[r] + value).astype(BF)


def back_step(own, low, high, factors, weights, t, flag=None, arrived=None):
    first = t == 0
    weights = pltpu.with_memory_space_constraint(weights, pltpu.VMEM)
    edge = block((ROWS, 8, CH), 4 + t, 0, 0)
    operands = [own, low, high]
    if first:
        specs = [block((ROWS, WIDTH, CH), 0, 0, 0), edge, edge]
    else:
        specs = [SMEM, block((1, ROWS, WIDTH, CH), t - 1, 0, 0, 0), edge, edge]
        specs += [block((ROWS, WIDE, CH), 0, 0, 0)]
        operands = [flag, *operands, arrived]
    specs += [block((1, ROWS, WIDE, CH), 0, 0, 0, 0), VMEM]
    return pl.pallas_call(
        lambda *refs: back_kernel(first, *refs),
        grid=(1,),
        out_shape=(
            jax.ShapeDtypeStruct((ROWS, WIDE, CH), BF),
            jax.ShapeDtypeStruct((ROWS, WIDE, CH), BF),
        ),
        in_specs=specs,
        out_specs=(block((ROWS, WIDE, CH), 0, 0, 0), block((ROWS, WIDE, CH), 0, 0, 0)),
        compiler_params=params(),
        cost_estimate=cost(1.1e9, 6e6),
    )(*operands, factors, weights)


def spread_kernel(place_ref, x_ref, source_ref, out0, out1, w_ref, done):
    copy = pltpu.make_async_copy(source_ref, w_ref, done)
    copy.start()
    h, j, k, c = (place_ref[n] for n in range(4))
    lane = lax.broadcasted_iota(jnp.int32, (8, CH), 1)
    chip = jnp.bitwise_xor(lane // HALF, k)
    core = jnp.bitwise_xor(lane // 128 % 2, c)
    far = jnp.bitwise_xor(lane // 64 % 2, h)
    turn = jnp.bitwise_and(lane // 16 + j, 3)
    source = ((far * 4 + turn) * 4 + chip * 2 + core) * 16 + lane % 16
    row = lax.broadcasted_iota(jnp.int32, (CH, CH), 0)
    order = jnp.where(row == source[:1], 1.0, 0.0).astype(BF)
    field = jnp.concatenate([x_ref[t, r] for t in range(STEPS) for r in range(ROWS)], axis=0)
    value = jnp.dot(field, order, preferred_element_type=F32).astype(BF)
    for n, out in enumerate((out0, out1)):
        for t in range(STEPS):
            for r in range(ROWS):
                at = (t * ROWS + r) * WIDTH
                out[t, r] = value[at : at + WIDTH, n * HALF : (n + 1) * HALF]
    copy.wait()


def spread(place, x, weights):
    x = pltpu.with_memory_space_constraint(x, pltpu.VMEM)
    weights = pltpu.with_memory_space_constraint(weights, pltpu.HBM)
    shape = jax.ShapeDtypeStruct((STEPS, ROWS, WIDTH, HALF), BF)
    return pl.pallas_call(
        spread_kernel,
        out_shape=(shape, shape, pltpu.VMEM(weights.shape, BF)),
        in_specs=[SMEM, VMEM, pl.BlockSpec(memory_space=pltpu.HBM)],
        out_specs=(VMEM, VMEM, VMEM),
        scratch_shapes=[pltpu.SemaphoreType.DMA],
        compiler_params=params(),
        cost_estimate=cost(4.5e8, 1.2e7),
    )(place, x, weights)


def tap_products(xs, gs):
    left, right = [], []
    for r in range(ROWS):
        left.append(jnp.concatenate([x[r] for x in xs], axis=0))
        taps = [[], [], []]
        for g in gs:
            plane = g[r].astype(F32)
            for b, shift in enumerate((WIDE - 1, 0, 1)):
                moved = pltpu.roll(plane, shift, 0) if shift else plane
                taps[b].append(moved[:WIDTH])
        right.append(
            jnp.concatenate([jnp.concatenate(parts, axis=0).astype(BF) for parts in taps], axis=1)
        )
    pairs = ((left[:2], right[1:]), (left, right), (left[1:], right[:2]))
    return [
        lax.dot_general(
            jnp.concatenate(ls, axis=0),
            jnp.concatenate(rs, axis=0),
            (((0,), (0,)), ((), ())),
            preferred_element_type=F32,
        )
        for ls, rs in pairs
    ]


def early_kernel(x0, x1, both0, both1, third0, third1, out_ref):
    for t in range(STEPS - 1):
        gs = (both0[t], both1[t]) if t < 2 else (third0, third1)
        values = tap_products((x0[t], x1[t]), gs)
        for a, value in enumerate(values):
            out_ref[a] = value if t == 0 else out_ref[a] + value


def early_products(xs, *gs):
    return pl.pallas_call(
        early_kernel,
        out_shape=jax.ShapeDtypeStruct((3, HALF, 3 * CH), F32),
        in_specs=[VMEM] * 6,
        out_specs=VMEM,
        compiler_params=params(),
        cost_estimate=cost(3e9, 8e6),
    )(*xs, *gs)


FIRST = 6


def late_kernel(x0, x1, g0, g1, total_ref, *outs):
    for a, value in enumerate(tap_products((x0[0], x1[0]), (g0, g1))):
        value = value + total_ref[a]
        for b in range(3):
            tap = a * 3 + b
            for core in range(2):
                for far in range(2):
                    for turn in range(4):
                        at = ((core * 2 + far) * 4 + turn) * 16
                        part = value[at : at + 16, b * CH : (b + 1) * CH].astype(BF)
                        if tap >= FIRST:
                            outs[4 + core][turn, far, tap - FIRST] = part
                        else:
                            outs[2 * far + core][turn, tap] = part


def late_products(xs, gs, total):
    shapes = [(4, FIRST, 16, CH)] * 4 + [(4, 2, 9 - FIRST, 16, CH)] * 2
    return pl.pallas_call(
        late_kernel,
        grid=(1,),
        out_shape=tuple(jax.ShapeDtypeStruct(shape, BF) for shape in shapes),
        in_specs=[block((1, ROWS, WIDTH, HALF), STEPS - 1, 0, 0, 0)] * 2
        + [block((ROWS, WIDE, CH), 0, 0, 0)] * 2
        + [block((3, HALF, 3 * CH), 0, 0, 0)],
        out_specs=tuple(block(shape, *(0,) * len(shape)) for shape in shapes),
        compiler_params=params(),
        cost_estimate=cost(1e9, 8e6),
    )(*xs, *gs, total)


def grad_kernel(flag_ref, own_ref, low_ref, high_ref, relay_ref, factor_ref, grad_ref):
    for r in range(ROWS):
        slope = widen(own_ref[0, r], high_ref[r], low_ref[r])
        slope = jnp.where(flag_ref[0] == 1, slope, relay_ref[r].astype(F32))
        grad_ref[r] = (slope * factor_ref[0, r]).astype(BF)


def last_grad(flag, top, low, high, arrived, factors):
    edge = block((ROWS, 8, CH), 3 + STEPS, 0, 0)
    return pl.pallas_call(
        grad_kernel,
        grid=(1,),
        out_shape=jax.ShapeDtypeStruct((ROWS, WIDE, CH), BF),
        in_specs=[
            SMEM,
            block((1, ROWS, WIDTH, CH), STEPS - 2, 0, 0, 0),
            edge,
            edge,
            block((ROWS, WIDE, CH), 0, 0, 0),
            block((1, ROWS, WIDE, CH), 0, 0, 0, 0),
        ],
        out_specs=block((ROWS, WIDE, CH), 0, 0, 0),
        compiler_params=params(),
        cost_estimate=cost(1e6, 1e6),
    )(flag, top, low, high, arrived, factors)


def total_of(*parts):
    value = parts[0].astype(F32)
    for part in parts[1:]:
        value = value + part.astype(F32)
    return value


def after(value, *others):
    return lax.optimization_barrier((value, *others))[0]


def body(stored_inputs, filter_weights, pending_slopes, topmost_slopes):
    x = stored_inputs[:, 0]
    pending = pending_slopes[0]
    top = topmost_slopes
    az = lax.axis_index("az")
    place = jnp.stack([az // 16, (az // 4) % 4, (az // 2) % 2, az % 2]).astype(jnp.int32)
    last = lax.axis_index("segment") == lax.axis_size("segment") - 1
    flag = last.astype(jnp.int32).reshape(1)
    scale = 1.0 / math.sqrt(STEPS * ROWS * WIDTH * lax.axis_size("az"))

    right_edge, left_edge, near_x = pack_edges(x, pending, top)
    low = send(right_edge, RIGHT)
    high = send(left_edge, LEFT)
    taps = filter_weights[0].reshape(9, CH, CH)
    mine, other, weights = spread(after(place, left_edge), near_x, taps)
    xs = (mine, send(other, PAIR))

    emitted, fields = [], []
    slope, arrived = pending, None
    weights = pltpu.with_memory_space_constraint(weights, pltpu.VMEM)
    factors = slope_factors(x, low, high, weights, 0)
    for t in range(STEPS):
        if t == STEPS - 1:
            own = last_grad(flag, top, low, high, arrived, factors)
        else:
            sent, grad = back_step(slope, low, high, factors, weights, t, flag, arrived)
            emitted.append(sent[:, :WIDTH])
            slope, weights = top, taps
            own = grad
            arrived = relay(sent)
            waits = (sent, *xs) if t == 1 else (sent,)
            factors = slope_factors(after(x, *waits), low, high, weights, t + 1)
            own = after(own, factors)
            if t == 1:
                own = jnp.stack([fields[0], own])
                fields = []
        fields.append(own if t == 0 else (own, send(own, PAIR)))

    total = early_products(xs, *fields[0], *fields[1])
    near, near_other, out_going, out_other, turns, turns_other = late_products(xs, fields[-1], total)
    out_going = total_of(out_going, send(out_other, CORE)).astype(BF)
    far = send(out_going, FAR)
    turns_other, near_other = lax.optimization_barrier((turns_other, near_other, out_going))[:2]
    turns_other, near_other = send(turns_other, CORE), send(near_other, CORE)
    turns = [total_of(turns[m], turns_other[m]).astype(BF) for m in range(4)]
    arrived = after(arrived, *turns[1:])
    arriving = (send(turns[2], ACROSS), send(turns[1], UP), send(turns[3], DOWN))
    near = total_of(near, near_other).astype(BF)
    near = total_of(near, far).astype(BF)
    across, ups, downs = send(near[2], ACROSS), send(near[1], UP), send(near[3], DOWN)
    arriving = lax.optimization_barrier((*arriving, near))[:3]
    turned = total_of(turns[0], *arriving).astype(BF)
    far = send(turned[1], FAR)
    sums = [total_of(near[0], ups, across, downs), total_of(turned[0], far)]
    sent, _ = back_step(top, low, high, factors, taps, STEPS - 1, flag, arrived)
    emitted.append(sent[:, :WIDTH])
    weight_grads = (jnp.concatenate(sums, axis=0) * scale).astype(BF).reshape(1, 3, 3, 16, CH)
    return (jnp.stack(emitted)[:, None], weight_grads)


def solution(mesh):
    return jax.shard_map(
        body,
        mesh=mesh,
        in_specs=(
            P(None, "segment", None, "az", None),
            P("segment", None, None, None, None),
            P("segment", None, "az", None),
            P(None, None, "az", None),
        ),
        out_specs=(P(None, "segment", None, "az", None), P("segment", None, None, "az", None)),
        check_vma=False,
    )
```

```python
import math

import jax
import jax.numpy as jnp
from jax import lax
from jax.experimental import pallas as pl
from jax.experimental.pallas import tpu as pltpu
from jax.sharding import PartitionSpec as P

BF = jnp.bfloat16
F32 = jnp.float32
ROWS, WIDTH, CH, STEPS = 3, 64, 512, 4
WIDE = WIDTH + 8
HALF = CH // 2


def az_route(move):
    route = []
    for i in range(32):
        h, z, c = move(i // 16, (i // 2) % 8, i % 2)
        route.append((i, (h % 2) * 16 + (z % 8) * 2 + c % 2))
    return route


RIGHT = [(i, (i + 1) % 32) for i in range(32)]
LEFT = [(i, (i - 1) % 32) for i in range(32)]
CORE = az_route(lambda h, z, c: (h, z, c + 1))
PAIR = az_route(lambda h, z, c: (h, z ^ 1, c))
FAR = az_route(lambda h, z, c: (h + 1, z, c))
UP = az_route(lambda h, z, c: (h, z + 2, c))
ACROSS = az_route(lambda h, z, c: (h, z + 4, c))
DOWN = az_route(lambda h, z, c: (h, z - 2, c))


def send(block, route):
    return lax.ppermute(block, "az", route)


def relay(block):
    count = lax.axis_size("segment")
    return lax.ppermute(block, "segment", [(i, (i - 1) % count) for i in range(count)])


def params(mib=24):
    return pltpu.CompilerParams(vmem_limit_bytes=mib * 1024 * 1024)


def cost(flops, size):
    return pl.CostEstimate(flops=int(flops), bytes_accessed=int(size), transcendentals=0)


VMEM = pl.BlockSpec(memory_space=pltpu.VMEM)
SMEM = pl.BlockSpec(memory_space=pltpu.SMEM)


def block(shape, *index):
    return pl.BlockSpec(shape, lambda *_: index)


def pack_kernel(x_right, p_right, t_right, x_left, p_left, t_left, right_ref, left_ref):
    for refs, first, out in (((x_right, p_right, t_right), 8, right_ref), ((x_left, p_left, t_left), 0, left_ref)):
        xs, ps, ts = refs
        for r in range(ROWS):
            planes = [xs[t, r] for t in range(STEPS)] + [ps[r]] + [ts[t, r] for t in range(STEPS - 1)]
            for n, plane in enumerate(planes):
                out[n * ROWS + r] = plane.astype(F32)[first : first + 8].astype(BF)


def pack_edges(x, pending, top):
    def specs(edge):
        return [
            block((STEPS, ROWS, 16, CH), 0, 0, edge, 0),
            block((ROWS, 16, CH), 0, edge, 0),
            block((STEPS - 1, ROWS, 16, CH), 0, 0, edge, 0),
        ]

    x, pending, top = (pltpu.with_memory_space_constraint(v, pltpu.HBM) for v in (x, pending, top))
    shape = jax.ShapeDtypeStruct((24, 8, CH), BF)
    return pl.pallas_call(
        pack_kernel,
        grid=(1,),
        out_shape=(shape, shape),
        in_specs=specs(3) + specs(0),
        out_specs=(block((24, 8, CH), 0, 0, 0),) * 2,
        compiler_params=params(),
        cost_estimate=cost(0, 1 << 20),
    )(x, pending, top, x, pending, top)


def first_four(high, low):
    pick = lax.broadcasted_iota(jnp.int32, high.shape, 0) < 4
    return jnp.where(pick, high, low)


def widen(own, high, low):
    return jnp.concatenate([own.astype(F32), first_four(high.astype(F32), low.astype(F32))], axis=0)


def factor_kernel(x_ref, low_ref, high_ref, w_ref, out_ref):
    wide = WIDTH + 16
    planes = [
        jnp.concatenate(
            [x_ref[0, r].astype(F32), high_ref[r].astype(F32), low_ref[r].astype(F32)], axis=0
        )
        for r in range(ROWS)
    ]
    field = jnp.concatenate(planes, axis=0).astype(BF)
    sums = []
    for b in range(3):
        up = jnp.dot(field[: 2 * wide], w_ref[b], preferred_element_type=F32)
        mid = jnp.dot(field, w_ref[3 + b], preferred_element_type=F32)
        down = jnp.dot(field[wide:], w_ref[6 + b], preferred_element_type=F32)
        rows = []
        for r in range(ROWS):
            value = mid[r * wide : (r + 1) * wide]
            if r > 0:
                value = value + up[(r - 1) * wide : r * wide]
            if r < 2:
                value = value + down[r * wide : (r + 1) * wide]
            rows.append(value)
        sums.append(rows)
    for r in range(ROWS):
        preact = pltpu.roll(sums[0][r], 1, 0) + sums[1][r] + pltpu.roll(sums[2][r], wide - 1, 0)
        gate = jax.nn.sigmoid(preact)
        value = gate * (1.0 + preact * (1.0 - gate))
        out_ref[0, r, :WIDTH] = value[:WIDTH]
        out_ref[0, r, WIDTH:] = first_four(value[WIDTH : WIDTH + 8], value[WIDTH + 8 :])


def slope_factors(x, low, high, weights, first):
    weights = pltpu.with_memory_space_constraint(weights, pltpu.VMEM)
    return pl.pallas_call(
        factor_kernel,
        grid=(1,),
        out_shape=jax.ShapeDtypeStruct((1, ROWS, WIDE, CH), F32),
        in_specs=[
            pl.BlockSpec((1, ROWS, WIDTH, CH), lambda n: (first + n, 0, 0, 0)),
            pl.BlockSpec((ROWS, 8, CH), lambda n: (first + n, 0, 0)),
            pl.BlockSpec((ROWS, 8, CH), lambda n: (first + n, 0, 0)),
            VMEM,
        ],
        out_specs=pl.BlockSpec((1, ROWS, WIDE, CH), lambda n: (n, 0, 0, 0)),
        compiler_params=params(),
        cost_estimate=cost(1.2e9, 5e6),
    )(x, low, high, weights)


def back_kernel(first, *refs):
    if first:
        own_ref, low_ref, high_ref, factor_ref, w_ref, sent_ref, grad_ref = refs
    else:
        flag_ref, own_ref, low_ref, high_ref, relay_ref, factor_ref, w_ref, sent_ref, grad_ref = refs
    slopes = []
    for r in range(ROWS):
        own = own_ref[r] if first else own_ref[0, r]
        slope = widen(own, high_ref[r], low_ref[r])
        if not first:
            slope = jnp.where(flag_ref[0] == 1, slope, relay_ref[r].astype(F32))
        slopes.append(slope)
    grads = []
    for r in range(ROWS):
        grad = slopes[r] * factor_ref[0, r]
        grad_ref[r] = grad.astype(BF)
        grads.append(grad)
    field = jnp.concatenate(grads, axis=0).astype(BF)
    above = jnp.concatenate(grads[1:], axis=0).astype(BF)
    below = jnp.concatenate(grads[:2], axis=0).astype(BF)
    turned = (((1,), (1,)), ((), ()))
    sums = []
    for b in range(3):
        up = lax.dot_general(above, w_ref[b], turned, preferred_element_type=F32)
        mid = lax.dot_general(field, w_ref[3 + b], turned, preferred_element_type=F32)
        down = lax.dot_general(below, w_ref[6 + b], turned, preferred_element_type=F32)
        rows = []
        for r in range(ROWS):
            value = mid[r * WIDE : (r + 1) * WIDE]
            if r < 2:
                value = value + up[r * WIDE : (r + 1) * WIDE]
            if r > 0:
                value = value + down[(r - 1) * WIDE : r * WIDE]
            rows.append(value)
        sums.append(rows)
    for r in range(ROWS):
        value = pltpu.roll(sums[0][r], WIDE - 1, 0) + sums[1][r] + pltpu.roll(sums[2][r], 1, 0)
        sent_ref[r] = (slopes[r] + value).astype(BF)


def back_step(own, low, high, factors, weights, t, flag=None, arrived=None):
    first = t == 0
    weights = pltpu.with_memory_space_constraint(weights, pltpu.VMEM)
    edge = block((ROWS, 8, CH), 4 + t, 0, 0)
    operands = [own, low, high]
    if first:
        specs = [block((ROWS, WIDTH, CH), 0, 0, 0), edge, edge]
    else:
        specs = [SMEM, block((1, ROWS, WIDTH, CH), t - 1, 0, 0, 0), edge, edge]
        specs += [block((ROWS, WIDE, CH), 0, 0, 0)]
        operands = [flag, *operands, arrived]
    specs += [block((1, ROWS, WIDE, CH), 0, 0, 0, 0), VMEM]
    return pl.pallas_call(
        lambda *refs: back_kernel(first, *refs),
        grid=(1,),
        out_shape=(
            jax.ShapeDtypeStruct((ROWS, WIDE, CH), BF),
            jax.ShapeDtypeStruct((ROWS, WIDE, CH), BF),
        ),
        in_specs=specs,
        out_specs=(block((ROWS, WIDE, CH), 0, 0, 0), block((ROWS, WIDE, CH), 0, 0, 0)),
        compiler_params=params(),
        cost_estimate=cost(1.1e9, 6e6),
    )(*operands, factors, weights)


def spread_kernel(place_ref, x_ref, source_ref, out0, out1, w_ref, field_ref, done):
    copies = [pltpu.make_async_copy(x_ref.at[t], field_ref.at[t], done.at[t]) for t in range(STEPS)]
    copies.append(pltpu.make_async_copy(source_ref, w_ref, done.at[STEPS]))
    for copy in copies:
        copy.start()
    h, j, k, c = (place_ref[n] for n in range(4))
    lane = lax.broadcasted_iota(jnp.int32, (8, CH), 1)
    chip = jnp.bitwise_xor(lane // HALF, k)
    core = jnp.bitwise_xor(lane // 128 % 2, c)
    far = jnp.bitwise_xor(lane // 64 % 2, h)
    turn = jnp.bitwise_and(lane // 16 + j, 3)
    source = ((far * 4 + turn) * 4 + chip * 2 + core) * 16 + lane % 16
    row = lax.broadcasted_iota(jnp.int32, (CH, CH), 0)
    order = jnp.where(row == source[:1], 1.0, 0.0).astype(BF)
    for copy in copies[:STEPS]:
        copy.wait()
    field = jnp.concatenate([field_ref[t, r] for t in range(STEPS) for r in range(ROWS)], axis=0)
    value = jnp.dot(field, order, preferred_element_type=F32).astype(BF)
    for n, out in enumerate((out0, out1)):
        for t in range(STEPS):
            for r in range(ROWS):
                at = (t * ROWS + r) * WIDTH
                out[t, r] = value[at : at + WIDTH, n * HALF : (n + 1) * HALF]
    copies[STEPS].wait()


def spread(place, x, weights):
    x, weights = (pltpu.with_memory_space_constraint(v, pltpu.HBM) for v in (x, weights))
    shape = jax.ShapeDtypeStruct((STEPS, ROWS, WIDTH, HALF), BF)
    return pl.pallas_call(
        spread_kernel,
        out_shape=(shape, shape, pltpu.VMEM(weights.shape, BF)),
        in_specs=[SMEM, pl.BlockSpec(memory_space=pltpu.HBM), pl.BlockSpec(memory_space=pltpu.HBM)],
        out_specs=(VMEM, VMEM, VMEM),
        scratch_shapes=[
            pltpu.VMEM((STEPS, ROWS, WIDTH, CH), BF),
            pltpu.SemaphoreType.DMA((STEPS + 1,)),
        ],
        compiler_params=params(),
        cost_estimate=cost(4.5e8, 1.2e7),
    )(place, x, weights)


def tap_products(xs, gs):
    left, right = [], []
    for r in range(ROWS):
        left.append(jnp.concatenate([x[r] for x in xs], axis=0))
        taps = [[], [], []]
        for g in gs:
            plane = g[r].astype(F32)
            for b, shift in enumerate((WIDE - 1, 0, 1)):
                moved = pltpu.roll(plane, shift, 0) if shift else plane
                taps[b].append(moved[:WIDTH])
        right.append(
            jnp.concatenate([jnp.concatenate(parts, axis=0).astype(BF) for parts in taps], axis=1)
        )
    pairs = ((left[:2], right[1:]), (left, right), (left[1:], right[:2]))
    return [
        lax.dot_general(
            jnp.concatenate(ls, axis=0),
            jnp.concatenate(rs, axis=0),
            (((0,), (0,)), ((), ())),
            preferred_element_type=F32,
        )
        for ls, rs in pairs
    ]


def early_kernel(x0, x1, both0, both1, third0, third1, out_ref):
    for t in range(STEPS - 1):
        gs = (both0[t], both1[t]) if t < 2 else (third0, third1)
        values = tap_products((x0[t], x1[t]), gs)
        for a, value in enumerate(values):
            out_ref[a] = value if t == 0 else out_ref[a] + value


def early_products(xs, *gs):
    return pl.pallas_call(
        early_kernel,
        out_shape=jax.ShapeDtypeStruct((3, HALF, 3 * CH), F32),
        in_specs=[VMEM] * 6,
        out_specs=VMEM,
        compiler_params=params(),
        cost_estimate=cost(3e9, 8e6),
    )(*xs, *gs)


FIRST = 6


def late_kernel(x0, x1, g0, g1, total_ref, *outs):
    for a, value in enumerate(tap_products((x0[0], x1[0]), (g0, g1))):
        value = value + total_ref[a]
        for b in range(3):
            tap = a * 3 + b
            for core in range(2):
                for far in range(2):
                    for turn in range(4):
                        at = ((core * 2 + far) * 4 + turn) * 16
                        part = value[at : at + 16, b * CH : (b + 1) * CH].astype(BF)
                        if tap >= FIRST:
                            outs[4 + core][turn, far, tap - FIRST] = part
                        else:
                            outs[2 * far + core][turn, tap] = part


def late_products(xs, gs, total):
    shapes = [(4, FIRST, 16, CH)] * 4 + [(4, 2, 9 - FIRST, 16, CH)] * 2
    return pl.pallas_call(
        late_kernel,
        grid=(1,),
        out_shape=tuple(jax.ShapeDtypeStruct(shape, BF) for shape in shapes),
        in_specs=[block((1, ROWS, WIDTH, HALF), STEPS - 1, 0, 0, 0)] * 2
        + [block((ROWS, WIDE, CH), 0, 0, 0)] * 2
        + [block((3, HALF, 3 * CH), 0, 0, 0)],
        out_specs=tuple(block(shape, *(0,) * len(shape)) for shape in shapes),
        compiler_params=params(),
        cost_estimate=cost(1e9, 8e6),
    )(*xs, *gs, total)


def grad_kernel(flag_ref, own_ref, low_ref, high_ref, relay_ref, factor_ref, grad_ref):
    for r in range(ROWS):
        slope = widen(own_ref[0, r], high_ref[r], low_ref[r])
        slope = jnp.where(flag_ref[0] == 1, slope, relay_ref[r].astype(F32))
        grad_ref[r] = (slope * factor_ref[0, r]).astype(BF)


def last_grad(flag, top, low, high, arrived, factors):
    edge = block((ROWS, 8, CH), 3 + STEPS, 0, 0)
    return pl.pallas_call(
        grad_kernel,
        grid=(1,),
        out_shape=jax.ShapeDtypeStruct((ROWS, WIDE, CH), BF),
        in_specs=[
            SMEM,
            block((1, ROWS, WIDTH, CH), STEPS - 2, 0, 0, 0),
            edge,
            edge,
            block((ROWS, WIDE, CH), 0, 0, 0),
            block((1, ROWS, WIDE, CH), 0, 0, 0, 0),
        ],
        out_specs=block((ROWS, WIDE, CH), 0, 0, 0),
        compiler_params=params(),
        cost_estimate=cost(1e6, 1e6),
    )(flag, top, low, high, arrived, factors)


def total_of(*parts):
    value = parts[0].astype(F32)
    for part in parts[1:]:
        value = value + part.astype(F32)
    return value


def after(value, *others):
    return lax.optimization_barrier((value, *others))[0]


def body(stored_inputs, filter_weights, pending_slopes, topmost_slopes):
    x = stored_inputs[:, 0]
    pending = pending_slopes[0]
    top = topmost_slopes
    az = lax.axis_index("az")
    place = jnp.stack([az // 16, (az // 4) % 4, (az // 2) % 2, az % 2]).astype(jnp.int32)
    last = lax.axis_index("segment") == lax.axis_size("segment") - 1
    flag = last.astype(jnp.int32).reshape(1)
    scale = 1.0 / math.sqrt(STEPS * ROWS * WIDTH * lax.axis_size("az"))

    right_edge, left_edge = pack_edges(x, pending, top)
    low = send(right_edge, RIGHT)
    high = send(left_edge, LEFT)
    taps = filter_weights[0].reshape(9, CH, CH)
    mine, other, weights = spread(after(place, left_edge), x, taps)
    xs = (mine, send(other, PAIR))

    emitted, fields = [], []
    slope, arrived = pending, None
    weights = pltpu.with_memory_space_constraint(weights, pltpu.VMEM)
    factors = slope_factors(x, low, high, weights, 0)
    for t in range(STEPS):
        if t == STEPS - 1:
            own = last_grad(flag, top, low, high, arrived, factors)
        else:
            sent, grad = back_step(slope, low, high, factors, weights, t, flag, arrived)
            emitted.append(sent[:, :WIDTH])
            slope, weights = top, taps
            own = grad
            arrived = relay(sent)
            waits = (sent, *xs) if t == 1 else (sent,)
            factors = slope_factors(after(x, *waits), low, high, weights, t + 1)
            own = after(own, factors)
            if t == 1:
                own = jnp.stack([fields[0], own])
                fields = []
        fields.append(own if t == 0 else (own, send(own, PAIR)))

    total = early_products(xs, *fields[0], *fields[1])
    near, near_other, out_going, out_other, turns, turns_other = late_products(xs, fields[-1], total)
    out_going = total_of(out_going, send(out_other, CORE)).astype(BF)
    far = send(out_going, FAR)
    turns_other, near_other = lax.optimization_barrier((turns_other, near_other, out_going))[:2]
    turns_other, near_other = send(turns_other, CORE), send(near_other, CORE)
    turns = [total_of(turns[m], turns_other[m]).astype(BF) for m in range(4)]
    arrived = after(arrived, *turns[1:])
    arriving = (send(turns[2], ACROSS), send(turns[1], UP), send(turns[3], DOWN))
    near = total_of(near, near_other).astype(BF)
    near = total_of(near, far).astype(BF)
    across, ups, downs = send(near[2], ACROSS), send(near[1], UP), send(near[3], DOWN)
    arriving = lax.optimization_barrier((*arriving, near))[:3]
    turned = total_of(turns[0], *arriving).astype(BF)
    far = send(turned[1], FAR)
    sums = [total_of(near[0], ups, across, downs), total_of(turned[0], far)]
    sent, _ = back_step(top, low, high, factors, taps, STEPS - 1, flag, arrived)
    emitted.append(sent[:, :WIDTH])
    weight_grads = (jnp.concatenate(sums, axis=0) * scale).astype(BF).reshape(1, 3, 3, 16, CH)
    return (jnp.stack(emitted)[:, None], weight_grads)


def solution(mesh):
    return jax.shard_map(
        body,
        mesh=mesh,
        in_specs=(
            P(None, "segment", None, "az", None),
            P("segment", None, None, None, None),
            P("segment", None, "az", None),
            P(None, None, "az", None),
        ),
        out_specs=(P(None, "segment", None, "az", None), P("segment", None, None, "az", None)),
        check_vma=False,
    )
```

```python
import math

import jax
import jax.numpy as jnp
from jax import lax
from jax.experimental import pallas as pl
from jax.experimental.pallas import tpu as pltpu
from jax.sharding import PartitionSpec as P

BF = jnp.bfloat16
F32 = jnp.float32
ROWS, WIDTH, CH, STEPS = 3, 64, 512, 4
WIDE = WIDTH + 8
HALF = CH // 2


def az_route(move):
    route = []
    for i in range(32):
        h, z, c = move(i // 16, (i // 2) % 8, i % 2)
        route.append((i, (h % 2) * 16 + (z % 8) * 2 + c % 2))
    return route


RIGHT = [(i, (i + 1) % 32) for i in range(32)]
LEFT = [(i, (i - 1) % 32) for i in range(32)]
CORE = az_route(lambda h, z, c: (h, z, c + 1))
PAIR = az_route(lambda h, z, c: (h, z ^ 1, c))
FAR = az_route(lambda h, z, c: (h + 1, z, c))
UP = az_route(lambda h, z, c: (h, z + 2, c))
ACROSS = az_route(lambda h, z, c: (h, z + 4, c))
DOWN = az_route(lambda h, z, c: (h, z - 2, c))


def send(block, route):
    return lax.ppermute(block, "az", route)


def relay(block):
    count = lax.axis_size("segment")
    return lax.ppermute(block, "segment", [(i, (i - 1) % count) for i in range(count)])


def params(mib=24):
    return pltpu.CompilerParams(vmem_limit_bytes=mib * 1024 * 1024)


def cost(flops, size):
    return pl.CostEstimate(flops=int(flops), bytes_accessed=int(size), transcendentals=0)


VMEM = pl.BlockSpec(memory_space=pltpu.VMEM)
SMEM = pl.BlockSpec(memory_space=pltpu.SMEM)


def block(shape, *index):
    return pl.BlockSpec(shape, lambda *_: index)


def pack_kernel(x_right, p_right, t_right, x_left, p_left, t_left, right_ref, left_ref):
    for refs, first, out in (((x_right, p_right, t_right), 8, right_ref), ((x_left, p_left, t_left), 0, left_ref)):
        xs, ps, ts = refs
        for r in range(ROWS):
            planes = [xs[t, r] for t in range(STEPS)] + [ps[r]] + [ts[t, r] for t in range(STEPS - 1)]
            for n, plane in enumerate(planes):
                out[n * ROWS + r] = plane.astype(F32)[first : first + 8].astype(BF)


def pack_edges(x, pending, top):
    def specs(edge):
        return [
            block((STEPS, ROWS, 16, CH), 0, 0, edge, 0),
            block((ROWS, 16, CH), 0, edge, 0),
            block((STEPS - 1, ROWS, 16, CH), 0, 0, edge, 0),
        ]

    x, pending, top = (pltpu.with_memory_space_constraint(v, pltpu.HBM) for v in (x, pending, top))
    shape = jax.ShapeDtypeStruct((24, 8, CH), BF)
    return pl.pallas_call(
        pack_kernel,
        grid=(1,),
        out_shape=(shape, shape),
        in_specs=specs(3) + specs(0),
        out_specs=(block((24, 8, CH), 0, 0, 0),) * 2,
        compiler_params=params(),
        cost_estimate=cost(0, 1 << 20),
    )(x, pending, top, x, pending, top)


def first_four(high, low):
    pick = lax.broadcasted_iota(jnp.int32, high.shape, 0) < 4
    return jnp.where(pick, high, low)


def widen(own, high, low):
    return jnp.concatenate([own.astype(F32), first_four(high.astype(F32), low.astype(F32))], axis=0)


def factor_kernel(x_ref, low_ref, high_ref, w_ref, out_ref):
    wide = WIDTH + 16
    planes = [
        jnp.concatenate(
            [x_ref[0, r].astype(F32), high_ref[r].astype(F32), low_ref[r].astype(F32)], axis=0
        )
        for r in range(ROWS)
    ]
    field = jnp.concatenate(planes, axis=0).astype(BF)
    sums = []
    for b in range(3):
        up = jnp.dot(field[: 2 * wide], w_ref[b], preferred_element_type=F32)
        mid = jnp.dot(field, w_ref[3 + b], preferred_element_type=F32)
        down = jnp.dot(field[wide:], w_ref[6 + b], preferred_element_type=F32)
        rows = []
        for r in range(ROWS):
            value = mid[r * wide : (r + 1) * wide]
            if r > 0:
                value = value + up[(r - 1) * wide : r * wide]
            if r < 2:
                value = value + down[r * wide : (r + 1) * wide]
            rows.append(value)
        sums.append(rows)
    for r in range(ROWS):
        preact = pltpu.roll(sums[0][r], 1, 0) + sums[1][r] + pltpu.roll(sums[2][r], wide - 1, 0)
        gate = jax.nn.sigmoid(preact)
        value = gate * (1.0 + preact * (1.0 - gate))
        out_ref[0, r, :WIDTH] = value[:WIDTH]
        out_ref[0, r, WIDTH:] = first_four(value[WIDTH : WIDTH + 8], value[WIDTH + 8 :])


def slope_factors(x, low, high, weights, first):
    weights = pltpu.with_memory_space_constraint(weights, pltpu.VMEM)
    return pl.pallas_call(
        factor_kernel,
        grid=(1,),
        out_shape=jax.ShapeDtypeStruct((1, ROWS, WIDE, CH), F32),
        in_specs=[
            pl.BlockSpec((1, ROWS, WIDTH, CH), lambda n: (first + n, 0, 0, 0)),
            pl.BlockSpec((ROWS, 8, CH), lambda n: (first + n, 0, 0)),
            pl.BlockSpec((ROWS, 8, CH), lambda n: (first + n, 0, 0)),
            VMEM,
        ],
        out_specs=pl.BlockSpec((1, ROWS, WIDE, CH), lambda n: (n, 0, 0, 0)),
        compiler_params=params(),
        cost_estimate=cost(1.2e9, 5e6),
    )(x, low, high, weights)


def back_kernel(first, *refs):
    if first:
        own_ref, low_ref, high_ref, factor_ref, w_ref, sent_ref, grad_ref = refs
    else:
        flag_ref, own_ref, low_ref, high_ref, relay_ref, factor_ref, w_ref, sent_ref, grad_ref = refs
    slopes = []
    for r in range(ROWS):
        own = own_ref[r] if first else own_ref[0, r]
        slope = widen(own, high_ref[r], low_ref[r])
        if not first:
            slope = jnp.where(flag_ref[0] == 1, slope, relay_ref[r].astype(F32))
        slopes.append(slope)
    grads = []
    for r in range(ROWS):
        grad = slopes[r] * factor_ref[0, r]
        grad_ref[r] = grad.astype(BF)
        grads.append(grad)
    field = jnp.concatenate(grads, axis=0).astype(BF)
    above = jnp.concatenate(grads[1:], axis=0).astype(BF)
    below = jnp.concatenate(grads[:2], axis=0).astype(BF)
    turned = (((1,), (1,)), ((), ()))
    sums = []
    for b in range(3):
        up = lax.dot_general(above, w_ref[b], turned, preferred_element_type=F32)
        mid = lax.dot_general(field, w_ref[3 + b], turned, preferred_element_type=F32)
        down = lax.dot_general(below, w_ref[6 + b], turned, preferred_element_type=F32)
        rows = []
        for r in range(ROWS):
            value = mid[r * WIDE : (r + 1) * WIDE]
            if r < 2:
                value = value + up[r * WIDE : (r + 1) * WIDE]
            if r > 0:
                value = value + down[(r - 1) * WIDE : r * WIDE]
            rows.append(value)
        sums.append(rows)
    for r in range(ROWS):
        value = pltpu.roll(sums[0][r], WIDE - 1, 0) + sums[1][r] + pltpu.roll(sums[2][r], 1, 0)
        sent_ref[r] = (slopes[r] + value).astype(BF)


def back_step(own, low, high, factors, weights, t, flag=None, arrived=None):
    first = t == 0
    weights = pltpu.with_memory_space_constraint(weights, pltpu.VMEM)
    edge = block((ROWS, 8, CH), 4 + t, 0, 0)
    operands = [own, low, high]
    if first:
        specs = [block((ROWS, WIDTH, CH), 0, 0, 0), edge, edge]
    else:
        specs = [SMEM, block((1, ROWS, WIDTH, CH), t - 1, 0, 0, 0), edge, edge]
        specs += [block((ROWS, WIDE, CH), 0, 0, 0)]
        operands = [flag, *operands, arrived]
    specs += [block((1, ROWS, WIDE, CH), 0, 0, 0, 0), VMEM]
    return pl.pallas_call(
        lambda *refs: back_kernel(first, *refs),
        grid=(1,),
        out_shape=(
            jax.ShapeDtypeStruct((ROWS, WIDE, CH), BF),
            jax.ShapeDtypeStruct((ROWS, WIDE, CH), BF),
        ),
        in_specs=specs,
        out_specs=(block((ROWS, WIDE, CH), 0, 0, 0), block((ROWS, WIDE, CH), 0, 0, 0)),
        compiler_params=params(),
        cost_estimate=cost(1.1e9, 6e6),
    )(*operands, factors, weights)


def spread_kernel(place_ref, x_ref, source_ref, out0, out1, w_ref, field_ref, done):
    copies = [pltpu.make_async_copy(x_ref.at[t], field_ref.at[t], done.at[t]) for t in range(STEPS)]
    copies.append(pltpu.make_async_copy(source_ref, w_ref, done.at[STEPS]))
    for copy in copies:
        copy.start()
    h, j, k, c = (place_ref[n] for n in range(4))
    lane = lax.broadcasted_iota(jnp.int32, (8, CH), 1)
    chip = jnp.bitwise_xor(lane // HALF, k)
    core = jnp.bitwise_xor(lane // 128 % 2, c)
    far = jnp.bitwise_xor(lane // 64 % 2, h)
    turn = jnp.bitwise_and(lane // 16 + j, 3)
    source = ((far * 4 + turn) * 4 + chip * 2 + core) * 16 + lane % 16
    row = lax.broadcasted_iota(jnp.int32, (CH, CH), 0)
    order = jnp.where(row == source[:1], 1.0, 0.0).astype(BF)
    for copy in copies[:STEPS]:
        copy.wait()
    field = jnp.concatenate([field_ref[t, r] for t in range(STEPS) for r in range(ROWS)], axis=0)
    value = jnp.dot(field, order, preferred_element_type=F32).astype(BF)
    for n, out in enumerate((out0, out1)):
        for t in range(STEPS):
            for r in range(ROWS):
                at = (t * ROWS + r) * WIDTH
                out[t, r] = value[at : at + WIDTH, n * HALF : (n + 1) * HALF]
    copies[STEPS].wait()


def spread(place, x, weights):
    x, weights = (pltpu.with_memory_space_constraint(v, pltpu.HBM) for v in (x, weights))
    shape = jax.ShapeDtypeStruct((STEPS, ROWS, WIDTH, HALF), BF)
    return pl.pallas_call(
        spread_kernel,
        out_shape=(shape, shape, pltpu.VMEM(weights.shape, BF)),
        in_specs=[SMEM, pl.BlockSpec(memory_space=pltpu.HBM), pl.BlockSpec(memory_space=pltpu.HBM)],
        out_specs=(VMEM, VMEM, VMEM),
        scratch_shapes=[
            pltpu.VMEM((STEPS, ROWS, WIDTH, CH), BF),
            pltpu.SemaphoreType.DMA((STEPS + 1,)),
        ],
        compiler_params=params(),
        cost_estimate=cost(4.5e8, 1.2e7),
    )(place, x, weights)


def tap_products(xs, gs):
    left, right = [], []
    for r in range(ROWS):
        left.append(jnp.concatenate([x[r] for x in xs], axis=0))
        taps = [[], [], []]
        for g in gs:
            plane = g[r].astype(F32)
            for b, shift in enumerate((WIDE - 1, 0, 1)):
                moved = pltpu.roll(plane, shift, 0) if shift else plane
                taps[b].append(moved[:WIDTH])
        right.append(
            jnp.concatenate([jnp.concatenate(parts, axis=0).astype(BF) for parts in taps], axis=1)
        )
    pairs = ((left[:2], right[1:]), (left, right), (left[1:], right[:2]))
    return [
        lax.dot_general(
            jnp.concatenate(ls, axis=0),
            jnp.concatenate(rs, axis=0),
            (((0,), (0,)), ((), ())),
            preferred_element_type=F32,
        )
        for ls, rs in pairs
    ]


def early_kernel(x0, x1, both0, both1, third0, third1, last0, out_ref):
    for t in range(STEPS):
        if t < STEPS - 1:
            gs = (both0[t], both1[t]) if t < 2 else (third0, third1)
            values = tap_products((x0[t], x1[t]), gs)
        else:
            values = tap_products((x0[t],), (last0,))
        for a, value in enumerate(values):
            out_ref[a] = value if t == 0 else out_ref[a] + value


def early_products(xs, *gs):
    return pl.pallas_call(
        early_kernel,
        out_shape=jax.ShapeDtypeStruct((3, HALF, 3 * CH), F32),
        in_specs=[VMEM] * 7,
        out_specs=VMEM,
        compiler_params=params(),
        cost_estimate=cost(3e9, 8e6),
    )(*xs, *gs)


FIRST = 6


def late_kernel(x_ref, g_ref, total_ref, *outs):
    for a, value in enumerate(tap_products((x_ref[0],), (g_ref,))):
        value = value + total_ref[a]
        for b in range(3):
            tap = a * 3 + b
            for core in range(2):
                for far in range(2):
                    for turn in range(4):
                        at = ((core * 2 + far) * 4 + turn) * 16
                        part = value[at : at + 16, b * CH : (b + 1) * CH].astype(BF)
                        if tap >= FIRST:
                            outs[4 + core][turn, far, tap - FIRST] = part
                        else:
                            outs[2 * far + core][turn, tap] = part


def late_products(x, g, total):
    shapes = [(4, FIRST, 16, CH)] * 4 + [(4, 2, 9 - FIRST, 16, CH)] * 2
    return pl.pallas_call(
        late_kernel,
        grid=(1,),
        out_shape=tuple(jax.ShapeDtypeStruct(shape, BF) for shape in shapes),
        in_specs=[block((1, ROWS, WIDTH, HALF), STEPS - 1, 0, 0, 0)]
        + [block((ROWS, WIDE, CH), 0, 0, 0)]
        + [block((3, HALF, 3 * CH), 0, 0, 0)],
        out_specs=tuple(block(shape, *(0,) * len(shape)) for shape in shapes),
        compiler_params=params(),
        cost_estimate=cost(1e9, 8e6),
    )(x, g, total)


def grad_kernel(flag_ref, own_ref, low_ref, high_ref, relay_ref, factor_ref, grad_ref):
    for r in range(ROWS):
        slope = widen(own_ref[0, r], high_ref[r], low_ref[r])
        slope = jnp.where(flag_ref[0] == 1, slope, relay_ref[r].astype(F32))
        grad_ref[r] = (slope * factor_ref[0, r]).astype(BF)


def last_grad(flag, top, low, high, arrived, factors):
    edge = block((ROWS, 8, CH), 3 + STEPS, 0, 0)
    return pl.pallas_call(
        grad_kernel,
        grid=(1,),
        out_shape=jax.ShapeDtypeStruct((ROWS, WIDE, CH), BF),
        in_specs=[
            SMEM,
            block((1, ROWS, WIDTH, CH), STEPS - 2, 0, 0, 0),
            edge,
            edge,
            block((ROWS, WIDE, CH), 0, 0, 0),
            block((1, ROWS, WIDE, CH), 0, 0, 0, 0),
        ],
        out_specs=block((ROWS, WIDE, CH), 0, 0, 0),
        compiler_params=params(),
        cost_estimate=cost(1e6, 1e6),
    )(flag, top, low, high, arrived, factors)


def total_of(*parts):
    value = parts[0].astype(F32)
    for part in parts[1:]:
        value = value + part.astype(F32)
    return value


def after(value, *others):
    return lax.optimization_barrier((value, *others))[0]


def body(stored_inputs, filter_weights, pending_slopes, topmost_slopes):
    x = stored_inputs[:, 0]
    pending = pending_slopes[0]
    top = topmost_slopes
    az = lax.axis_index("az")
    place = jnp.stack([az // 16, (az // 4) % 4, (az // 2) % 2, az % 2]).astype(jnp.int32)
    last = lax.axis_index("segment") == lax.axis_size("segment") - 1
    flag = last.astype(jnp.int32).reshape(1)
    scale = 1.0 / math.sqrt(STEPS * ROWS * WIDTH * lax.axis_size("az"))

    right_edge, left_edge = pack_edges(x, pending, top)
    low = send(right_edge, RIGHT)
    high = send(left_edge, LEFT)
    taps = filter_weights[0].reshape(9, CH, CH)
    mine, other, weights = spread(after(place, left_edge), x, taps)
    xs = (mine, send(other, PAIR))

    emitted, fields = [], []
    slope, arrived = pending, None
    weights = pltpu.with_memory_space_constraint(weights, pltpu.VMEM)
    factors = slope_factors(x, low, high, weights, 0)
    for t in range(STEPS):
        if t == STEPS - 1:
            own = last_grad(flag, top, low, high, arrived, factors)
        else:
            sent, grad = back_step(slope, low, high, factors, weights, t, flag, arrived)
            emitted.append(sent[:, :WIDTH])
            slope, weights = top, taps
            own = grad
            arrived = relay(sent)
            waits = (sent, *xs) if t == 1 else (sent,)
            factors = slope_factors(after(x, *waits), low, high, weights, t + 1)
            own = after(own, factors)
            if t == 1:
                own = jnp.stack([fields[0], own])
                fields = []
        fields.append(own if t == 0 else (own, send(own, PAIR)))

    own, pair = fields[-1]
    total = early_products(xs, *fields[0], *fields[1], own)
    near, near_other, out_going, out_other, turns, turns_other = late_products(xs[1], pair, total)
    out_going = total_of(out_going, send(out_other, CORE)).astype(BF)
    far = send(out_going, FAR)
    turns_other, near_other = lax.optimization_barrier((turns_other, near_other, out_going))[:2]
    turns_other, near_other = send(turns_other, CORE), send(near_other, CORE)
    turns = [total_of(turns[m], turns_other[m]).astype(BF) for m in range(4)]
    arrived = after(arrived, *turns[1:])
    arriving = (send(turns[2], ACROSS), send(turns[1], UP), send(turns[3], DOWN))
    near = total_of(near, near_other).astype(BF)
    near = total_of(near, far).astype(BF)
    across, ups, downs = send(near[2], ACROSS), send(near[1], UP), send(near[3], DOWN)
    arriving = lax.optimization_barrier((*arriving, near))[:3]
    turned = total_of(turns[0], *arriving).astype(BF)
    far = send(turned[1], FAR)
    sums = [total_of(near[0], ups, across, downs), total_of(turned[0], far)]
    sent, _ = back_step(top, low, high, factors, taps, STEPS - 1, flag, arrived)
    emitted.append(sent[:, :WIDTH])
    weight_grads = (jnp.concatenate(sums, axis=0) * scale).astype(BF).reshape(1, 3, 3, 16, CH)
    return (jnp.stack(emitted)[:, None], weight_grads)


def solution(mesh):
    return jax.shard_map(
        body,
        mesh=mesh,
        in_specs=(
            P(None, "segment", None, "az", None),
            P("segment", None, None, None, None),
            P("segment", None, "az", None),
            P(None, None, "az", None),
        ),
        out_specs=(P(None, "segment", None, "az", None), P("segment", None, None, "az", None)),
        check_vma=False,
    )
```

```python
import math

import jax
import jax.numpy as jnp
from jax import lax
from jax.experimental import pallas as pl
from jax.experimental.pallas import tpu as pltpu
from jax.sharding import PartitionSpec as P

BF = jnp.bfloat16
F32 = jnp.float32
ROWS, WIDTH, CH, STEPS = 3, 64, 512, 4
WIDE = WIDTH + 8
HALF = CH // 2


def az_route(move):
    route = []
    for i in range(32):
        h, z, c = move(i // 16, (i // 2) % 8, i % 2)
        route.append((i, (h % 2) * 16 + (z % 8) * 2 + c % 2))
    return route


RIGHT = [(i, (i + 1) % 32) for i in range(32)]
LEFT = [(i, (i - 1) % 32) for i in range(32)]
CORE = az_route(lambda h, z, c: (h, z, c + 1))
PAIR = az_route(lambda h, z, c: (h, z ^ 1, c))
FAR = az_route(lambda h, z, c: (h + 1, z, c))
UP = az_route(lambda h, z, c: (h, z + 2, c))
ACROSS = az_route(lambda h, z, c: (h, z + 4, c))
DOWN = az_route(lambda h, z, c: (h, z - 2, c))


def send(block, route):
    return lax.ppermute(block, "az", route)


def relay(block):
    count = lax.axis_size("segment")
    return lax.ppermute(block, "segment", [(i, (i - 1) % count) for i in range(count)])


def params(mib=24):
    return pltpu.CompilerParams(vmem_limit_bytes=mib * 1024 * 1024)


def cost(flops, size):
    return pl.CostEstimate(flops=int(flops), bytes_accessed=int(size), transcendentals=0)


VMEM = pl.BlockSpec(memory_space=pltpu.VMEM)
SMEM = pl.BlockSpec(memory_space=pltpu.SMEM)


def block(shape, *index):
    return pl.BlockSpec(shape, lambda *_: index)


def pack_kernel(x_right, p_right, t_right, x_left, p_left, t_left, right_ref, left_ref):
    for refs, first, out in (((x_right, p_right, t_right), 8, right_ref), ((x_left, p_left, t_left), 0, left_ref)):
        xs, ps, ts = refs
        for r in range(ROWS):
            planes = [xs[t, r] for t in range(STEPS)] + [ps[r]] + [ts[t, r] for t in range(STEPS - 1)]
            for n, plane in enumerate(planes):
                out[n * ROWS + r] = plane.astype(F32)[first : first + 8].astype(BF)


def pack_edges(x, pending, top):
    def specs(edge):
        return [
            block((STEPS, ROWS, 16, CH), 0, 0, edge, 0),
            block((ROWS, 16, CH), 0, edge, 0),
            block((STEPS - 1, ROWS, 16, CH), 0, 0, edge, 0),
        ]

    x, pending, top = (pltpu.with_memory_space_constraint(v, pltpu.HBM) for v in (x, pending, top))
    shape = jax.ShapeDtypeStruct((24, 8, CH), BF)
    return pl.pallas_call(
        pack_kernel,
        grid=(1,),
        out_shape=(shape, shape),
        in_specs=specs(3) + specs(0),
        out_specs=(block((24, 8, CH), 0, 0, 0),) * 2,
        compiler_params=params(),
        cost_estimate=cost(0, 1 << 20),
    )(x, pending, top, x, pending, top)


def first_four(high, low):
    pick = lax.broadcasted_iota(jnp.int32, high.shape, 0) < 4
    return jnp.where(pick, high, low)


def widen(own, high, low):
    return jnp.concatenate([own.astype(F32), first_four(high.astype(F32), low.astype(F32))], axis=0)


def factor_kernel(x_ref, low_ref, high_ref, w_ref, out_ref):
    wide = WIDTH + 16
    planes = [
        jnp.concatenate(
            [x_ref[0, r].astype(F32), high_ref[r].astype(F32), low_ref[r].astype(F32)], axis=0
        )
        for r in range(ROWS)
    ]
    field = jnp.concatenate(planes, axis=0).astype(BF)
    sums = []
    for b in range(3):
        up = jnp.dot(field[: 2 * wide], w_ref[b], preferred_element_type=F32)
        mid = jnp.dot(field, w_ref[3 + b], preferred_element_type=F32)
        down = jnp.dot(field[wide:], w_ref[6 + b], preferred_element_type=F32)
        rows = []
        for r in range(ROWS):
            value = mid[r * wide : (r + 1) * wide]
            if r > 0:
                value = value + up[(r - 1) * wide : r * wide]
            if r < 2:
                value = value + down[r * wide : (r + 1) * wide]
            rows.append(value)
        sums.append(rows)
    for r in range(ROWS):
        preact = pltpu.roll(sums[0][r], 1, 0) + sums[1][r] + pltpu.roll(sums[2][r], wide - 1, 0)
        gate = jax.nn.sigmoid(preact)
        value = gate * (1.0 + preact * (1.0 - gate))
        out_ref[0, r, :WIDTH] = value[:WIDTH]
        out_ref[0, r, WIDTH:] = first_four(value[WIDTH : WIDTH + 8], value[WIDTH + 8 :])


def slope_factors(x, low, high, weights, first):
    weights = pltpu.with_memory_space_constraint(weights, pltpu.VMEM)
    return pl.pallas_call(
        factor_kernel,
        grid=(1,),
        out_shape=jax.ShapeDtypeStruct((1, ROWS, WIDE, CH), F32),
        in_specs=[
            pl.BlockSpec((1, ROWS, WIDTH, CH), lambda n: (first + n, 0, 0, 0)),
            pl.BlockSpec((ROWS, 8, CH), lambda n: (first + n, 0, 0)),
            pl.BlockSpec((ROWS, 8, CH), lambda n: (first + n, 0, 0)),
            VMEM,
        ],
        out_specs=pl.BlockSpec((1, ROWS, WIDE, CH), lambda n: (n, 0, 0, 0)),
        compiler_params=params(),
        cost_estimate=cost(1.2e9, 5e6),
    )(x, low, high, weights)


def back_kernel(first, *refs):
    if first:
        own_ref, low_ref, high_ref, factor_ref, w_ref, sent_ref, grad_ref = refs
    else:
        flag_ref, own_ref, low_ref, high_ref, relay_ref, factor_ref, w_ref, sent_ref, grad_ref = refs
    slopes = []
    for r in range(ROWS):
        own = own_ref[r] if first else own_ref[0, r]
        slope = widen(own, high_ref[r], low_ref[r])
        if not first:
            slope = jnp.where(flag_ref[0] == 1, slope, relay_ref[r].astype(F32))
        slopes.append(slope)
    grads = []
    for r in range(ROWS):
        grad = slopes[r] * factor_ref[0, r]
        grad_ref[r] = grad.astype(BF)
        grads.append(grad)
    field = jnp.concatenate(grads, axis=0).astype(BF)
    above = jnp.concatenate(grads[1:], axis=0).astype(BF)
    below = jnp.concatenate(grads[:2], axis=0).astype(BF)
    turned = (((1,), (1,)), ((), ()))
    sums = []
    for b in range(3):
        up = lax.dot_general(above, w_ref[b], turned, preferred_element_type=F32)
        mid = lax.dot_general(field, w_ref[3 + b], turned, preferred_element_type=F32)
        down = lax.dot_general(below, w_ref[6 + b], turned, preferred_element_type=F32)
        rows = []
        for r in range(ROWS):
            value = mid[r * WIDE : (r + 1) * WIDE]
            if r < 2:
                value = value + up[r * WIDE : (r + 1) * WIDE]
            if r > 0:
                value = value + down[(r - 1) * WIDE : r * WIDE]
            rows.append(value)
        sums.append(rows)
    for r in range(ROWS):
        value = pltpu.roll(sums[0][r], WIDE - 1, 0) + sums[1][r] + pltpu.roll(sums[2][r], 1, 0)
        sent_ref[r] = (slopes[r] + value).astype(BF)


def back_step(own, low, high, factors, weights, t, flag=None, arrived=None):
    first = t == 0
    weights = pltpu.with_memory_space_constraint(weights, pltpu.VMEM)
    edge = block((ROWS, 8, CH), 4 + t, 0, 0)
    operands = [own, low, high]
    if first:
        specs = [block((ROWS, WIDTH, CH), 0, 0, 0), edge, edge]
    else:
        specs = [SMEM, block((1, ROWS, WIDTH, CH), t - 1, 0, 0, 0), edge, edge]
        specs += [block((ROWS, WIDE, CH), 0, 0, 0)]
        operands = [flag, *operands, arrived]
    specs += [block((1, ROWS, WIDE, CH), 0, 0, 0, 0), VMEM]
    return pl.pallas_call(
        lambda *refs: back_kernel(first, *refs),
        grid=(1,),
        out_shape=(
            jax.ShapeDtypeStruct((ROWS, WIDE, CH), BF),
            jax.ShapeDtypeStruct((ROWS, WIDE, CH), BF),
        ),
        in_specs=specs,
        out_specs=(block((ROWS, WIDE, CH), 0, 0, 0), block((ROWS, WIDE, CH), 0, 0, 0)),
        compiler_params=params(),
        cost_estimate=cost(1.1e9, 6e6),
    )(*operands, factors, weights)


def spread_kernel(place_ref, x_ref, source_ref, out0, out1, w_ref, field_ref, done):
    copies = [pltpu.make_async_copy(x_ref.at[t], field_ref.at[t], done.at[t]) for t in range(STEPS)]
    for n in range(3):
        rows = slice(3 * n, 3 * n + 3)
        copies.append(pltpu.make_async_copy(source_ref.at[rows], w_ref.at[rows], done.at[STEPS + n]))
    for copy in copies:
        copy.start()
    h, j, k, c = (place_ref[n] for n in range(4))
    lane = lax.broadcasted_iota(jnp.int32, (8, CH), 1)
    chip = jnp.bitwise_xor(lane // HALF, k)
    core = jnp.bitwise_xor(lane // 128 % 2, c)
    far = jnp.bitwise_xor(lane // 64 % 2, h)
    turn = jnp.bitwise_and(lane // 16 + j, 3)
    source = ((far * 4 + turn) * 4 + chip * 2 + core) * 16 + lane % 16
    row = lax.broadcasted_iota(jnp.int32, (CH, CH), 0)
    order = jnp.where(row == source[:1], 1.0, 0.0).astype(BF)
    for copy in copies[:STEPS]:
        copy.wait()
    field = jnp.concatenate([field_ref[t, r] for t in range(STEPS) for r in range(ROWS)], axis=0)
    value = jnp.dot(field, order, preferred_element_type=F32).astype(BF)
    for n, out in enumerate((out0, out1)):
        for t in range(STEPS):
            for r in range(ROWS):
                at = (t * ROWS + r) * WIDTH
                out[t, r] = value[at : at + WIDTH, n * HALF : (n + 1) * HALF]
    for copy in copies[STEPS:]:
        copy.wait()


def spread(place, x, weights):
    x, weights = (pltpu.with_memory_space_constraint(v, pltpu.HBM) for v in (x, weights))
    shape = jax.ShapeDtypeStruct((STEPS, ROWS, WIDTH, HALF), BF)
    return pl.pallas_call(
        spread_kernel,
        out_shape=(shape, shape, pltpu.VMEM(weights.shape, BF)),
        in_specs=[SMEM, pl.BlockSpec(memory_space=pltpu.HBM), pl.BlockSpec(memory_space=pltpu.HBM)],
        out_specs=(VMEM, VMEM, VMEM),
        scratch_shapes=[
            pltpu.VMEM((STEPS, ROWS, WIDTH, CH), BF),
            pltpu.SemaphoreType.DMA((STEPS + 3,)),
        ],
        compiler_params=params(),
        cost_estimate=cost(4.5e8, 1.2e7),
    )(place, x, weights)


def tap_products(xs, gs):
    left, right = [], []
    for r in range(ROWS):
        left.append(jnp.concatenate([x[r] for x in xs], axis=0))
        taps = [[], [], []]
        for g in gs:
            plane = g[r].astype(F32)
            for b, shift in enumerate((WIDE - 1, 0, 1)):
                moved = pltpu.roll(plane, shift, 0) if shift else plane
                taps[b].append(moved[:WIDTH])
        right.append(
            jnp.concatenate([jnp.concatenate(parts, axis=0).astype(BF) for parts in taps], axis=1)
        )
    pairs = ((left[:2], right[1:]), (left, right), (left[1:], right[:2]))
    return [
        lax.dot_general(
            jnp.concatenate(ls, axis=0),
            jnp.concatenate(rs, axis=0),
            (((0,), (0,)), ((), ())),
            preferred_element_type=F32,
        )
        for ls, rs in pairs
    ]


def early_kernel(x0, x1, both0, both1, third0, third1, last0, out_ref):
    for t in range(STEPS):
        if t < STEPS - 1:
            gs = (both0[t], both1[t]) if t < 2 else (third0, third1)
            values = tap_products((x0[t], x1[t]), gs)
        else:
            values = tap_products((x0[t],), (last0,))
        for a, value in enumerate(values):
            out_ref[a] = value if t == 0 else out_ref[a] + value


def early_products(xs, *gs):
    return pl.pallas_call(
        early_kernel,
        out_shape=jax.ShapeDtypeStruct((3, HALF, 3 * CH), F32),
        in_specs=[VMEM] * 7,
        out_specs=VMEM,
        compiler_params=params(),
        cost_estimate=cost(3e9, 8e6),
    )(*xs, *gs)


FIRST = 6


def late_kernel(x_ref, g_ref, total_ref, *outs):
    for a, value in enumerate(tap_products((x_ref[0],), (g_ref,))):
        value = value + total_ref[a]
        for b in range(3):
            tap = a * 3 + b
            for core in range(2):
                for far in range(2):
                    for turn in range(4):
                        at = ((core * 2 + far) * 4 + turn) * 16
                        part = value[at : at + 16, b * CH : (b + 1) * CH].astype(BF)
                        if tap >= FIRST:
                            outs[4 + core][turn, far, tap - FIRST] = part
                        else:
                            outs[2 * far + core][turn, tap] = part


def late_products(x, g, total):
    shapes = [(4, FIRST, 16, CH)] * 4 + [(4, 2, 9 - FIRST, 16, CH)] * 2
    return pl.pallas_call(
        late_kernel,
        grid=(1,),
        out_shape=tuple(jax.ShapeDtypeStruct(shape, BF) for shape in shapes),
        in_specs=[block((1, ROWS, WIDTH, HALF), STEPS - 1, 0, 0, 0)]
        + [block((ROWS, WIDE, CH), 0, 0, 0)]
        + [block((3, HALF, 3 * CH), 0, 0, 0)],
        out_specs=tuple(block(shape, *(0,) * len(shape)) for shape in shapes),
        compiler_params=params(),
        cost_estimate=cost(1e9, 8e6),
    )(x, g, total)


def grad_kernel(flag_ref, own_ref, low_ref, high_ref, relay_ref, factor_ref, grad_ref):
    for r in range(ROWS):
        slope = widen(own_ref[0, r], high_ref[r], low_ref[r])
        slope = jnp.where(flag_ref[0] == 1, slope, relay_ref[r].astype(F32))
        grad_ref[r] = (slope * factor_ref[0, r]).astype(BF)


def last_grad(flag, top, low, high, arrived, factors):
    edge = block((ROWS, 8, CH), 3 + STEPS, 0, 0)
    return pl.pallas_call(
        grad_kernel,
        grid=(1,),
        out_shape=jax.ShapeDtypeStruct((ROWS, WIDE, CH), BF),
        in_specs=[
            SMEM,
            block((1, ROWS, WIDTH, CH), STEPS - 2, 0, 0, 0),
            edge,
            edge,
            block((ROWS, WIDE, CH), 0, 0, 0),
            block((1, ROWS, WIDE, CH), 0, 0, 0, 0),
        ],
        out_specs=block((ROWS, WIDE, CH), 0, 0, 0),
        compiler_params=params(),
        cost_estimate=cost(1e6, 1e6),
    )(flag, top, low, high, arrived, factors)


def total_of(*parts):
    value = parts[0].astype(F32)
    for part in parts[1:]:
        value = value + part.astype(F32)
    return value


def after(value, *others):
    return lax.optimization_barrier((value, *others))[0]


def body(stored_inputs, filter_weights, pending_slopes, topmost_slopes):
    x = stored_inputs[:, 0]
    pending = pending_slopes[0]
    top = topmost_slopes
    az = lax.axis_index("az")
    place = jnp.stack([az // 16, (az // 4) % 4, (az // 2) % 2, az % 2]).astype(jnp.int32)
    last = lax.axis_index("segment") == lax.axis_size("segment") - 1
    flag = last.astype(jnp.int32).reshape(1)
    scale = 1.0 / math.sqrt(STEPS * ROWS * WIDTH * lax.axis_size("az"))

    right_edge, left_edge = pack_edges(x, pending, top)
    low = send(right_edge, RIGHT)
    high = send(left_edge, LEFT)
    taps = filter_weights[0].reshape(9, CH, CH)
    mine, other, weights = spread(after(place, left_edge), x, taps)
    xs = (mine, send(other, PAIR))

    emitted, fields = [], []
    slope, arrived = pending, None
    weights = pltpu.with_memory_space_constraint(weights, pltpu.VMEM)
    factors = slope_factors(x, low, high, weights, 0)
    for t in range(STEPS):
        if t == STEPS - 1:
            own = last_grad(flag, top, low, high, arrived, factors)
        else:
            sent, grad = back_step(slope, low, high, factors, weights, t, flag, arrived)
            emitted.append(sent[:, :WIDTH])
            slope, weights = top, taps
            own = grad
            arrived = relay(sent)
            waits = (sent, *xs) if t == 1 else (sent,)
            factors = slope_factors(after(x, *waits), low, high, weights, t + 1)
            own = after(own, factors)
            if t == 1:
                own = jnp.stack([fields[0], own])
                fields = []
        fields.append(own if t == 0 else (own, send(own, PAIR)))

    own, pair = fields[-1]
    total = early_products(xs, *fields[0], *fields[1], own)
    near, near_other, out_going, out_other, turns, turns_other = late_products(xs[1], pair, total)
    out_going = total_of(out_going, send(out_other, CORE)).astype(BF)
    far = send(out_going, FAR)
    turns_other, near_other = lax.optimization_barrier((turns_other, near_other, out_going))[:2]
    turns_other, near_other = send(turns_other, CORE), send(near_other, CORE)
    turns = [total_of(turns[m], turns_other[m]).astype(BF) for m in range(4)]
    arrived = after(arrived, *turns[1:])
    arriving = (send(turns[2], ACROSS), send(turns[1], UP), send(turns[3], DOWN))
    near = total_of(near, near_other).astype(BF)
    near = total_of(near, far).astype(BF)
    across, ups, downs = send(near[2], ACROSS), send(near[1], UP), send(near[3], DOWN)
    arriving = lax.optimization_barrier((*arriving, near))[:3]
    turned = total_of(turns[0], *arriving).astype(BF)
    far = send(turned[1], FAR)
    sums = [total_of(near[0], ups, across, downs), total_of(turned[0], far)]
    sent, _ = back_step(top, low, high, factors, taps, STEPS - 1, flag, arrived)
    emitted.append(sent[:, :WIDTH])
    weight_grads = (jnp.concatenate(sums, axis=0) * scale).astype(BF).reshape(1, 3, 3, 16, CH)
    return (jnp.stack(emitted)[:, None], weight_grads)


def solution(mesh):
    return jax.shard_map(
        body,
        mesh=mesh,
        in_specs=(
            P(None, "segment", None, "az", None),
            P("segment", None, None, None, None),
            P("segment", None, "az", None),
            P(None, None, "az", None),
        ),
        out_specs=(P(None, "segment", None, "az", None), P("segment", None, None, "az", None)),
        check_vma=False,
    )
```
